32 devices in a mesh: blk: 8 (over z, y), group: 4 (over x, core).
Axes of the slice: x: 2, y: 2, z: 4, core: 2. Of those that a mesh axis runs over, the one named last changes fastest.
Arguments:
- image_embeds: bfloat16 [4, 768, 1152], P('group', 'blk')
- text_embeds: bfloat16 [4, 768, 1152], P('group', 'blk'), may hold values from -0.1875 to 0.1875
- positives: int32 [4, 768], P('group', 'blk'), may hold values from 0 to 767, each once within a row
- partner: int32 [4], replicated, may hold values from 0 to 3, each once
- log_temp: float32 [1], replicated, may hold values from 1.6 to 2.4
- bias: float32 [1], replicated, may hold values from -4 to -2
Outputs:
- image_grads: float32 [4, 768, 1152], P('group', 'blk')
- text_grads: float32 [4, 768, 1152], P('group', 'blk')
- loss: float32 [1], replicated
The draws below stay inside these ranges and needn't reach their ends.
Inputs may be any that keep to these rules, and one draw needn't show every extreme that they name: Each group's positives name every text row of its partner group exactly once. `partner`: every group is named exactly once.
All inputs are finite; a program needn't handle non-finite values.
Results may differ from the reference program's by a relative error of at most 0.0015.
Values may be sent and summed in bfloat16 or wider, within the bound.
No kernel may reach another device: no remote copies, remote signals or barrier semaphores. Data moves between devices by JAX's collectives and lax.ppermute only.
A program may use at most 64 MiB of HBM per device.

```python
import math
import jax
import jax.numpy as jnp

D = 1152
BLOCKS = 8
GROUPS = 4
GROUP_ROWS = 768
IMAGES = 3072


def draw_image_embeds(key, part):
    key = jax.random.fold_in(key, 11)
    first, second = jax.random.split(key)
    place = (jnp.arange(GROUPS, dtype=jnp.float32)[:, None] * GROUP_ROWS + jnp.arange(GROUP_ROWS, dtype=jnp.float32)[None, :]) / IMAGES
    jitter = jax.random.uniform(second, (GROUPS, GROUP_ROWS), jnp.float32, 0.7, 1.4)
    top_scale = 10.0
    values = jax.random.normal(first, (GROUPS, GROUP_ROWS, D), jnp.float32)
    scale = jnp.exp(place * math.log(top_scale)) * jitter / math.sqrt(D)
    return (values * scale[:, :, None]).astype(jnp.bfloat16)


def level_of(own_key, shape, shards, smallest, top_value):
    level, own = 1.0, jax.random.fold_in(own_key, 6)
    for position, blocks in shards:
        heights = jnp.exp(jax.random.uniform(jax.random.fold_in(own, position), (blocks,), jnp.float32, smallest / len(shards), top_value / len(shards)))
        level = level * jnp.repeat(heights, shape[position] // blocks).reshape([-1 if axis == position else 1 for axis in range(len(shape))])
    return level


def normal_values(rng, dims, scale, limit, shards=(), kind=jnp.bfloat16):
    gain = level_of(rng, dims, shards, -0.22, 0.18) if shards else 1.0
    result = jax.random.normal(rng, dims, jnp.float32) * scale * gain
    return jnp.minimum(jnp.maximum(result, -limit), limit).astype(kind)


def setup_inputs(seed: int = 0) -> dict:
    arg_keys = jax.random.split(jax.random.key(seed), 7)
    return {
        "image_embeds": draw_image_embeds(jax.random.fold_in(arg_keys[6], 71), 0),
        "text_embeds": normal_values(arg_keys[1], (GROUPS, GROUP_ROWS, D), D ** -0.5, 0.1875, ((0, 4), (1, 8))),
        "positives": jax.vmap(lambda own: jax.random.permutation(own, GROUP_ROWS))(jax.random.split(arg_keys[2], GROUPS)).reshape((GROUPS, GROUP_ROWS)).astype(jnp.int32),
        "partner": jax.random.permutation(arg_keys[3], GROUPS).astype(jnp.int32),
        "log_temp": jnp.clip(jax.random.uniform(arg_keys[4], (1,), jnp.float32, 1.6, 2.4), 1.6, 2.4),
        "bias": jnp.clip(jax.random.uniform(arg_keys[5], (1,), jnp.float32, -4.0, -2.0), -4.0, -2.0),
    }


def pair_block(images, texts, hits, temper, offset):
    logits = temper * jnp.dot(images, texts.T, preferred_element_type=jnp.float32) + offset
    hit_values = hits.astype(jnp.float32)
    losses = jax.nn.softplus(logits) - hit_values * logits
    slopes = (jax.nn.sigmoid(logits) - hit_values).astype(jnp.bfloat16)
    return jnp.sum(losses), slopes


def reference(image_embeds, text_embeds, positives, partner, log_temp, bias):
    temper = jnp.exp(log_temp[0])
    offset = bias[0]
    columns = jnp.arange(GROUP_ROWS, dtype=jnp.int32)
    image_list = []
    text_grads = jnp.zeros((GROUPS, GROUP_ROWS, D), jnp.float32)
    total = jnp.zeros((), jnp.float32)
    for group in range(GROUPS):
        texts = text_embeds[partner[group]]
        hits = positives[group][:, None] == columns[None, :]
        part, slopes = pair_block(image_embeds[group], texts, hits, temper, offset)
        image_list.append(temper * jnp.dot(slopes, texts, preferred_element_type=jnp.float32))
        back = temper * jnp.dot(slopes.T, image_embeds[group], preferred_element_type=jnp.float32)
        text_grads = text_grads.at[partner[group]].set(back)
        total = total + part
    loss = total / (IMAGES * BLOCKS)
    return jnp.stack(image_list), text_grads, jnp.reshape(loss, (1,))
```

```python
import jax
import jax.numpy as jnp
from jax import lax
from jax.sharding import PartitionSpec as P


def pair_slopes(rows, others, hits, temper, offset):
    logits = temper * jnp.dot(rows, others.T, preferred_element_type=jnp.float32) + offset
    hit_values = hits.astype(jnp.float32)
    slopes = (jax.nn.sigmoid(logits) - hit_values).astype(jnp.bfloat16)
    return logits, hit_values, slopes


def shards(image_embeds, text_embeds, positives, partner, log_temp, bias):
    temper = jnp.exp(log_temp[0])
    offset = bias[0]
    images = image_embeds[0]
    texts = text_embeds[0]
    labels = positives[0]
    rows = images.shape[0]
    blocks = lax.axis_size("blk")
    groups = lax.axis_size("group")
    blk_place = lax.axis_index("blk")
    group_place = lax.axis_index("group")
    target = partner[group_place]
    scorer = jnp.argmax(partner == group_place).astype(jnp.int32)

    group_texts = lax.all_gather(texts, "group", axis=0)
    group_images = lax.all_gather(images, "group", axis=0)
    partner_text = lax.dynamic_index_in_dim(group_texts, target, 0, keepdims=False)
    scorer_image = lax.dynamic_index_in_dim(group_images, scorer, 0, keepdims=False)
    all_texts = lax.all_gather(partner_text, "blk", axis=0, tiled=True)
    all_images = lax.all_gather(scorer_image, "blk", axis=0, tiled=True)
    every_label = lax.all_gather(labels, ("blk", "group"), axis=0).reshape(blocks, groups, rows)
    scorer_labels = lax.dynamic_index_in_dim(every_label, scorer, 1, keepdims=False).reshape(-1)

    text_index = jnp.arange(blocks * rows, dtype=jnp.int32)
    hits = labels[:, None] == text_index[None, :]
    logits, hit_values, slopes = pair_slopes(images, all_texts, hits, temper, offset)
    total = jnp.sum(jax.nn.softplus(logits) - hit_values * logits)
    image_grads = temper * jnp.dot(slopes, all_texts, preferred_element_type=jnp.float32)

    own_index = blk_place * rows + jnp.arange(rows, dtype=jnp.int32)
    back_hits = own_index[:, None] == scorer_labels[None, :]
    back_slopes = pair_slopes(texts, all_images, back_hits, temper, offset)[2]
    text_grads = temper * jnp.dot(back_slopes, all_images, preferred_element_type=jnp.float32)

    total = lax.psum(total, ("blk", "group"))
    loss = total / (groups * rows * blocks * blocks)
    return (image_grads[None], text_grads[None], jnp.reshape(loss, (1,)))


def solution(mesh):
    in_specs = (P("group", "blk", None), P("group", "blk", None), P("group", "blk"), P(), P(), P())
    out_specs = (P("group", "blk", None), P("group", "blk", None), P())
    return jax.shard_map(shards, mesh=mesh, in_specs=in_specs, out_specs=out_specs, check_vma=False)
```

```python
import jax
import jax.numpy as jnp
from jax import lax
from jax.sharding import PartitionSpec as P


def pair_slopes(rows, others, hits, temper, offset):
    logits = temper * jnp.dot(rows, others.T, preferred_element_type=jnp.float32) + offset
    hit_values = hits.astype(jnp.float32)
    slopes = (jax.nn.sigmoid(logits) - hit_values).astype(jnp.bfloat16)
    return logits, hit_values, slopes


def exchange(array, axis, size, mate):
    return lax.ppermute(array, axis, [(place, mate(place)) for place in range(size)])


def pick(own, wanted, here, mate_wanted, groups):
    across = exchange(own, "group", groups, lambda place: place ^ 2)
    for_mate = jnp.where((mate_wanted ^ here) >> 1 == 0, own, across)
    from_mate = exchange(for_mate, "group", groups, lambda place: place ^ 1)
    held = jnp.where((wanted ^ here) >> 1 == 0, own, across)
    return jnp.where((wanted ^ here) & 1 == 0, held, from_mate)


def spread(own, blocks):
    found = [own]
    for hop in (1, blocks // 2 - 1, *range(2, blocks // 2 - 1)):
        found.append(exchange(own, "blk", blocks, lambda place: (place + 2 * hop) % blocks))
    return found + [exchange(block, "blk", blocks, lambda place: place ^ 1) for block in found]


def gather_order(place, blocks):
    hops = (0, 1, blocks // 2 - 1, *range(2, blocks // 2 - 1))
    column = [(place - 2 * hop) % blocks for hop in hops]
    return column + [source ^ 1 for source in column]


def shards(image_embeds, text_embeds, positives, partner, log_temp, bias):
    temper = jnp.exp(log_temp[0])
    offset = bias[0]
    images = image_embeds[0]
    texts = text_embeds[0]
    labels = positives[0]
    rows = images.shape[0]
    blocks = lax.axis_size("blk")
    groups = lax.axis_size("group")
    blk_place = lax.axis_index("blk")
    group_place = lax.axis_index("group")

    def partner_of(group):
        return jnp.sum(jnp.where(jnp.arange(groups) == group, partner, 0))

    def scorer_of(group):
        return jnp.sum(jnp.where(partner == group, jnp.arange(groups), 0))

    every_label = lax.all_gather(labels, ("blk", "group"), axis=0).reshape(blocks, groups, rows)
    partner_text = pick(texts, partner_of(group_place), group_place, partner_of(group_place ^ 1), groups)
    scorer = scorer_of(group_place)
    scorer_image = pick(images, scorer, group_place, scorer_of(group_place ^ 1), groups)
    scorer_labels = lax.dynamic_index_in_dim(every_label, scorer, 1, keepdims=False)

    if blocks == 8:
        order = jnp.stack(gather_order(blk_place, blocks))
        all_texts = jnp.concatenate(spread(partner_text, blocks))
        all_images = jnp.concatenate(spread(scorer_image, blocks))
    else:
        order = jnp.arange(blocks)
        all_texts = lax.all_gather(partner_text, "blk", axis=0, tiled=True)
        all_images = lax.all_gather(scorer_image, "blk", axis=0, tiled=True)

    text_index = (order[:, None] * rows + jnp.arange(rows)[None, :]).reshape(-1)
    hits = labels[:, None] == text_index[None, :]
    logits, hit_values, slopes = pair_slopes(images, all_texts, hits, temper, offset)
    total = jnp.sum(jax.nn.softplus(logits) - hit_values * logits)
    image_grads = temper * jnp.dot(slopes, all_texts, preferred_element_type=jnp.float32)

    own_index = blk_place * rows + jnp.arange(rows)
    back_labels = scorer_labels[order].reshape(-1)
    back_hits = own_index[:, None] == back_labels[None, :]
    back_slopes = pair_slopes(texts, all_images, back_hits, temper, offset)[2]
    text_grads = temper * jnp.dot(back_slopes, all_images, preferred_element_type=jnp.float32)

    total = lax.psum(total, ("blk", "group"))
    loss = total / (groups * rows * blocks * blocks)
    return (image_grads[None], text_grads[None], jnp.reshape(loss, (1,)))


def solution(mesh):
    in_specs = (P("group", "blk", None), P("group", "blk", None), P("group", "blk"), P(), P(), P())
    out_specs = (P("group", "blk", None), P("group", "blk", None), P())
    return jax.shard_map(shards, mesh=mesh, in_specs=in_specs, out_specs=out_specs, check_vma=False)
```

```python
import jax
import jax.numpy as jnp
from jax import lax
from jax.sharding import PartitionSpec as P

RING = {0: 2, 2: 3, 3: 1, 1: 0}


def pair_slopes(rows, others, hits, temper, offset):
    logits = temper * jnp.dot(rows, others.T, preferred_element_type=jnp.float32) + offset
    hit_values = hits.astype(jnp.float32)
    slopes = (jax.nn.sigmoid(logits) - hit_values).astype(jnp.bfloat16)
    return logits, hit_values, slopes


def exchange(array, axis, size, mate):
    return lax.ppermute(array, axis, [(place, mate(place)) for place in range(size)])


def swap(array, axis, size, bit):
    return exchange(array, axis, size, lambda place: place ^ bit)


def after(array, *earlier):
    return lax.optimization_barrier((array, *earlier))[0]


def pick(own, across, wanted, here, mate_wanted, groups):
    for_mate = jnp.where((mate_wanted ^ here) >> 1 == 0, own, across)
    from_mate = swap(for_mate, "group", groups, 1)
    held = jnp.where((wanted ^ here) >> 1 == 0, own, across)
    return jnp.where((wanted ^ here) & 1 == 0, held, from_mate)


def spread(own, blocks):
    column = [own]
    for _ in range(blocks // 2 - 1):
        column.append(exchange(column[-1], "blk", blocks, lambda place: 2 * RING[place // 2] + place % 2))
    return column + [swap(block, "blk", blocks, 1) for block in column]


def gather_order(place, blocks):
    back = jnp.array([source for source, _ in sorted(RING.items(), key=lambda pair: pair[1])])
    column = [place]
    for _ in range(blocks // 2 - 1):
        column.append(2 * back[column[-1] // 2] + place % 2)
    return jnp.stack(column + [source ^ 1 for source in column])


def shards(image_embeds, text_embeds, positives, partner, log_temp, bias):
    temper = jnp.exp(log_temp[0])
    offset = bias[0]
    images = image_embeds[0]
    texts = text_embeds[0]
    labels = positives[0]
    rows = images.shape[0]
    blocks = lax.axis_size("blk")
    groups = lax.axis_size("group")
    blk_place = lax.axis_index("blk")
    group_place = lax.axis_index("group")

    def partner_of(group):
        return jnp.sum(jnp.where(jnp.arange(groups) == group, partner, 0))

    def scorer_of(group):
        return jnp.sum(jnp.where(partner == group, jnp.arange(groups), 0))

    scorer = scorer_of(group_place)
    texts_across = swap(texts, "group", groups, 2)
    images_across = swap(after(images, texts_across), "group", groups, 2)
    partner_text = pick(texts, texts_across, partner_of(group_place), group_place, partner_of(group_place ^ 1), groups)
    scorer_image = pick(images, images_across, scorer, group_place, scorer_of(group_place ^ 1), groups)

    held_labels = labels[None]
    for bit in (1, 2):
        held_labels = jnp.concatenate([held_labels, swap(held_labels, "group", groups, bit)])
    scorer_labels = lax.dynamic_index_in_dim(held_labels, scorer ^ group_place, 0)

    if blocks == 8:
        order = gather_order(blk_place, blocks)
        all_texts = jnp.concatenate(spread(partner_text, blocks))
        all_images = jnp.concatenate(spread(scorer_image, blocks))
        for bit in (1, 2, 4):
            scorer_labels = jnp.concatenate([scorer_labels, swap(scorer_labels, "blk", blocks, bit)])
        back_labels = scorer_labels[order ^ blk_place].reshape(-1)
    else:
        order = jnp.arange(blocks)
        all_texts = lax.all_gather(partner_text, "blk", axis=0, tiled=True)
        all_images = lax.all_gather(scorer_image, "blk", axis=0, tiled=True)
        back_labels = lax.all_gather(scorer_labels, "blk", axis=0).reshape(-1)

    text_index = (order[:, None] * rows + jnp.arange(rows)[None, :]).reshape(-1)
    hits = labels[:, None] == text_index[None, :]
    logits, hit_values, slopes = pair_slopes(images, all_texts, hits, temper, offset)
    total = jnp.sum(jax.nn.softplus(logits) - hit_values * logits)
    image_grads = temper * jnp.dot(slopes, all_texts, preferred_element_type=jnp.float32)

    own_index = blk_place * rows + jnp.arange(rows)
    back_hits = own_index[:, None] == back_labels[None, :]
    back_slopes = pair_slopes(texts, all_images, back_hits, temper, offset)[2]
    text_grads = temper * jnp.dot(back_slopes, all_images, preferred_element_type=jnp.float32)

    total = total.reshape(1)
    for axis, size in (("group", groups), ("blk", blocks)):
        bit = 1
        while bit < size:
            total = total + swap(total, axis, size, bit)
            bit *= 2
    loss = total / (groups * rows * blocks * blocks)
    return (image_grads[None], text_grads[None], loss)


def solution(mesh):
    in_specs = (P("group", "blk", None), P("group", "blk", None), P("group", "blk"), P(), P(), P())
    out_specs = (P("group", "blk", None), P("group", "blk", None), P())
    return jax.shard_map(shards, mesh=mesh, in_specs=in_specs, out_specs=out_specs, check_vma=False)
```

```python
import jax
import jax.numpy as jnp
from jax import lax
from jax.sharding import PartitionSpec as P

RING = {0: 2, 2: 3, 3: 1, 1: 0}


def pair_slopes(rows, others, hits, temper, offset):
    logits = temper * jnp.dot(rows, others.T, preferred_element_type=jnp.float32) + offset
    hit_values = hits.astype(jnp.float32)
    slopes = (jax.nn.sigmoid(logits) - hit_values).astype(jnp.bfloat16)
    return logits, hit_values, slopes


def exchange(array, axis, size, mate):
    return lax.ppermute(array, axis, [(place, mate(place)) for place in range(size)])


def swap(array, axis, size, bit):
    return exchange(array, axis, size, lambda place: place ^ bit)


def after(array, *earlier):
    return lax.optimization_barrier((array, *earlier))[0]


def pick(own, across, wanted, here, mate_wanted, groups):
    for_mate = jnp.where((mate_wanted ^ here) >> 1 == 0, own, across)
    from_mate = swap(for_mate, "group", groups, 1)
    held = jnp.where((wanted ^ here) >> 1 == 0, own, across)
    return jnp.where((wanted ^ here) & 1 == 0, held, from_mate)


def ring(array, blocks):
    return exchange(array, "blk", blocks, lambda place: 2 * RING[place // 2] + place % 2)


def ring_sources(place, blocks):
    back = {target: source for source, target in RING.items()}
    sources = [place]
    for _ in range(blocks // 2 - 1):
        here = sources[-1] // 2
        before = sum(jnp.where(here == target, source, 0) for target, source in back.items())
        sources.append(2 * before + place % 2)
    return sources


def shards(image_embeds, text_embeds, positives, partner, log_temp, bias):
    temper = jnp.exp(log_temp[0])
    offset = bias[0]
    images = image_embeds[0]
    texts = text_embeds[0]
    labels = positives[0]
    rows = images.shape[0]
    blocks = lax.axis_size("blk")
    groups = lax.axis_size("group")
    blk_place = lax.axis_index("blk")
    group_place = lax.axis_index("group")

    def partner_of(group):
        return jnp.sum(jnp.where(jnp.arange(groups) == group, partner, 0))

    def scorer_of(group):
        return jnp.sum(jnp.where(partner == group, jnp.arange(groups), 0))

    scorer = scorer_of(group_place)
    texts_across = swap(texts, "group", groups, 2)
    images_across = swap(after(images, texts_across), "group", groups, 2)
    partner_text = pick(texts, texts_across, partner_of(group_place), group_place, partner_of(group_place ^ 1), groups)
    scorer_image = pick(images, images_across, scorer, group_place, scorer_of(group_place ^ 1), groups)

    if blocks == 8:
        sources = ring_sources(blk_place, blocks)
        order = jnp.stack([place for source in sources for place in (source, source ^ 1)])
        text_blocks = [partner_text, swap(partner_text, "blk", blocks, 1)]
        image_blocks = [scorer_image, swap(scorer_image, "blk", blocks, 1)]
        cut = rows * 2 // 3 // 16 * 16
        text_moving = partner_text
        image_moving = jnp.concatenate([scorer_image, image_blocks[1][cut:]])
        held_labels = after(labels[None], text_blocks[1])
        for step in range(blocks // 2 - 1):
            text_moving = ring(text_moving, blocks)
            text_blocks += [text_moving, swap(text_moving, "blk", blocks, 1)]
            if step < 2:
                held_labels = jnp.concatenate([held_labels, swap(after(held_labels, text_moving), "group", groups, 1 << step)])
        label_rows = lax.dynamic_index_in_dim(held_labels, scorer ^ group_place, 0)
        for step in range(blocks // 2 - 1):
            image_moving = ring(image_moving, blocks)
            relayed = swap(image_moving[:cut], "blk", blocks, 1)
            image_blocks += [image_moving[:rows], relayed, image_moving[rows:]]
            if step < 3:
                label_rows = jnp.concatenate([label_rows, swap(after(label_rows, text_blocks[2 * step + 3]), "blk", blocks, 1 << step)])
        all_texts = jnp.concatenate(text_blocks)
        all_images = jnp.concatenate(image_blocks)
        marks = [text_blocks[-1], image_blocks[5], image_blocks[6], image_blocks[8], image_blocks[8]]
        back_labels = label_rows[order ^ blk_place].reshape(-1)
    else:
        order = jnp.arange(blocks)
        all_texts = lax.all_gather(partner_text, "blk", axis=0, tiled=True)
        all_images = lax.all_gather(scorer_image, "blk", axis=0, tiled=True)
        every_label = lax.all_gather(labels, ("group", "blk"), axis=0).reshape(groups, -1)
        back_labels = lax.dynamic_index_in_dim(every_label, scorer, 0, keepdims=False)
        marks = []

    text_index = (order[:, None] * rows + jnp.arange(rows)[None, :]).reshape(-1)
    hits = labels[:, None] == text_index[None, :]
    logits, hit_values, slopes = pair_slopes(images, all_texts, hits, temper, offset)
    total = jnp.sum(jax.nn.softplus(logits) - hit_values * logits)
    image_grads = temper * jnp.dot(slopes, all_texts, preferred_element_type=jnp.float32)

    own_index = blk_place * rows + jnp.arange(rows)
    back_hits = own_index[:, None] == back_labels[None, :]
    back_slopes = pair_slopes(texts, all_images, back_hits, temper, offset)[2]
    text_grads = temper * jnp.dot(back_slopes, all_images, preferred_element_type=jnp.float32)

    total = total.reshape(1)
    for axis, size in (("group", groups), ("blk", blocks)):
        for step in range(size.bit_length() - 1):
            if marks:
                total = after(total, marks.pop(0))
            total = total + swap(total, axis, size, 1 << step)
    loss = total / (groups * rows * blocks * blocks)
    return (image_grads[None], text_grads[None], loss)


def solution(mesh):
    in_specs = (P("group", "blk", None), P("group", "blk", None), P("group", "blk"), P(), P(), P())
    out_specs = (P("group", "blk", None), P("group", "blk", None), P())
    return jax.shard_map(shards, mesh=mesh, in_specs=in_specs, out_specs=out_specs, check_vma=False)
```

```python
import jax
import jax.numpy as jnp
from jax import lax
from jax.sharding import PartitionSpec as P

RING = {0: 2, 2: 3, 3: 1, 1: 0}
TAIL = 16
DIGIT = 128


def pair_slopes(rows, others, hits, temper, offset):
    logits = temper * jnp.dot(rows, others.T, preferred_element_type=jnp.float32) + offset
    hit_values = hits.astype(jnp.float32)
    slopes = (jax.nn.sigmoid(logits) - hit_values).astype(jnp.bfloat16)
    return logits, hit_values, slopes


def exchange(array, axis, size, mate):
    return lax.ppermute(array, axis, [(place, mate(place)) for place in range(size)])


def swap(array, axis, size, bit):
    return exchange(array, axis, size, lambda place: place ^ bit)


def after(array, *earlier):
    return lax.optimization_barrier((array, *earlier))[0]


def pick(own, across, wanted, here, mate_wanted, groups):
    for_mate = jnp.where((mate_wanted ^ here) >> 1 == 0, own, across)
    from_mate = swap(for_mate, "group", groups, 1)
    held = jnp.where((wanted ^ here) >> 1 == 0, own, across)
    return jnp.where((wanted ^ here) & 1 == 0, held, from_mate)


def ring(array, blocks):
    return exchange(array, "blk", blocks, lambda place: 2 * RING[place // 2] + place % 2)


def ring_sources(place, blocks):
    back = {target: source for source, target in RING.items()}
    sources = [place]
    for _ in range(blocks // 2 - 1):
        here = sources[-1] // 2
        before = sum(jnp.where(here == target, source, 0) for target, source in back.items())
        sources.append(2 * before + place % 2)
    return sources


def with_labels(images, labels):
    digits = jnp.stack([labels // DIGIT, labels % DIGIT]).astype(images.dtype)
    return jnp.concatenate([images, jnp.pad(digits, ((0, TAIL - 2), (0, images.shape[1] - labels.shape[0])))])


def labels_of(block, rows):
    digits = block[rows : rows + 2, :rows].astype(jnp.int32)
    return digits[0] * DIGIT + digits[1]


def all_sum(total, axis, size, marks):
    for step in range(size.bit_length() - 1):
        if marks:
            total = after(total, marks.pop(0))
        total = total + swap(total, axis, size, 1 << step)
    return total


def shards(image_embeds, text_embeds, positives, partner, log_temp, bias):
    temper = jnp.exp(log_temp[0])
    offset = bias[0]
    texts = text_embeds[0]
    labels = positives[0]
    rows = texts.shape[0]
    blocks = lax.axis_size("blk")
    groups = lax.axis_size("group")
    blk_place = lax.axis_index("blk")
    group_place = lax.axis_index("group")
    images = with_labels(image_embeds[0], labels)

    def partner_of(group):
        return jnp.sum(jnp.where(jnp.arange(groups) == group, partner, 0))

    def scorer_of(group):
        return jnp.sum(jnp.where(partner == group, jnp.arange(groups), 0))

    def index_of(places):
        return (jnp.stack(places)[:, None] * rows + jnp.arange(rows)[None, :]).reshape(-1)

    def matches(some_labels, index):
        return some_labels[:, None] == index[None, :]

    def grads(slopes, others):
        return temper * jnp.dot(slopes, others, preferred_element_type=jnp.float32)

    scorer = scorer_of(group_place)
    texts_across = swap(texts, "group", groups, 2)
    images_across = swap(after(images, texts_across), "group", groups, 2)
    partner_text = pick(texts, texts_across, partner_of(group_place), group_place, partner_of(group_place ^ 1), groups)
    images_across = after(images_across, partner_text)
    scorer_image = pick(images, images_across, scorer, group_place, scorer_of(group_place ^ 1), groups)
    own_images = images[:rows]

    if blocks == 8:
        sources = ring_sources(blk_place, blocks)
        text_blocks = [partner_text]
        image_blocks = [scorer_image]
        relayed = [swap(scorer_image, "blk", blocks, 1)]
        mate_images = swap(images, "blk", blocks, 1)
        for _ in range(blocks // 2 - 1):
            text_blocks.append(ring(text_blocks[-1], blocks))
            image_blocks.append(ring(image_blocks[-1], blocks))
            relayed.append(swap(image_blocks[-1], "blk", blocks, 1))

        column_texts = jnp.concatenate(text_blocks)
        two_images = jnp.concatenate([own_images, mate_images[:rows]])
        two_labels = jnp.concatenate([labels, labels_of(mate_images, rows)])
        hits = matches(two_labels, index_of(sources))
        logits, hit_values, slopes = pair_slopes(two_images, column_texts, hits, temper, offset)
        total = jnp.sum(jax.nn.softplus(logits) - hit_values * logits)
        mate_part = swap(grads(slopes[rows:], column_texts), "blk", blocks, 1)
        image_grads = grads(slopes[:rows], column_texts) + mate_part

        all_blocks = image_blocks + relayed
        all_images = jnp.concatenate([block[:rows] for block in all_blocks])
        back_labels = jnp.concatenate([labels_of(block, rows) for block in all_blocks])
        marks = [column_texts, image_blocks[2], relayed[2], image_blocks[3], image_blocks[3]]
    else:
        all_texts = lax.all_gather(partner_text, "blk", axis=0, tiled=True)
        every_image = lax.all_gather(scorer_image, "blk", axis=0)
        hits = matches(labels, jnp.arange(blocks * rows))
        logits, hit_values, slopes = pair_slopes(own_images, all_texts, hits, temper, offset)
        total = jnp.sum(jax.nn.softplus(logits) - hit_values * logits)
        image_grads = grads(slopes, all_texts)
        all_images = every_image[:, :rows].reshape(blocks * rows, -1)
        back_labels = jax.vmap(lambda block: labels_of(block, rows))(every_image).reshape(-1)
        marks = []

    back_hits = index_of([blk_place])[:, None] == back_labels[None, :]
    back_slopes = pair_slopes(texts, all_images, back_hits, temper, offset)[2]
    text_grads = grads(back_slopes, all_images)

    total = jnp.full((8, 128), total)
    total = all_sum(total, "group", groups, marks)
    total = all_sum(total, "blk", blocks, marks)
    loss = total[0, :1] / (groups * rows * blocks * blocks)
    return (image_grads[None], text_grads[None], loss)


def solution(mesh):
    in_specs = (P("group", "blk", None), P("group", "blk", None), P("group", "blk"), P(), P(), P())
    out_specs = (P("group", "blk", None), P("group", "blk", None), P())
    return jax.shard_map(shards, mesh=mesh, in_specs=in_specs, out_specs=out_specs, check_vma=False)
```

```python
import jax
import jax.numpy as jnp
from jax import lax
from jax.sharding import PartitionSpec as P

TAIL = 16
DIGIT = 128


def pair_slopes(rows, others, hits, temper, offset):
    logits = temper * jnp.dot(rows, others.T, preferred_element_type=jnp.float32) + offset
    hit_values = hits.astype(jnp.float32)
    slopes = (jax.nn.sigmoid(logits) - hit_values).astype(jnp.bfloat16)
    return logits, hit_values, slopes


def exchange(array, axis, size, mate):
    return lax.ppermute(array, axis, [(place, mate(place)) for place in range(size)])


def swap(array, axis, size, bit):
    return exchange(array, axis, size, lambda place: place ^ bit)


def after(array, *earlier):
    return lax.optimization_barrier((array, *earlier))[0]


def pick(own, across, wanted, here, mate_wanted, groups):
    for_mate = jnp.where((mate_wanted ^ here) >> 1 == 0, own, across)
    from_mate = swap(for_mate, "group", groups, 1)
    held = jnp.where((wanted ^ here) >> 1 == 0, own, across)
    return jnp.where((wanted ^ here) & 1 == 0, held, from_mate)


def line_gather(own, place):
    z = place // 2

    def send(block, targets):
        return lax.ppermute(block, "blk", [(2 * source + y, 2 * target + y) for source, target in targets.items() for y in range(2)])

    two_off = send(own, {0: 2, 1: 3, 2: 0, 3: 1})
    from_below = send(own, {0: 1, 1: 2, 2: 3})
    from_above = send(own, {3: 2, 2: 1, 1: 0})
    far = send(two_off, {2: 3, 1: 0})
    near = jnp.where(z == 0, from_above, from_below)
    last = jnp.where((z == 0) | (z == 3), far, from_above)
    return [own, two_off, near, last]


def line_order(place):
    z, y = place // 2, place % 2
    near = jnp.where(z == 0, 1, z - 1)
    last = jnp.where(z == 1, 2, jnp.where(z == 3, 0, 3))
    return [2 * source + y for source in (z, z ^ 2, near, last)]


def with_labels(images, labels):
    digits = jnp.stack([labels // DIGIT, labels % DIGIT]).astype(images.dtype)
    return jnp.concatenate([images, jnp.pad(digits, ((0, TAIL - 2), (0, images.shape[1] - labels.shape[0])))])


def labels_of(block, rows):
    digits = block[rows : rows + 2, :rows].astype(jnp.int32)
    return digits[0] * DIGIT + digits[1]


def hop_sum(total, hops):
    for axis, size, bit in hops:
        total = total + swap(total, axis, size, bit)
    return total


def shards(image_embeds, text_embeds, positives, partner, log_temp, bias):
    texts = text_embeds[0]
    labels = positives[0]
    rows = texts.shape[0]
    blocks = lax.axis_size("blk")
    groups = lax.axis_size("group")
    blk_place = lax.axis_index("blk")
    group_place = lax.axis_index("group")
    images = with_labels(image_embeds[0], labels)

    def partner_of(group):
        return jnp.sum(jnp.where(jnp.arange(groups) == group, partner, 0))

    def scorer_of(group):
        return jnp.sum(jnp.where(partner == group, jnp.arange(groups), 0))

    def index_of(places):
        return (jnp.stack(places)[:, None] * rows + jnp.arange(rows)[None, :]).reshape(-1)

    def matches(some_labels, index):
        return some_labels[:, None] == index[None, :]

    def grads(slopes, others):
        return temper * jnp.dot(slopes, others, preferred_element_type=jnp.float32)

    packed = after(jnp.concatenate([images, texts]))
    tailed = images.shape[0]
    own_images, own_texts = packed[:rows], packed[tailed:]
    hops = [(axis, size, 1 << step) for axis, size in (("group", groups), ("blk", blocks)) for step in range(size.bit_length() - 1)]
    scorer = scorer_of(group_place)
    texts_across = swap(texts, "group", groups, 2)
    images_across = swap(after(packed[:tailed], texts_across), "group", groups, 2)
    partner_text = pick(own_texts, texts_across, partner_of(group_place), group_place, partner_of(group_place ^ 1), groups)
    images_across = after(images_across, partner_text)
    scorer_image = pick(packed[:tailed], images_across, scorer, group_place, scorer_of(group_place ^ 1), groups)
    log_temp, bias, blk_place, labels = lax.optimization_barrier((log_temp, bias, blk_place, labels, partner_text))[:4]
    temper = jnp.exp(log_temp[0])
    offset = bias[0]

    if blocks == 8:
        mate = swap(packed, "blk", blocks, 1)
        places = line_order(blk_place)
        text_blocks = line_gather(partner_text, blk_place)
        image_blocks = line_gather(scorer_image, blk_place)

        column_texts = jnp.concatenate(text_blocks)
        two_images = jnp.concatenate([own_images, mate[:rows]])
        two_labels = jnp.concatenate([labels, labels_of(mate, rows)])
        hits = matches(two_labels, index_of(places))
        logits, hit_values, slopes = pair_slopes(two_images, column_texts, hits, temper, offset)
        total = jnp.sum(jax.nn.softplus(logits) - hit_values * logits)
        total = hop_sum(jnp.full((8, 128), total), hops[:3])
        image_part = swap(grads(slopes[rows:], column_texts), "blk", blocks, 1)
        image_grads = grads(slopes[:rows], column_texts) + image_part

        column_images = after(jnp.concatenate([block[:rows] for block in image_blocks]), total)
        column_labels = jnp.concatenate([labels_of(block, rows) for block in image_blocks])
        two_texts = jnp.concatenate([own_texts, mate[tailed:]])
        back_hits = matches(index_of([blk_place, blk_place ^ 1]), column_labels)
        back_slopes = pair_slopes(two_texts, column_images, back_hits, temper, offset)[2]
        text_part = swap(grads(back_slopes[rows:], column_images), "blk", blocks, 1)
        text_grads = grads(back_slopes[:rows], column_images) + text_part
    else:
        all_texts = lax.all_gather(partner_text, "blk", axis=0, tiled=True)
        every_image = lax.all_gather(scorer_image, "blk", axis=0)
        hits = matches(labels, jnp.arange(blocks * rows))
        logits, hit_values, slopes = pair_slopes(own_images, all_texts, hits, temper, offset)
        total = jnp.sum(jax.nn.softplus(logits) - hit_values * logits)
        total = hop_sum(jnp.full((8, 128), total), hops[:3])
        image_grads = grads(slopes, all_texts)
        all_images = every_image[:, :rows].reshape(blocks * rows, -1)
        back_labels = jax.vmap(lambda block: labels_of(block, rows))(every_image).reshape(-1)
        back_hits = matches(index_of([blk_place]), back_labels)
        back_slopes = pair_slopes(own_texts, all_images, back_hits, temper, offset)[2]
        text_grads = grads(back_slopes, all_images)

    total = hop_sum(total, hops[3:])
    loss = total[0, :1] / (groups * rows * blocks * blocks)
    return (image_grads[None], text_grads[None], loss)


def solution(mesh):
    in_specs = (P("group", "blk", None), P("group", "blk", None), P("group", "blk"), P(), P(), P())
    out_specs = (P("group", "blk", None), P("group", "blk", None), P())
    return jax.shard_map(shards, mesh=mesh, in_specs=in_specs, out_specs=out_specs, check_vma=False)
```

```python
import jax
import jax.numpy as jnp
from jax import lax
from jax.experimental import pallas as pl
from jax.experimental.pallas import tpu as pltpu
from jax.sharding import PartitionSpec as P

TAIL = 16
DIGIT = 128


def pair_slopes(rows, others, hits, temper, offset):
    logits = temper * jnp.dot(rows, others.T, preferred_element_type=jnp.float32) + offset
    hit_values = hits.astype(jnp.float32)
    slopes = (jax.nn.sigmoid(logits) - hit_values).astype(jnp.bfloat16)
    return logits, hit_values, slopes


def exchange(array, axis, size, mate):
    return lax.ppermute(array, axis, [(place, mate(place)) for place in range(size)])


def swap(array, axis, size, bit):
    return exchange(array, axis, size, lambda place: place ^ bit)


def after(array, *earlier):
    return lax.optimization_barrier((array, *earlier))[0]


def pick(own, across, wanted, here, mate_wanted, groups):
    for_mate = jnp.where((mate_wanted ^ here) >> 1 == 0, own, across)
    from_mate = swap(for_mate, "group", groups, 1)
    held = jnp.where((wanted ^ here) >> 1 == 0, own, across)
    return jnp.where((wanted ^ here) & 1 == 0, held, from_mate)


def line_gather(own, blocks):
    two_off = swap(own, "blk", blocks, 4)
    one_off = swap(own, "blk", blocks, 2)
    return [own, two_off, one_off, swap(two_off, "blk", blocks, 2)]


LINE = (0, 4, 2, 6)


def with_labels(images, labels):
    digits = jnp.stack([labels // DIGIT, labels % DIGIT]).astype(images.dtype)
    return jnp.concatenate([images, jnp.pad(digits, ((0, TAIL - 2), (0, images.shape[1] - labels.shape[0])))])


def labels_of(block, rows):
    digits = block[rows : rows + TAIL, :rows].astype(jnp.int32)
    return digits[:1] * DIGIT + digits[1:2]


def rows_by_rows(left, right):
    return lax.dot_general(left, right, (((1,), (1,)), ((), ())), preferred_element_type=jnp.float32)


def columns_by_rows(left, right):
    return lax.dot_general(left, right, (((0,), (0,)), ((), ())), preferred_element_type=jnp.float32)


def slopes_and_loss(products, temper, offset, hits):
    logits = temper * products + offset
    hit_values = hits.astype(jnp.float32)
    losses = jnp.maximum(logits, 0.0) + jnp.log1p(jnp.exp(-jnp.abs(logits))) - hit_values * logits
    return (jax.nn.sigmoid(logits) - hit_values).astype(jnp.bfloat16), losses


def image_kernel(log_temp, bias, images, mate, *refs):
    texts, (own_part, mate_part, loss) = refs[:-3], refs[-3:]
    rows = texts[0].shape[0]
    temper = jnp.exp(jnp.full((1, 1), log_temp[0]))
    offset = bias[0]
    place = lax.axis_index("blk")
    loss[...] = jnp.zeros_like(loss)
    for block, part in ((mate, mate_part), (images, own_part)):
        labels = labels_of(block, rows)
        total = jnp.zeros((rows, block.shape[1]), jnp.float32)
        for flip, some_texts in zip(LINE, texts):
            index = (place ^ flip) * rows + lax.broadcasted_iota(jnp.int32, (rows, rows), 0)
            products = rows_by_rows(some_texts[...], block[:rows, :])
            slopes, losses = slopes_and_loss(products, temper, offset, index == labels)
            loss[:, :rows] += losses.reshape(rows // 8, 8, rows).sum(axis=0)
            total += columns_by_rows(slopes, some_texts[...])
        part[...] = temper * total


def text_kernel(log_temp, bias, texts, mate, *refs):
    images, (own_part, mate_part) = refs[:-2], refs[-2:]
    rows = texts.shape[0]
    temper = jnp.exp(jnp.full((1, 1), log_temp[0]))
    offset = bias[0]
    place = lax.axis_index("blk")
    for some_texts, home, part in ((mate, place ^ 1, mate_part), (texts, place, own_part)):
        index = home * rows + lax.broadcasted_iota(jnp.int32, (rows, rows), 0)
        total = jnp.zeros(part.shape, jnp.float32)
        for block in images:
            products = rows_by_rows(some_texts[...], block[:rows, :])
            slopes, _ = slopes_and_loss(products, temper, offset, index == labels_of(block, rows))
            total += jnp.dot(slopes, block[:rows, :], preferred_element_type=jnp.float32)
        part[...] = temper * total


def call(kernel, scalars, arrays, shapes, name):
    return pl.pallas_call(
        kernel,
        out_shape=[jax.ShapeDtypeStruct(shape, jnp.float32) for shape in shapes],
        in_specs=[pl.BlockSpec(memory_space=pltpu.SMEM)] * len(scalars) + [pl.BlockSpec(memory_space=pltpu.VMEM)] * len(arrays),
        out_specs=[pl.BlockSpec(memory_space=pltpu.VMEM)] * len(shapes),
        compiler_params=pltpu.CompilerParams(vmem_limit_bytes=16 * 2**20),
        name=name,
    )(*scalars, *arrays)


def hop_sum(total, hops):
    for axis, size, bit in hops:
        total = total + swap(total, axis, size, bit)
    return total


def shards(image_embeds, text_embeds, positives, partner, log_temp, bias):
    texts = text_embeds[0]
    labels = positives[0]
    rows = texts.shape[0]
    blocks = lax.axis_size("blk")
    groups = lax.axis_size("group")
    blk_place = lax.axis_index("blk")
    group_place = lax.axis_index("group")
    images = with_labels(image_embeds[0], labels)

    def partner_of(group):
        return jnp.sum(jnp.where(jnp.arange(groups) == group, partner, 0))

    def scorer_of(group):
        return jnp.sum(jnp.where(partner == group, jnp.arange(groups), 0))

    def index_of(places):
        return (jnp.stack(places)[:, None] * rows + jnp.arange(rows)[None, :]).reshape(-1)

    def matches(some_labels, index):
        return some_labels[:, None] == index[None, :]

    def grads(slopes, others):
        return temper * jnp.dot(slopes, others, preferred_element_type=jnp.float32)

    packed = after(jnp.concatenate([images, texts]))
    tailed = images.shape[0]
    own_images, own_texts = packed[:rows], packed[tailed:]
    hops = [(axis, size, 1 << step) for axis, size in (("group", groups), ("blk", blocks)) for step in range(size.bit_length() - 1)]
    scorer = scorer_of(group_place)
    texts_across = swap(texts, "group", groups, 2)
    images_across = swap(after(packed[:tailed], texts_across), "group", groups, 2)
    partner_text = pick(own_texts, texts_across, partner_of(group_place), group_place, partner_of(group_place ^ 1), groups)
    images_across = after(images_across, partner_text)
    scorer_image = pick(packed[:tailed], images_across, scorer, group_place, scorer_of(group_place ^ 1), groups)

    if blocks == 8:
        mate = swap(packed, "blk", blocks, 1)
        text_blocks = line_gather(partner_text, blocks)
        image_blocks = line_gather(scorer_image, blocks)
        scalars = (log_temp, bias)
        block_shape = texts.shape
        own_part, mate_part, total = call(
            image_kernel, scalars, [packed[:tailed], mate[:tailed], *text_blocks], [block_shape, block_shape, (8, 128)], "image_side"
        )
        image_grads = own_part + swap(mate_part, "blk", blocks, 1)
        total = hop_sum(total, hops[:1])
        total = hop_sum(after(total, image_blocks[1]), hops[1:3])
        image_blocks[3] = after(image_blocks[3], total)
        own_part, mate_part = call(
            text_kernel, scalars, [own_texts, mate[tailed:], *image_blocks], [block_shape, block_shape], "text_side"
        )
        text_grads = own_part + swap(mate_part, "blk", blocks, 1)
        total = after(total, image_grads)
    else:
        temper = jnp.exp(log_temp[0])
        offset = bias[0]
        all_texts = lax.all_gather(partner_text, "blk", axis=0, tiled=True)
        every_image = lax.all_gather(scorer_image, "blk", axis=0)
        hits = matches(labels, jnp.arange(blocks * rows))
        logits, hit_values, slopes = pair_slopes(own_images, all_texts, hits, temper, offset)
        total = jnp.sum(jax.nn.softplus(logits) - hit_values * logits)
        total = hop_sum(jnp.zeros((8, 128)).at[0, 0].set(total), hops[:3])
        image_grads = grads(slopes, all_texts)
        all_images = every_image[:, :rows].reshape(blocks * rows, -1)
        back_labels = jax.vmap(lambda block: labels_of(block, rows)[0])(every_image).reshape(-1)
        back_hits = matches(index_of([blk_place]), back_labels)
        back_slopes = pair_slopes(own_texts, all_images, back_hits, temper, offset)[2]
        text_grads = grads(back_slopes, all_images)

    total = hop_sum(total, hops[3:])
    loss = jnp.sum(total).reshape(1) / (groups * rows * blocks * blocks)
    return (image_grads[None], text_grads[None], loss)


def solution(mesh):
    in_specs = (P("group", "blk", None), P("group", "blk", None), P("group", "blk"), P(), P(), P())
    out_specs = (P("group", "blk", None), P("group", "blk", None), P())
    return jax.shard_map(shards, mesh=mesh, in_specs=in_specs, out_specs=out_specs, check_vma=False)
```

```python
import functools

import jax
import jax.numpy as jnp
from jax import lax
from jax.experimental import pallas as pl
from jax.experimental.pallas import tpu as pltpu
from jax.sharding import PartitionSpec as P

TAIL = 16
DIGIT = 128


def pair_slopes(rows, others, hits, temper, offset):
    logits = temper * jnp.dot(rows, others.T, preferred_element_type=jnp.float32) + offset
    hit_values = hits.astype(jnp.float32)
    slopes = (jax.nn.sigmoid(logits) - hit_values).astype(jnp.bfloat16)
    return logits, hit_values, slopes


def exchange(array, axis, size, mate):
    return lax.ppermute(array, axis, [(place, mate(place)) for place in range(size)])


def swap(array, axis, size, bit):
    return exchange(array, axis, size, lambda place: place ^ bit)


def after(array, *earlier):
    return lax.optimization_barrier((array, *earlier))[0]


def pick(own, across, wanted, here, mate_wanted, groups):
    for_mate = jnp.where((mate_wanted ^ here) >> 1 == 0, own, across)
    from_mate = swap(for_mate, "group", groups, 1)
    held = jnp.where((wanted ^ here) >> 1 == 0, own, across)
    return jnp.where((wanted ^ here) & 1 == 0, held, from_mate)


def line_gather(own, blocks, *earlier):
    two_off = swap(own, "blk", blocks, 4)
    one_off = swap(own, "blk", blocks, 2)
    return [own, two_off, one_off, swap(after(two_off, *earlier), "blk", blocks, 2)]


LINE = (0, 4, 2, 6)


def with_labels(images, labels):
    digits = jnp.stack([labels // DIGIT, labels % DIGIT]).astype(images.dtype)
    return jnp.concatenate([images, jnp.pad(digits, ((0, TAIL - 2), (0, images.shape[1] - labels.shape[0])))])


def labels_of(block, rows):
    digits = block[rows : rows + TAIL, :rows].astype(jnp.int32)
    return digits[:1] * DIGIT + digits[1:2]


def rows_by_rows(left, right):
    return lax.dot_general(left, right, (((1,), (1,)), ((), ())), preferred_element_type=jnp.float32)


def columns_by_rows(left, right):
    return lax.dot_general(left, right, (((0,), (0,)), ((), ())), preferred_element_type=jnp.float32)


def slopes_and_loss(products, temper, offset, hits):
    logits = temper * products + offset
    hit_values = hits.astype(jnp.float32)
    losses = jnp.maximum(logits, 0.0) + jnp.log1p(jnp.exp(-jnp.abs(logits))) - hit_values * logits
    return (jax.nn.sigmoid(logits) - hit_values).astype(jnp.bfloat16), losses


def image_kernel(log_temp, bias, images, mate, *refs):
    texts, (own_part, mate_part, loss) = refs[:-3], refs[-3:]
    rows = texts[0].shape[0]
    temper = jnp.exp(log_temp[...])
    offset = bias[...]
    place = lax.axis_index("blk")
    loss[...] = jnp.zeros_like(loss)
    for block, part in ((mate, mate_part), (images, own_part)):
        labels = labels_of(block, rows)
        total = jnp.zeros((rows, block.shape[1]), jnp.float32)
        for flip, some_texts in zip(LINE, texts):
            index = (place ^ flip) * rows + lax.broadcasted_iota(jnp.int32, (rows, rows), 0)
            products = rows_by_rows(some_texts[...], block[:rows, :])
            slopes, losses = slopes_and_loss(products, temper, offset, index == labels)
            loss[:, :rows] += losses.reshape(rows // 8, 8, rows).sum(axis=0)
            total += columns_by_rows(slopes, some_texts[...])
        part[...] = temper * total


def text_kernel(flip, log_temp, bias, texts, *refs):
    images, part = refs[:-1], refs[-1]
    rows = texts.shape[0]
    temper = jnp.exp(log_temp[...])
    index = (lax.axis_index("blk") ^ flip) * rows + lax.broadcasted_iota(jnp.int32, (rows, rows), 0)
    total = jnp.zeros(part.shape, jnp.float32)
    for block in images:
        products = rows_by_rows(texts[...], block[:rows, :])
        slopes, _ = slopes_and_loss(products, temper, bias[...], index == labels_of(block, rows))
        total += jnp.dot(slopes, block[:rows, :], preferred_element_type=jnp.float32)
    part[...] = temper * total


def call(kernel, arrays, shapes, name):
    return pl.pallas_call(
        kernel,
        out_shape=[jax.ShapeDtypeStruct(shape, jnp.float32) for shape in shapes],
        in_specs=[pl.BlockSpec(memory_space=pltpu.VMEM)] * len(arrays),
        out_specs=[pl.BlockSpec(memory_space=pltpu.VMEM)] * len(shapes),
        compiler_params=pltpu.CompilerParams(vmem_limit_bytes=16 * 2**20),
        name=name,
    )(*arrays)


def hop_sum(total, hops):
    for axis, size, bit in hops:
        total = total + swap(total, axis, size, bit)
    return total


def shards(image_embeds, text_embeds, positives, partner, log_temp, bias):
    texts = text_embeds[0]
    labels = positives[0]
    rows = texts.shape[0]
    blocks = lax.axis_size("blk")
    groups = lax.axis_size("group")
    blk_place = lax.axis_index("blk")
    group_place = lax.axis_index("group")
    images = with_labels(image_embeds[0], labels)

    def partner_of(group):
        return jnp.sum(jnp.where(jnp.arange(groups) == group, partner, 0))

    def scorer_of(group):
        return jnp.sum(jnp.where(partner == group, jnp.arange(groups), 0))

    def index_of(places):
        return (jnp.stack(places)[:, None] * rows + jnp.arange(rows)[None, :]).reshape(-1)

    def matches(some_labels, index):
        return some_labels[:, None] == index[None, :]

    def grads(slopes, others):
        return temper * jnp.dot(slopes, others, preferred_element_type=jnp.float32)

    packed = after(jnp.concatenate([images, texts]))
    tailed = images.shape[0]
    own_images, own_texts = packed[:rows], packed[tailed:]
    hops = [(axis, size, 1 << step) for axis, size in (("group", groups), ("blk", blocks)) for step in range(size.bit_length() - 1)]
    scorer = scorer_of(group_place)
    texts_across = swap(texts, "group", groups, 2)
    partner_text = pick(own_texts, texts_across, partner_of(group_place), group_place, partner_of(group_place ^ 1), groups)
    group_images = lax.all_gather(after(packed[:tailed], partner_text), "group")
    scorer_image = lax.dynamic_index_in_dim(group_images, scorer, 0, keepdims=False)

    if blocks == 8:
        mate = swap(packed, "blk", blocks, 1)
        text_blocks = line_gather(partner_text, blocks, mate)
        image_blocks = line_gather(scorer_image, blocks)
        scalars = (log_temp.reshape(1, 1), bias.reshape(1, 1))
        block_shape = texts.shape
        own_part, mate_part, total = call(
            image_kernel, [*scalars, packed[:tailed], mate[:tailed], *text_blocks], [block_shape, block_shape, (8, 128)], "image_side"
        )
        image_grads = own_part + swap(mate_part, "blk", blocks, 1)
        total = hop_sum(total, hops[:1])
        total = hop_sum(after(total, image_blocks[1]), hops[1:3])
        image_blocks[3] = after(image_blocks[3], total)
        mate_part = call(functools.partial(text_kernel, 1), [*scalars, mate[tailed:], *image_blocks], [block_shape], "text_side_mate")[0]
        own_part = call(functools.partial(text_kernel, 0), [*scalars, own_texts, *image_blocks], [block_shape], "text_side_own")[0]
        text_grads = own_part + swap(mate_part, "blk", blocks, 1)
        total = after(total, image_grads)
    else:
        temper = jnp.exp(log_temp[0])
        offset = bias[0]
        all_texts = lax.all_gather(partner_text, "blk", axis=0, tiled=True)
        every_image = lax.all_gather(scorer_image, "blk", axis=0)
        hits = matches(labels, jnp.arange(blocks * rows))
        logits, hit_values, slopes = pair_slopes(own_images, all_texts, hits, temper, offset)
        total = jnp.sum(jax.nn.softplus(logits) - hit_values * logits)
        total = hop_sum(jnp.zeros((8, 128)).at[0, 0].set(total), hops[:3])
        image_grads = grads(slopes, all_texts)
        all_images = every_image[:, :rows].reshape(blocks * rows, -1)
        back_labels = jax.vmap(lambda block: labels_of(block, rows)[0])(every_image).reshape(-1)
        back_hits = matches(index_of([blk_place]), back_labels)
        back_slopes = pair_slopes(own_texts, all_images, back_hits, temper, offset)[2]
        text_grads = grads(back_slopes, all_images)

    total = hop_sum(total, hops[3:])
    loss = jnp.sum(total).reshape(1) / (groups * rows * blocks * blocks)
    return (image_grads[None], text_grads[None], loss)


def solution(mesh):
    in_specs = (P("group", "blk", None), P("group", "blk", None), P("group", "blk"), P(), P(), P())
    out_specs = (P("group", "blk", None), P("group", "blk", None), P())
    return jax.shard_map(shards, mesh=mesh, in_specs=in_specs, out_specs=out_specs, check_vma=False)
```

```python
import functools

import jax
import jax.numpy as jnp
from jax import lax
from jax.experimental import pallas as pl
from jax.experimental.pallas import tpu as pltpu
from jax.sharding import PartitionSpec as P

TAIL = 16
DIGIT = 128


def pair_slopes(rows, others, hits, temper, offset):
    logits = temper * jnp.dot(rows, others.T, preferred_element_type=jnp.float32) + offset
    hit_values = hits.astype(jnp.float32)
    slopes = (jax.nn.sigmoid(logits) - hit_values).astype(jnp.bfloat16)
    return logits, hit_values, slopes


def exchange(array, axis, size, mate):
    return lax.ppermute(array, axis, [(place, mate(place)) for place in range(size)])


def swap(array, axis, size, bit):
    return exchange(array, axis, size, lambda place: place ^ bit)


def after(array, *earlier):
    return lax.optimization_barrier((array, *earlier))[0]


def entry(partner, group):
    lane = lax.broadcasted_iota(jnp.int32, partner.shape, 1)
    return jnp.sum(jnp.where(lane == group, partner[...], 0), axis=1, keepdims=True)


def position(partner, group):
    lane = lax.broadcasted_iota(jnp.int32, partner.shape, 1)
    return jnp.sum(jnp.where(partner[...] == group, lane, 0), axis=1, keepdims=True)


def same_chip(group, other):
    return (group ^ other) >> 1 == 0


def offer_kernel(partner, own, across, out):
    here = lax.axis_index("group")
    out[...] = jnp.where(same_chip(entry(partner, here ^ 1), here), own[...], across[...])


def choose_kernel(partner, own, across, offered, out):
    here = lax.axis_index("group")
    wanted = entry(partner, here)
    held = jnp.where(same_chip(wanted, here), own[...], across[...])
    out[...] = jnp.where((wanted ^ here) & 1 == 0, held, offered[...])


def scorer_kernel(partner, every, out):
    wanted = position(partner, lax.axis_index("group"))
    found = every[0]
    for group in range(1, every.shape[0]):
        found = jnp.where(wanted == group, every[group], found)
    out[...] = found


def line_gather(own, blocks, *earlier):
    two_off = swap(own, "blk", blocks, 4)
    one_off = swap(own, "blk", blocks, 2)
    return [own, two_off, one_off, swap(after(two_off, one_off, *earlier), "blk", blocks, 2)]


LINE = (0, 4, 2, 6)


def with_labels(images, labels):
    digits = jnp.stack([labels // DIGIT, labels % DIGIT]).astype(images.dtype)
    return jnp.concatenate([images, jnp.pad(digits, ((0, TAIL - 2), (0, images.shape[1] - labels.shape[0])))])


def labels_of(block, rows):
    digits = block[rows : rows + TAIL, :rows].astype(jnp.int32)
    return digits[:1] * DIGIT + digits[1:2]


def rows_by_rows(left, right):
    return lax.dot_general(left, right, (((1,), (1,)), ((), ())), preferred_element_type=jnp.float32)


def columns_by_rows(left, right):
    return lax.dot_general(left, right, (((0,), (0,)), ((), ())), preferred_element_type=jnp.float32)


def slopes_and_loss(products, temper, offset, hits):
    logits = temper * products + offset
    hit_values = hits.astype(jnp.float32)
    losses = jnp.maximum(logits, 0.0) + jnp.log1p(jnp.exp(-jnp.abs(logits))) - hit_values * logits
    return (jax.nn.sigmoid(logits) - hit_values).astype(jnp.bfloat16), losses


def image_kernel(log_temp, bias, images, mate, *refs):
    texts, (own_part, mate_part, loss) = refs[:-3], refs[-3:]
    rows = texts[0].shape[0]
    temper = jnp.exp(log_temp[...])
    offset = bias[...]
    place = lax.axis_index("blk")
    loss[...] = jnp.zeros_like(loss)
    for block, part in ((mate, mate_part), (images, own_part)):
        labels = labels_of(block, rows)
        total = jnp.zeros((rows, block.shape[1]), jnp.float32)
        for flip, some_texts in zip(LINE, texts):
            index = (place ^ flip) * rows + lax.broadcasted_iota(jnp.int32, (rows, rows), 0)
            products = rows_by_rows(some_texts[...], block[:rows, :])
            slopes, losses = slopes_and_loss(products, temper, offset, index == labels)
            loss[:, :rows] += losses.reshape(rows // 8, 8, rows).sum(axis=0)
            total += columns_by_rows(slopes, some_texts[...])
        part[...] = temper * total


def text_kernel(flip, log_temp, bias, texts, *refs):
    images, part = refs[:-1], refs[-1]
    rows = texts.shape[0]
    temper = jnp.exp(log_temp[...])
    index = (lax.axis_index("blk") ^ flip) * rows + lax.broadcasted_iota(jnp.int32, (rows, rows), 0)
    total = jnp.zeros(part.shape, jnp.float32)
    for block in images:
        products = rows_by_rows(texts[...], block[:rows, :])
        slopes, _ = slopes_and_loss(products, temper, bias[...], index == labels_of(block, rows))
        total += jnp.dot(slopes, block[:rows, :], preferred_element_type=jnp.float32)
    part[...] = temper * total


def call(kernel, arrays, shapes, name, dtype=jnp.float32):
    return pl.pallas_call(
        kernel,
        out_shape=[jax.ShapeDtypeStruct(shape, dtype) for shape in shapes],
        in_specs=[pl.BlockSpec(memory_space=pltpu.VMEM)] * len(arrays),
        out_specs=[pl.BlockSpec(memory_space=pltpu.VMEM)] * len(shapes),
        compiler_params=pltpu.CompilerParams(vmem_limit_bytes=16 * 2**20),
        name=name,
    )(*arrays)


def hop_sum(total, hops):
    for axis, size, bit in hops:
        total = total + swap(total, axis, size, bit)
    return total


def shards(image_embeds, text_embeds, positives, partner, log_temp, bias):
    texts = text_embeds[0]
    labels = positives[0]
    rows = texts.shape[0]
    blocks = lax.axis_size("blk")
    groups = lax.axis_size("group")
    blk_place = lax.axis_index("blk")
    images = with_labels(image_embeds[0], labels)

    def index_of(places):
        return (jnp.stack(places)[:, None] * rows + jnp.arange(rows)[None, :]).reshape(-1)

    def matches(some_labels, index):
        return some_labels[:, None] == index[None, :]

    def grads(slopes, others):
        return temper * jnp.dot(slopes, others, preferred_element_type=jnp.float32)

    packed = after(jnp.concatenate([images, texts]))
    tailed = images.shape[0]
    own_images, own_texts = packed[:rows], packed[tailed:]
    hops = [(axis, size, 1 << step) for axis, size in (("group", groups), ("blk", blocks)) for step in range(size.bit_length() - 1)]
    choice = partner.reshape(1, groups)
    texts_across = swap(texts, "group", groups, 2)
    offer = call(offer_kernel, [choice, own_texts, texts_across], [texts.shape], "offer", texts.dtype)[0]
    offered = swap(offer, "group", groups, 1)
    partner_text = call(choose_kernel, [choice, own_texts, texts_across, offered], [texts.shape], "choose", texts.dtype)[0]
    group_images = lax.all_gather(after(packed[:tailed], partner_text), "group")
    scorer_image = call(scorer_kernel, [choice, group_images], [images.shape], "scorer", images.dtype)[0]

    if blocks == 8:
        mate = swap(packed, "blk", blocks, 1)
        text_blocks = line_gather(partner_text, blocks, mate)
        scalars = (log_temp.reshape(1, 1), bias.reshape(1, 1))
        block_shape = texts.shape
        own_part, mate_part, total = call(
            image_kernel, [*scalars, packed[:tailed], mate[:tailed], *text_blocks], [block_shape, block_shape, (8, 128)], "image_side"
        )
        image_blocks = line_gather(scorer_image, blocks, total)
        image_grads = own_part + swap(mate_part, "blk", blocks, 1)
        total = hop_sum(after(total, image_blocks[1]), hops[:2])
        image_blocks[3] = after(image_blocks[3], total)
        mate_part = call(functools.partial(text_kernel, 1), [*scalars, mate[tailed:], *image_blocks], [block_shape], "text_side_mate")[0]
        own_part = call(functools.partial(text_kernel, 0), [*scalars, own_texts, *image_blocks], [block_shape], "text_side_own")[0]
        text_grads = own_part + swap(mate_part, "blk", blocks, 1)
        total = after(total, image_grads)
    else:
        temper = jnp.exp(log_temp[0])
        offset = bias[0]
        all_texts = lax.all_gather(partner_text, "blk", axis=0, tiled=True)
        every_image = lax.all_gather(scorer_image, "blk", axis=0)
        hits = matches(labels, jnp.arange(blocks * rows))
        logits, hit_values, slopes = pair_slopes(own_images, all_texts, hits, temper, offset)
        total = jnp.sum(jax.nn.softplus(logits) - hit_values * logits)
        total = hop_sum(jnp.zeros((8, 128)).at[0, 0].set(total), hops[:2])
        image_grads = grads(slopes, all_texts)
        all_images = every_image[:, :rows].reshape(blocks * rows, -1)
        back_labels = jax.vmap(lambda block: labels_of(block, rows)[0])(every_image).reshape(-1)
        back_hits = matches(index_of([blk_place]), back_labels)
        back_slopes = pair_slopes(own_texts, all_images, back_hits, temper, offset)[2]
        text_grads = grads(back_slopes, all_images)

    total = hop_sum(total, hops[2:])
    loss = jnp.sum(total).reshape(1) / (groups * rows * blocks * blocks)
    return (image_grads[None], text_grads[None], loss)


def solution(mesh):
    in_specs = (P("group", "blk", None), P("group", "blk", None), P("group", "blk"), P(), P(), P())
    out_specs = (P("group", "blk", None), P("group", "blk", None), P())
    return jax.shard_map(shards, mesh=mesh, in_specs=in_specs, out_specs=out_specs, check_vma=False)
```

```python
import functools

import jax
import jax.numpy as jnp
from jax import lax
from jax.experimental import pallas as pl
from jax.experimental.pallas import tpu as pltpu
from jax.sharding import PartitionSpec as P

TAIL = 16
DIGIT = 128


def pair_slopes(rows, others, hits, temper, offset):
    logits = temper * jnp.dot(rows, others.T, preferred_element_type=jnp.float32) + offset
    hit_values = hits.astype(jnp.float32)
    slopes = (jax.nn.sigmoid(logits) - hit_values).astype(jnp.bfloat16)
    return logits, hit_values, slopes


def exchange(array, axis, size, mate):
    return lax.ppermute(array, axis, [(place, mate(place)) for place in range(size)])


def swap(array, axis, size, bit):
    return exchange(array, axis, size, lambda place: place ^ bit)


def after(array, *earlier):
    return lax.optimization_barrier((array, *earlier))[0]


def entry(partner, group):
    lane = lax.broadcasted_iota(jnp.int32, partner.shape, 1)
    return jnp.sum(jnp.where(lane == group, partner[...], 0), axis=1, keepdims=True)


def position(partner, group):
    lane = lax.broadcasted_iota(jnp.int32, partner.shape, 1)
    return jnp.sum(jnp.where(partner[...] == group, lane, 0), axis=1, keepdims=True)


def same_chip(group, other):
    return (group ^ other) >> 1 == 0


def offer_kernel(wanted_by, partner, own, across, out):
    here = lax.axis_index("group")
    out[...] = jnp.where(same_chip(wanted_by(partner, here ^ 1), here), own[...], across[...])


def choose_kernel(wanted_by, partner, own, across, offered, out):
    here = lax.axis_index("group")
    wanted = wanted_by(partner, here)
    held = jnp.where(same_chip(wanted, here), own[...], across[...])
    out[...] = jnp.where((wanted ^ here) & 1 == 0, held, offered[...])


def scorer_kernel(partner, every, out):
    wanted = position(partner, lax.axis_index("group"))
    found = every[0]
    for group in range(1, every.shape[0]):
        found = jnp.where(wanted == group, every[group], found)
    out[...] = found


def pick(wanted_by, choice, own, groups, name):
    across = swap(own, "group", groups, 2)
    offer = call(functools.partial(offer_kernel, wanted_by), [choice, own, across], [own.shape], "offer_" + name, own.dtype)[0]
    offered = swap(offer, "group", groups, 1)
    return call(functools.partial(choose_kernel, wanted_by), [choice, own, across, offered], [own.shape], "choose_" + name, own.dtype)[0]


LINE = (0, 4, 2, 6)


def with_labels(images, labels):
    digits = jnp.stack([labels // DIGIT, labels % DIGIT]).astype(images.dtype)
    return jnp.concatenate([images, jnp.pad(digits, ((0, TAIL - 2), (0, images.shape[1] - labels.shape[0])))])


def labels_of(block, rows):
    digits = block[rows : rows + TAIL, :rows].astype(jnp.int32)
    return digits[:1] * DIGIT + digits[1:2]


def rows_by_rows(left, right):
    return lax.dot_general(left, right, (((1,), (1,)), ((), ())), preferred_element_type=jnp.float32)


def columns_by_rows(left, right):
    return lax.dot_general(left, right, (((0,), (0,)), ((), ())), preferred_element_type=jnp.float32)


def slopes_and_loss(products, temper, offset, hits):
    logits = temper * products + offset
    hit_values = hits.astype(jnp.float32)
    losses = jnp.maximum(logits, 0.0) + jnp.log1p(jnp.exp(-jnp.abs(logits))) - hit_values * logits
    return (jax.nn.sigmoid(logits) - hit_values).astype(jnp.bfloat16), losses


def image_kernel(flips, last, log_temp, bias, images, *refs):
    texts, refs = refs[: len(flips)], refs[len(flips) :]
    earlier, (part, loss) = refs[:-2], refs[-2:]
    rows = texts[0].shape[0]
    temper = jnp.exp(log_temp[...])
    place = lax.axis_index("blk")
    labels = labels_of(images, rows)
    total = earlier[0][...] if earlier else jnp.zeros(part.shape, jnp.float32)
    loss[...] = earlier[1][...] if earlier else jnp.zeros_like(loss)
    for flip, some_texts in zip(flips, texts):
        index = (place ^ flip) * rows + lax.broadcasted_iota(jnp.int32, (rows, rows), 0)
        products = rows_by_rows(some_texts[...], images[:rows, :])
        slopes, losses = slopes_and_loss(products, temper, bias[...], index == labels)
        loss[:, :rows] += losses.reshape(rows // 8, 8, rows).sum(axis=0)
        total += columns_by_rows(slopes, some_texts[...])
    part[...] = temper * total if last else total


def text_kernel(count, last, log_temp, bias, texts, *refs):
    images, earlier, part = refs[:count], refs[count:-1], refs[-1]
    rows = texts.shape[0]
    temper = jnp.exp(log_temp[...])
    index = lax.axis_index("blk") * rows + lax.broadcasted_iota(jnp.int32, (rows, rows), 0)
    total = earlier[0][...] if earlier else jnp.zeros(part.shape, jnp.float32)
    for block in images:
        products = rows_by_rows(texts[...], block[:rows, :])
        slopes, _ = slopes_and_loss(products, temper, bias[...], index == labels_of(block, rows))
        total += jnp.dot(slopes, block[:rows, :], preferred_element_type=jnp.float32)
    part[...] = temper * total if last else total


def call(kernel, arrays, shapes, name, dtype=jnp.float32):
    return pl.pallas_call(
        kernel,
        out_shape=[jax.ShapeDtypeStruct(shape, dtype) for shape in shapes],
        in_specs=[pl.BlockSpec(memory_space=pltpu.VMEM)] * len(arrays),
        out_specs=[pl.BlockSpec(memory_space=pltpu.VMEM)] * len(shapes),
        compiler_params=pltpu.CompilerParams(vmem_limit_bytes=16 * 2**20),
        name=name,
    )(*arrays)


def hop_sum(total, hops):
    for axis, size, bit in hops:
        total = total + swap(total, axis, size, bit)
    return total


def shards(image_embeds, text_embeds, positives, partner, log_temp, bias):
    texts = text_embeds[0]
    labels = positives[0]
    rows = texts.shape[0]
    blocks = lax.axis_size("blk")
    groups = lax.axis_size("group")
    blk_place = lax.axis_index("blk")
    images = with_labels(image_embeds[0], labels)

    def index_of(places):
        return (jnp.stack(places)[:, None] * rows + jnp.arange(rows)[None, :]).reshape(-1)

    def matches(some_labels, index):
        return some_labels[:, None] == index[None, :]

    def grads(slopes, others):
        return temper * jnp.dot(slopes, others, preferred_element_type=jnp.float32)

    choice = partner.reshape(1, groups)
    hops = [("blk", blocks, 1)] + [("group", groups, 1 << step) for step in range(groups.bit_length() - 1)]
    hops += [("blk", blocks, 1 << step) for step in range(1, blocks.bit_length() - 1)]

    def along(array, flip):
        return swap(array, "blk", blocks, flip)

    partner_text = pick(entry, choice, texts, groups, "text")
    images = after(images, partner_text)

    if blocks == 8:
        scalars = (log_temp.reshape(1, 1), bias.reshape(1, 1))
        grad_shape, loss_shape = texts.shape, (8, 128)
        text_one_off = along(partner_text, 2)
        text_two_off = along(partner_text, 4)
        relayed_text = along(partner_text, 1)
        group_images = after(lax.all_gather(images, "group"), text_two_off, relayed_text)
        scorer_image = call(scorer_kernel, [choice, group_images], [images.shape], "scorer", images.dtype)[0]
        image_two_off = along(scorer_image, 4)
        text_three_off = along(after(text_two_off, text_one_off), 2)
        early_texts = [partner_text, text_two_off, text_one_off, relayed_text, along(text_two_off, 1), along(text_one_off, 1)]
        early = call(
            functools.partial(image_kernel, (0, 4, 2, 1, 5, 3), False), [*scalars, images, *early_texts], [grad_shape, loss_shape], "image_side_early"
        )
        image_one_off = along(after(scorer_image, text_three_off), 2)
        image_three_off = along(after(image_two_off, early[1]), 2)
        late_texts = [text_three_off, along(text_three_off, 1)]
        image_two_off_mate = along(after(image_two_off, late_texts[1]), 1)
        image_grads, total = call(
            functools.partial(image_kernel, (6, 7), True), [*scalars, images, *late_texts, *early], [grad_shape, loss_shape], "image_side_late"
        )
        total = hop_sum(total, hops[:1])
        total = hop_sum(after(total, image_one_off), hops[1:2])

        early_images = [scorer_image, along(scorer_image, 1), image_two_off, image_two_off_mate, image_one_off]
        text_part = call(functools.partial(text_kernel, 5, False), [*scalars, texts, *early_images], [grad_shape], "text_side_early")
        image_three_off = after(image_three_off, total, *text_part)
        late_images = [along(image_one_off, 1), image_three_off, along(image_three_off, 1)]
        text_grads = call(functools.partial(text_kernel, 3, True), [*scalars, texts, *late_images, *text_part], [grad_shape], "text_side_late")[0]
    else:
        temper = jnp.exp(log_temp[0])
        offset = bias[0]
        all_texts = lax.all_gather(partner_text, "blk", axis=0, tiled=True)
        scorer_image = pick(position, choice, images, groups, "image")
        every_image = lax.all_gather(scorer_image, "blk", axis=0)
        hits = matches(labels, jnp.arange(blocks * rows))
        logits, hit_values, slopes = pair_slopes(images[:rows], all_texts, hits, temper, offset)
        total = jnp.sum(jax.nn.softplus(logits) - hit_values * logits)
        total = hop_sum(jnp.zeros((8, 128)).at[0, 0].set(total), hops[:2])
        image_grads = grads(slopes, all_texts)
        all_images = every_image[:, :rows].reshape(blocks * rows, -1)
        back_labels = jax.vmap(lambda block: labels_of(block, rows)[0])(every_image).reshape(-1)
        back_hits = matches(index_of([blk_place]), back_labels)
        back_slopes = pair_slopes(texts, all_images, back_hits, temper, offset)[2]
        text_grads = grads(back_slopes, all_images)

    total = hop_sum(total, hops[2:])
    loss = jnp.sum(total).reshape(1) / (groups * rows * blocks * blocks)
    return (image_grads[None], text_grads[None], loss)


def solution(mesh):
    in_specs = (P("group", "blk", None), P("group", "blk", None), P("group", "blk"), P(), P(), P())
    out_specs = (P("group", "blk", None), P("group", "blk", None), P())
    return jax.shard_map(shards, mesh=mesh, in_specs=in_specs, out_specs=out_specs, check_vma=False)
```

```python
import functools

import jax
import jax.numpy as jnp
from jax import lax
from jax.experimental import pallas as pl
from jax.experimental.pallas import tpu as pltpu
from jax.sharding import PartitionSpec as P

TAIL = 16
DIGIT = 128


def pair_slopes(rows, others, hits, temper, offset):
    logits = temper * jnp.dot(rows, others.T, preferred_element_type=jnp.float32) + offset
    hit_values = hits.astype(jnp.float32)
    slopes = (jax.nn.sigmoid(logits) - hit_values).astype(jnp.bfloat16)
    return logits, hit_values, slopes


def exchange(array, axis, size, mate):
    return lax.ppermute(array, axis, [(place, mate(place)) for place in range(size)])


def swap(array, axis, size, bit):
    return exchange(array, axis, size, lambda place: place ^ bit)


def after(array, *earlier):
    return lax.optimization_barrier((array, *earlier))[0]


def entry(partner, group):
    lane = lax.broadcasted_iota(jnp.int32, partner.shape, 1)
    return jnp.sum(jnp.where(lane == group, partner[...], 0), axis=1, keepdims=True)


def position(partner, group):
    lane = lax.broadcasted_iota(jnp.int32, partner.shape, 1)
    return jnp.sum(jnp.where(partner[...] == group, lane, 0), axis=1, keepdims=True)


def same_chip(group, other):
    return (group ^ other) >> 1 == 0


def offer_kernel(partner, own, across, out):
    here = lax.axis_index("group")
    out[...] = jnp.where(same_chip(entry(partner, here ^ 1), here), own[...], across[...])


def choose_kernel(partner, own, across, offered, out):
    here = lax.axis_index("group")
    wanted = entry(partner, here)
    held = jnp.where(same_chip(wanted, here), own[...], across[...])
    out[...] = jnp.where((wanted ^ here) & 1 == 0, held, offered[...])


def scorer_kernel(partner, every, out):
    wanted = position(partner, lax.axis_index("group"))
    found = every[0]
    for group in range(1, every.shape[0]):
        found = jnp.where(wanted == group, every[group], found)
    out[...] = found


LINE = (0, 4, 2, 6)


def with_labels(images, labels):
    digits = jnp.stack([labels // DIGIT, labels % DIGIT]).astype(images.dtype)
    return jnp.concatenate([images, jnp.pad(digits, ((0, TAIL - 2), (0, images.shape[1] - labels.shape[0])))])


def labels_of(block, rows):
    digits = block[rows : rows + TAIL, :rows].astype(jnp.int32)
    return digits[:1] * DIGIT + digits[1:2]


def rows_by_rows(left, right):
    return lax.dot_general(left, right, (((1,), (1,)), ((), ())), preferred_element_type=jnp.float32)


def columns_by_rows(left, right):
    return lax.dot_general(left, right, (((0,), (0,)), ((), ())), preferred_element_type=jnp.float32)


def slopes_and_loss(products, temper, offset, hits):
    logits = temper * products + offset
    hit_values = hits.astype(jnp.float32)
    losses = jnp.maximum(logits, 0.0) + jnp.log1p(jnp.exp(-jnp.abs(logits))) - hit_values * logits
    return (jax.nn.sigmoid(logits) - hit_values).astype(jnp.bfloat16), losses


def image_kernel(log_temp, bias, images, mate, *refs):
    texts, (own_part, mate_part, loss) = refs[:-3], refs[-3:]
    rows = texts[0].shape[0]
    temper = jnp.exp(log_temp[...])
    offset = bias[...]
    place = lax.axis_index("blk")
    loss[...] = jnp.zeros_like(loss)
    for block, part in ((mate, mate_part), (images, own_part)):
        labels = labels_of(block, rows)
        total = jnp.zeros((rows, block.shape[1]), jnp.float32)
        for flip, some_texts in zip(LINE, texts):
            index = (place ^ flip) * rows + lax.broadcasted_iota(jnp.int32, (rows, rows), 0)
            products = rows_by_rows(some_texts[...], block[:rows, :])
            slopes, losses = slopes_and_loss(products, temper, offset, index == labels)
            loss[:, :rows] += losses.reshape(rows // 8, 8, rows).sum(axis=0)
            total += columns_by_rows(slopes, some_texts[...])
        part[...] = temper * total


def text_kernel(flip, log_temp, bias, texts, *refs):
    images, part = refs[:-1], refs[-1]
    rows = texts.shape[0]
    temper = jnp.exp(log_temp[...])
    index = (lax.axis_index("blk") ^ flip) * rows + lax.broadcasted_iota(jnp.int32, (rows, rows), 0)
    total = jnp.zeros(part.shape, jnp.float32)
    for block in images:
        products = rows_by_rows(texts[...], block[:rows, :])
        slopes, _ = slopes_and_loss(products, temper, bias[...], index == labels_of(block, rows))
        total += jnp.dot(slopes, block[:rows, :], preferred_element_type=jnp.float32)
    part[...] = temper * total


def call(kernel, arrays, shapes, name, dtype=jnp.float32):
    return pl.pallas_call(
        kernel,
        out_shape=[jax.ShapeDtypeStruct(shape, dtype) for shape in shapes],
        in_specs=[pl.BlockSpec(memory_space=pltpu.VMEM)] * len(arrays),
        out_specs=[pl.BlockSpec(memory_space=pltpu.VMEM)] * len(shapes),
        compiler_params=pltpu.CompilerParams(vmem_limit_bytes=16 * 2**20),
        name=name,
    )(*arrays)


def hop_sum(total, hops):
    for axis, size, bit in hops:
        total = total + swap(total, axis, size, bit)
    return total


def shards(image_embeds, text_embeds, positives, partner, log_temp, bias):
    texts = text_embeds[0]
    labels = positives[0]
    rows = texts.shape[0]
    blocks = lax.axis_size("blk")
    groups = lax.axis_size("group")
    blk_place = lax.axis_index("blk")
    images = with_labels(image_embeds[0], labels)

    def index_of(places):
        return (jnp.stack(places)[:, None] * rows + jnp.arange(rows)[None, :]).reshape(-1)

    def matches(some_labels, index):
        return some_labels[:, None] == index[None, :]

    def grads(slopes, others):
        return temper * jnp.dot(slopes, others, preferred_element_type=jnp.float32)

    packed = after(jnp.concatenate([images, texts]))
    tailed = images.shape[0]
    own_images, own_texts = packed[:rows], packed[tailed:]
    hops = [("blk", blocks, 1)] + [("group", groups, 1 << step) for step in range(groups.bit_length() - 1)]
    hops += [("blk", blocks, 1 << step) for step in range(1, blocks.bit_length() - 1)]
    choice = partner.reshape(1, groups)
    texts_across = swap(texts, "group", groups, 2)
    offer = call(offer_kernel, [choice, own_texts, texts_across], [texts.shape], "offer", texts.dtype)[0]
    offered = swap(offer, "group", groups, 1)
    partner_text = call(choose_kernel, [choice, own_texts, texts_across, offered], [texts.shape], "choose", texts.dtype)[0]
    group_images = lax.all_gather(after(packed[:tailed], partner_text), "group")
    scorer_image = call(scorer_kernel, [choice, group_images], [images.shape], "scorer", images.dtype)[0]

    if blocks == 8:

        def along(array, flip):
            return swap(array, "blk", blocks, flip)

        mate = along(packed, 1)
        text_two_off = along(partner_text, 4)
        text_one_off = along(partner_text, 2)
        text_three_off = along(after(text_two_off, text_one_off, mate, scorer_image), 2)
        image_two_off = along(scorer_image, 4)
        image_one_off = along(after(scorer_image, text_three_off), 2)
        column_texts = [partner_text, text_two_off, text_one_off, after(text_three_off, image_two_off)]
        scalars = (log_temp.reshape(1, 1), bias.reshape(1, 1))
        block_shape = texts.shape
        own_part, mate_part, total = call(
            image_kernel, [*scalars, packed[:tailed], mate[:tailed], *column_texts], [block_shape, block_shape, (8, 128)], "image_side"
        )
        image_three_off = along(after(image_two_off, image_one_off, total), 2)
        image_grads = own_part + along(mate_part, 1)
        total = hop_sum(total, hops[:2])
        column_images = [scorer_image, image_two_off, image_one_off, after(image_three_off, total)]
        mate_part = call(functools.partial(text_kernel, 1), [*scalars, mate[tailed:], *column_images], [block_shape], "text_side_mate")[0]
        own_part = call(functools.partial(text_kernel, 0), [*scalars, own_texts, *column_images], [block_shape], "text_side_own")[0]
        text_grads = own_part + along(mate_part, 1)
        total = after(total, image_grads)
    else:
        temper = jnp.exp(log_temp[0])
        offset = bias[0]
        all_texts = lax.all_gather(partner_text, "blk", axis=0, tiled=True)
        every_image = lax.all_gather(scorer_image, "blk", axis=0)
        hits = matches(labels, jnp.arange(blocks * rows))
        logits, hit_values, slopes = pair_slopes(own_images, all_texts, hits, temper, offset)
        total = jnp.sum(jax.nn.softplus(logits) - hit_values * logits)
        total = hop_sum(jnp.zeros((8, 128)).at[0, 0].set(total), hops[:2])
        image_grads = grads(slopes, all_texts)
        all_images = every_image[:, :rows].reshape(blocks * rows, -1)
        back_labels = jax.vmap(lambda block: labels_of(block, rows)[0])(every_image).reshape(-1)
        back_hits = matches(index_of([blk_place]), back_labels)
        back_slopes = pair_slopes(own_texts, all_images, back_hits, temper, offset)[2]
        text_grads = grads(back_slopes, all_images)

    total = hop_sum(total, hops[2:])
    loss = jnp.sum(total).reshape(1) / (groups * rows * blocks * blocks)
    return (image_grads[None], text_grads[None], loss)


def solution(mesh):
    in_specs = (P("group", "blk", None), P("group", "blk", None), P("group", "blk"), P(), P(), P())
    out_specs = (P("group", "blk", None), P("group", "blk", None), P())
    return jax.shard_map(shards, mesh=mesh, in_specs=in_specs, out_specs=out_specs, check_vma=False)
```

```python
import functools

import jax
import jax.numpy as jnp
from jax import lax
from jax.experimental import pallas as pl
from jax.experimental.pallas import tpu as pltpu
from jax.sharding import PartitionSpec as P

TAIL = 16
DIGIT = 128


def pair_slopes(rows, others, hits, temper, offset):
    logits = temper * jnp.dot(rows, others.T, preferred_element_type=jnp.float32) + offset
    hit_values = hits.astype(jnp.float32)
    slopes = (jax.nn.sigmoid(logits) - hit_values).astype(jnp.bfloat16)
    return logits, hit_values, slopes


def exchange(array, axis, size, mate):
    return lax.ppermute(array, axis, [(place, mate(place)) for place in range(size)])


def swap(array, axis, size, bit):
    return exchange(array, axis, size, lambda place: place ^ bit)


def after(array, *earlier):
    return lax.optimization_barrier((array, *earlier))[0]


def entry(partner, group):
    lane = lax.broadcasted_iota(jnp.int32, partner.shape, 1)
    return jnp.sum(jnp.where(lane == group, partner[...], 0), axis=1, keepdims=True)


def position(partner, group):
    lane = lax.broadcasted_iota(jnp.int32, partner.shape, 1)
    return jnp.sum(jnp.where(partner[...] == group, lane, 0), axis=1, keepdims=True)


def same_chip(group, other):
    return (group ^ other) >> 1 == 0


def offer_kernel(partner, own, across, out):
    here = lax.axis_index("group")
    out[...] = jnp.where(same_chip(entry(partner, here ^ 1), here), own[...], across[...])


def choose_kernel(partner, own, across, offered, out):
    here = lax.axis_index("group")
    wanted = entry(partner, here)
    held = jnp.where(same_chip(wanted, here), own[...], across[...])
    out[...] = jnp.where((wanted ^ here) & 1 == 0, held, offered[...])


def scorer_kernel(partner, every, out):
    wanted = position(partner, lax.axis_index("group"))
    found = every[0]
    for group in range(1, every.shape[0]):
        found = jnp.where(wanted == group, every[group], found)
    out[...] = found


LINE = (0, 4, 2, 6)


def with_labels(images, labels):
    digits = jnp.stack([labels // DIGIT, labels % DIGIT]).astype(images.dtype)
    return jnp.concatenate([images, jnp.pad(digits, ((0, TAIL - 2), (0, images.shape[1] - labels.shape[0])))])


def labels_of(block, rows):
    digits = block[rows : rows + TAIL, :rows].astype(jnp.int32)
    return digits[:1] * DIGIT + digits[1:2]


def rows_by_rows(left, right):
    return lax.dot_general(left, right, (((1,), (1,)), ((), ())), preferred_element_type=jnp.float32)


def columns_by_rows(left, right):
    return lax.dot_general(left, right, (((0,), (0,)), ((), ())), preferred_element_type=jnp.float32)


def slopes_and_loss(products, temper, offset, hits):
    logits = temper * products + offset
    hit_values = hits.astype(jnp.float32)
    losses = jnp.maximum(logits, 0.0) + jnp.log1p(jnp.exp(-jnp.abs(logits))) - hit_values * logits
    return (jax.nn.sigmoid(logits) - hit_values).astype(jnp.bfloat16), losses


def image_kernel(log_temp, bias, images, mate, *refs):
    texts, (own_part, mate_part, loss) = refs[:-3], refs[-3:]
    rows = texts[0].shape[0]
    temper = jnp.exp(log_temp[...])
    offset = bias[...]
    place = lax.axis_index("blk")
    loss[...] = jnp.zeros_like(loss)
    for block, part in ((mate, mate_part), (images, own_part)):
        labels = labels_of(block, rows)
        total = jnp.zeros((rows, block.shape[1]), jnp.float32)
        for flip, some_texts in zip(LINE, texts):
            index = (place ^ flip) * rows + lax.broadcasted_iota(jnp.int32, (rows, rows), 0)
            products = rows_by_rows(some_texts[...], block[:rows, :])
            slopes, losses = slopes_and_loss(products, temper, offset, index == labels)
            loss[:, :rows] += losses.reshape(rows // 8, 8, rows).sum(axis=0)
            total += columns_by_rows(slopes, some_texts[...])
        part[...] = temper * total


def text_kernel(flip, log_temp, bias, texts, *refs):
    images, part = refs[:-1], refs[-1]
    rows = texts.shape[0]
    temper = jnp.exp(log_temp[...])
    index = (lax.axis_index("blk") ^ flip) * rows + lax.broadcasted_iota(jnp.int32, (rows, rows), 0)
    total = jnp.zeros(part.shape, jnp.float32)
    for block in images:
        products = rows_by_rows(texts[...], block[:rows, :])
        slopes, _ = slopes_and_loss(products, temper, bias[...], index == labels_of(block, rows))
        total += jnp.dot(slopes, block[:rows, :], preferred_element_type=jnp.float32)
    part[...] = temper * total


def call(kernel, arrays, shapes, name, dtype=jnp.float32):
    return pl.pallas_call(
        kernel,
        out_shape=[jax.ShapeDtypeStruct(shape, dtype) for shape in shapes],
        in_specs=[pl.BlockSpec(memory_space=pltpu.VMEM)] * len(arrays),
        out_specs=[pl.BlockSpec(memory_space=pltpu.VMEM)] * len(shapes),
        compiler_params=pltpu.CompilerParams(vmem_limit_bytes=16 * 2**20),
        name=name,
    )(*arrays)


def hop_sum(total, hops):
    for axis, size, bit in hops:
        total = total + swap(total, axis, size, bit)
    return total


def shards(image_embeds, text_embeds, positives, partner, log_temp, bias):
    texts = text_embeds[0]
    labels = positives[0]
    rows = texts.shape[0]
    blocks = lax.axis_size("blk")
    groups = lax.axis_size("group")
    blk_place = lax.axis_index("blk")
    images = with_labels(image_embeds[0], labels)

    def index_of(places):
        return (jnp.stack(places)[:, None] * rows + jnp.arange(rows)[None, :]).reshape(-1)

    def matches(some_labels, index):
        return some_labels[:, None] == index[None, :]

    def grads(slopes, others):
        return temper * jnp.dot(slopes, others, preferred_element_type=jnp.float32)

    packed = after(jnp.concatenate([images, texts]))
    tailed = images.shape[0]
    own_images, own_texts = packed[:rows], packed[tailed:]
    hops = [("blk", blocks, 1)] + [("group", groups, 1 << step) for step in range(groups.bit_length() - 1)]
    hops += [("blk", blocks, 1 << step) for step in range(1, blocks.bit_length() - 1)]
    choice = partner.reshape(1, groups)
    texts_across = swap(texts, "group", groups, 2)
    offer = call(offer_kernel, [choice, own_texts, texts_across], [texts.shape], "offer", texts.dtype)[0]
    offered = swap(offer, "group", groups, 1)
    partner_text = call(choose_kernel, [choice, own_texts, texts_across, offered], [texts.shape], "choose", texts.dtype)[0]
    group_images = lax.all_gather(after(packed[:tailed], partner_text), "group")
    scorer_image = call(scorer_kernel, [choice, group_images], [images.shape], "scorer", images.dtype)[0]

    if blocks == 8:

        def along(array, flip):
            return swap(array, "blk", blocks, flip)

        mate = along(packed, 1)
        text_two_off = along(partner_text, 4)
        text_one_off = along(partner_text, 2)
        text_three_off = along(after(text_two_off, text_one_off, mate, scorer_image), 2)
        image_two_off = along(scorer_image, 4)
        image_one_off = along(after(scorer_image, text_three_off), 2)
        column_texts = [partner_text, text_two_off, text_one_off, after(text_three_off, image_two_off)]
        scalars = (log_temp.reshape(1, 1), bias.reshape(1, 1))
        block_shape = texts.shape
        own_part, mate_part, total = call(
            image_kernel, [*scalars, packed[:tailed], mate[:tailed], *column_texts], [block_shape, block_shape, (8, 128)], "image_side"
        )
        image_three_off = along(image_two_off, 2)
        total = hop_sum(total, hops[:1])
        image_grads = own_part + along(after(mate_part, total), 1)
        total = hop_sum(after(total, image_one_off), hops[1:3])
        column_images = [scorer_image, image_two_off, image_one_off, after(image_three_off, total)]
        mate_part = call(functools.partial(text_kernel, 1), [*scalars, mate[tailed:], *column_images], [block_shape], "text_side_mate")[0]
        own_part = call(functools.partial(text_kernel, 0), [*scalars, own_texts, *column_images], [block_shape], "text_side_own")[0]
        text_grads = own_part + along(mate_part, 1)
        total = hop_sum(after(total, image_grads), hops[3:4])
        total = after(total, own_part)
        hops = hops[:3] + hops[4:]
    else:
        temper = jnp.exp(log_temp[0])
        offset = bias[0]
        all_texts = lax.all_gather(partner_text, "blk", axis=0, tiled=True)
        every_image = lax.all_gather(scorer_image, "blk", axis=0)
        hits = matches(labels, jnp.arange(blocks * rows))
        logits, hit_values, slopes = pair_slopes(own_images, all_texts, hits, temper, offset)
        total = jnp.sum(jax.nn.softplus(logits) - hit_values * logits)
        total = hop_sum(jnp.zeros((8, 128)).at[0, 0].set(total), hops[:3])
        image_grads = grads(slopes, all_texts)
        all_images = every_image[:, :rows].reshape(blocks * rows, -1)
        back_labels = jax.vmap(lambda block: labels_of(block, rows)[0])(every_image).reshape(-1)
        back_hits = matches(index_of([blk_place]), back_labels)
        back_slopes = pair_slopes(own_texts, all_images, back_hits, temper, offset)[2]
        text_grads = grads(back_slopes, all_images)

    total = hop_sum(total, hops[3:])
    loss = jnp.sum(total).reshape(1) / (groups * rows * blocks * blocks)
    return (image_grads[None], text_grads[None], loss)


def solution(mesh):
    in_specs = (P("group", "blk", None), P("group", "blk", None), P("group", "blk"), P(), P(), P())
    out_specs = (P("group", "blk", None), P("group", "blk", None), P())
    return jax.shard_map(shards, mesh=mesh, in_specs=in_specs, out_specs=out_specs, check_vma=False)
```

```python
import functools

import jax
import jax.numpy as jnp
from jax import lax
from jax.experimental import pallas as pl
from jax.experimental.pallas import tpu as pltpu
from jax.sharding import PartitionSpec as P

TAIL = 16
DIGIT = 128


def pair_slopes(rows, others, hits, temper, offset):
    logits = temper * jnp.dot(rows, others.T, preferred_element_type=jnp.float32) + offset
    hit_values = hits.astype(jnp.float32)
    slopes = (jax.nn.sigmoid(logits) - hit_values).astype(jnp.bfloat16)
    return logits, hit_values, slopes


def exchange(array, axis, size, mate):
    return lax.ppermute(array, axis, [(place, mate(place)) for place in range(size)])


def swap(array, axis, size, bit):
    return exchange(array, axis, size, lambda place: place ^ bit)


def after(array, *earlier):
    return lax.optimization_barrier((array, *earlier))[0]


def entry(partner, group):
    lane = lax.broadcasted_iota(jnp.int32, partner.shape, 1)
    return jnp.sum(jnp.where(lane == group, partner[...], 0), axis=1, keepdims=True)


def position(partner, group):
    lane = lax.broadcasted_iota(jnp.int32, partner.shape, 1)
    return jnp.sum(jnp.where(partner[...] == group, lane, 0), axis=1, keepdims=True)


def same_chip(group, other):
    return (group ^ other) >> 1 == 0


def offer_kernel(partner, own, across, out):
    here = lax.axis_index("group")
    out[...] = jnp.where(same_chip(entry(partner, here ^ 1), here), own[...], across[...])


def choose_kernel(partner, own, across, offered, out):
    here = lax.axis_index("group")
    wanted = entry(partner, here)
    held = jnp.where(same_chip(wanted, here), own[...], across[...])
    out[...] = jnp.where((wanted ^ here) & 1 == 0, held, offered[...])


def scorer_kernel(partner, every, out):
    wanted = position(partner, lax.axis_index("group"))
    found = every[0]
    for group in range(1, every.shape[0]):
        found = jnp.where(wanted == group, every[group], found)
    out[...] = found


LINE = (0, 4, 2, 6)


def with_labels(images, labels):
    digits = jnp.stack([labels // DIGIT, labels % DIGIT]).astype(images.dtype)
    return jnp.concatenate([images, jnp.pad(digits, ((0, TAIL - 2), (0, images.shape[1] - labels.shape[0])))])


def labels_of(block, rows):
    digits = block[rows : rows + TAIL, :rows].astype(jnp.int32)
    return digits[:1] * DIGIT + digits[1:2]


def rows_by_rows(left, right):
    return lax.dot_general(left, right, (((1,), (1,)), ((), ())), preferred_element_type=jnp.float32)


def columns_by_rows(left, right):
    return lax.dot_general(left, right, (((0,), (0,)), ((), ())), preferred_element_type=jnp.float32)


def slopes_and_loss(products, temper, offset, hits):
    logits = temper * products + offset
    hit_values = hits.astype(jnp.float32)
    losses = jnp.maximum(logits, 0.0) + jnp.log1p(jnp.exp(-jnp.abs(logits))) - hit_values * logits
    return (jax.nn.sigmoid(logits) - hit_values).astype(jnp.bfloat16), losses


def image_kernel(settings, images, *refs):
    texts, (part, loss) = refs[:-2], refs[-2:]
    rows = texts[0].shape[0]
    temper = jnp.exp(settings[:, :1])
    place = lax.axis_index("blk")
    labels = labels_of(images, rows)
    loss[...] = jnp.zeros_like(loss)
    total = jnp.zeros(part.shape, jnp.float32)
    for flip, some_texts in zip(LINE, texts):
        index = (place ^ flip) * rows + lax.broadcasted_iota(jnp.int32, (rows, rows), 0)
        products = rows_by_rows(some_texts[...], images[:rows, :])
        slopes, losses = slopes_and_loss(products, temper, settings[:, 1:2], index == labels)
        loss[:, :rows] += losses.reshape(rows // 8, 8, rows).sum(axis=0)
        total += columns_by_rows(slopes, some_texts[...])
    part[...] = temper * total


def text_kernel(flip, settings, texts, *refs):
    images, part = refs[:-1], refs[-1]
    rows = texts.shape[0]
    temper = jnp.exp(settings[:, :1])
    index = (lax.axis_index("blk") ^ flip) * rows + lax.broadcasted_iota(jnp.int32, (rows, rows), 0)
    total = jnp.zeros(part.shape, jnp.float32)
    for block in images:
        products = rows_by_rows(texts[...], block[:rows, :])
        slopes, _ = slopes_and_loss(products, temper, settings[:, 1:2], index == labels_of(block, rows))
        total += jnp.dot(slopes, block[:rows, :], preferred_element_type=jnp.float32)
    part[...] = temper * total


def call(kernel, arrays, shapes, name, dtype=jnp.float32):
    return pl.pallas_call(
        kernel,
        out_shape=[jax.ShapeDtypeStruct(shape, dtype) for shape in shapes],
        in_specs=[pl.BlockSpec(memory_space=pltpu.VMEM)] * len(arrays),
        out_specs=[pl.BlockSpec(memory_space=pltpu.VMEM)] * len(shapes),
        compiler_params=pltpu.CompilerParams(vmem_limit_bytes=16 * 2**20),
        name=name,
    )(*arrays)


def hop_sum(total, hops):
    for axis, size, bit in hops:
        total = total + swap(total, axis, size, bit)
    return total


def shards(image_embeds, text_embeds, positives, partner, log_temp, bias):
    texts = text_embeds[0]
    labels = positives[0]
    rows = texts.shape[0]
    blocks = lax.axis_size("blk")
    groups = lax.axis_size("group")
    blk_place = lax.axis_index("blk")
    images = with_labels(image_embeds[0], labels)

    def index_of(places):
        return (jnp.stack(places)[:, None] * rows + jnp.arange(rows)[None, :]).reshape(-1)

    def matches(some_labels, index):
        return some_labels[:, None] == index[None, :]

    def grads(slopes, others):
        return temper * jnp.dot(slopes, others, preferred_element_type=jnp.float32)

    settings = jnp.concatenate([log_temp, bias]).reshape(1, 2)
    packed = after(jnp.concatenate([images, texts]), settings)
    tailed = images.shape[0]
    own_images, own_texts = packed[:rows], packed[tailed:]
    hops = [("blk", blocks, 1)] + [("group", groups, 1 << step) for step in range(groups.bit_length() - 1)]
    hops += [("blk", blocks, 1 << step) for step in range(1, blocks.bit_length() - 1)]
    choice = partner.reshape(1, groups)
    texts_across = swap(texts, "group", groups, 2)
    offer = call(offer_kernel, [choice, own_texts, texts_across], [texts.shape], "offer", texts.dtype)[0]
    offered = swap(offer, "group", groups, 1)
    partner_text = call(choose_kernel, [choice, own_texts, texts_across, offered], [texts.shape], "choose", texts.dtype)[0]
    group_images = lax.all_gather(after(packed[:tailed], partner_text), "group")
    scorer_image = call(scorer_kernel, [choice, group_images], [images.shape], "scorer", images.dtype)[0]

    if blocks == 8:

        def along(array, flip):
            return swap(array, "blk", blocks, flip)

        mate = along(packed, 1)
        text_two_off = along(partner_text, 4)
        text_one_off = along(partner_text, 2)
        text_three_off = along(after(text_two_off, text_one_off, mate, scorer_image), 2)
        image_two_off = along(scorer_image, 4)
        image_one_off = along(after(scorer_image, text_three_off), 2)
        column_texts = [partner_text, text_two_off, text_one_off, text_three_off]
        grad_shape, loss_shape = texts.shape, (8, 128)
        mate_part, mate_loss = call(image_kernel, [settings, mate[:tailed], *column_texts], [grad_shape, loss_shape], "image_side_mate")
        image_two_off = along(scorer_image, 4)
        image_one_off = along(after(scorer_image, text_three_off), 2)
        image_three_off = along(after(image_two_off, mate_part), 2)
        image_part = along(mate_part, 1)
        own_images = after(packed[:tailed], image_two_off)
        own_part, own_loss = call(image_kernel, [settings, own_images, *column_texts], [grad_shape, loss_shape], "image_side_own")
        image_grads = own_part + image_part

        total = hop_sum(after(mate_loss + own_loss, image_part), hops[:1])
        total = hop_sum(after(total, image_one_off), hops[1:2])
        column_images = [scorer_image, image_two_off, image_one_off, after(image_three_off, total)]
        mate_part = call(functools.partial(text_kernel, 1), [settings, mate[tailed:], *column_images], [grad_shape], "text_side_mate")[0]
        own_part = call(functools.partial(text_kernel, 0), [settings, own_texts, *column_images], [grad_shape], "text_side_own")[0]
        text_grads = own_part + along(mate_part, 1)
        total = hop_sum(after(total, mate_part), hops[2:4])
        total = after(total, own_part)
        hops = hops[:2] + hops[4:]
    else:
        temper = jnp.exp(log_temp[0])
        offset = bias[0]
        all_texts = lax.all_gather(partner_text, "blk", axis=0, tiled=True)
        every_image = lax.all_gather(scorer_image, "blk", axis=0)
        hits = matches(labels, jnp.arange(blocks * rows))
        logits, hit_values, slopes = pair_slopes(own_images, all_texts, hits, temper, offset)
        total = jnp.sum(jax.nn.softplus(logits) - hit_values * logits)
        total = hop_sum(jnp.zeros((8, 128)).at[0, 0].set(total), hops[:2])
        image_grads = grads(slopes, all_texts)
        all_images = every_image[:, :rows].reshape(blocks * rows, -1)
        back_labels = jax.vmap(lambda block: labels_of(block, rows)[0])(every_image).reshape(-1)
        back_hits = matches(index_of([blk_place]), back_labels)
        back_slopes = pair_slopes(own_texts, all_images, back_hits, temper, offset)[2]
        text_grads = grads(back_slopes, all_images)

    total = hop_sum(total, hops[2:])
    loss = jnp.sum(total * (1.0 / (groups * rows * blocks * blocks))).reshape(1)
    return (image_grads[None], text_grads[None], loss)


def solution(mesh):
    in_specs = (P("group", "blk", None), P("group", "blk", None), P("group", "blk"), P(), P(), P())
    out_specs = (P("group", "blk", None), P("group", "blk", None), P())
    return jax.shard_map(shards, mesh=mesh, in_specs=in_specs, out_specs=out_specs, check_vma=False)
```

```python
import functools

import jax
import jax.numpy as jnp
from jax import lax
from jax.experimental import pallas as pl
from jax.experimental.pallas import tpu as pltpu
from jax.sharding import PartitionSpec as P

TAIL = 16
DIGIT = 128


def pair_slopes(rows, others, hits, temper, offset):
    logits = temper * jnp.dot(rows, others.T, preferred_element_type=jnp.float32) + offset
    hit_values = hits.astype(jnp.float32)
    slopes = (jax.nn.sigmoid(logits) - hit_values).astype(jnp.bfloat16)
    return logits, hit_values, slopes


def exchange(array, axis, size, mate):
    return lax.ppermute(array, axis, [(place, mate(place)) for place in range(size)])


def swap(array, axis, size, bit):
    return exchange(array, axis, size, lambda place: place ^ bit)


def after(array, *earlier):
    return lax.optimization_barrier((array, *earlier))[0]


def entry(partner, group):
    lane = lax.broadcasted_iota(jnp.int32, partner.shape, 1)
    return jnp.sum(jnp.where(lane == group, partner[...], 0), axis=1, keepdims=True)


def position(partner, group):
    lane = lax.broadcasted_iota(jnp.int32, partner.shape, 1)
    return jnp.sum(jnp.where(partner[...] == group, lane, 0), axis=1, keepdims=True)


def same_chip(group, other):
    return (group ^ other) >> 1 == 0


def offer_kernel(partner, own, across, out):
    here = lax.axis_index("group")
    out[...] = jnp.where(same_chip(entry(partner, here ^ 1), here), own[...], across[...])


def choose_kernel(partner, own, across, offered, out):
    here = lax.axis_index("group")
    wanted = entry(partner, here)
    held = jnp.where(same_chip(wanted, here), own[...], across[...])
    out[...] = jnp.where((wanted ^ here) & 1 == 0, held, offered[...])


def scorer_kernel(partner, every, out):
    wanted = position(partner, lax.axis_index("group"))
    found = every[0]
    for group in range(1, every.shape[0]):
        found = jnp.where(wanted == group, every[group], found)
    out[...] = found


LINE = (0, 4, 2, 6)


def with_labels(images, labels):
    digits = jnp.stack([labels // DIGIT, labels % DIGIT]).astype(images.dtype)
    return jnp.concatenate([images, jnp.pad(digits, ((0, TAIL - 2), (0, images.shape[1] - labels.shape[0])))])


def labels_of(block, rows):
    digits = block[rows : rows + TAIL, :rows].astype(jnp.int32)
    return digits[:1] * DIGIT + digits[1:2]


def rows_by_rows(left, right):
    return lax.dot_general(left, right, (((1,), (1,)), ((), ())), preferred_element_type=jnp.float32)


def columns_by_rows(left, right):
    return lax.dot_general(left, right, (((0,), (0,)), ((), ())), preferred_element_type=jnp.float32)


def slopes_and_loss(products, temper, offset, hits):
    logits = temper * products + offset
    hit_values = hits.astype(jnp.float32)
    losses = jnp.maximum(logits, 0.0) + jnp.log1p(jnp.exp(-jnp.abs(logits))) - hit_values * logits
    return (jax.nn.sigmoid(logits) - hit_values).astype(jnp.bfloat16), losses


def image_kernel(settings, images, mate, *refs):
    texts, (own_part, mate_part, loss) = refs[:-3], refs[-3:]
    rows = texts[0].shape[0]
    temper = jnp.exp(settings[:, :1])
    offset = settings[:, 1:2]
    place = lax.axis_index("blk")
    loss[...] = jnp.zeros_like(loss)
    for block, part in ((mate, mate_part), (images, own_part)):
        labels = labels_of(block, rows)
        total = jnp.zeros((rows, block.shape[1]), jnp.float32)
        for flip, some_texts in zip(LINE, texts):
            index = (place ^ flip) * rows + lax.broadcasted_iota(jnp.int32, (rows, rows), 0)
            products = rows_by_rows(some_texts[...], block[:rows, :])
            slopes, losses = slopes_and_loss(products, temper, offset, index == labels)
            loss[:, :rows] += losses.reshape(rows // 8, 8, rows).sum(axis=0)
            total += columns_by_rows(slopes, some_texts[...])
        part[...] = temper * total


def text_kernel(flip, settings, texts, *refs):
    images, part = refs[:-1], refs[-1]
    rows = texts.shape[0]
    temper = jnp.exp(settings[:, :1])
    index = (lax.axis_index("blk") ^ flip) * rows + lax.broadcasted_iota(jnp.int32, (rows, rows), 0)
    total = jnp.zeros(part.shape, jnp.float32)
    for block in images:
        products = rows_by_rows(texts[...], block[:rows, :])
        slopes, _ = slopes_and_loss(products, temper, settings[:, 1:2], index == labels_of(block, rows))
        total += jnp.dot(slopes, block[:rows, :], preferred_element_type=jnp.float32)
    part[...] = temper * total


def call(kernel, arrays, shapes, name, dtype=jnp.float32):
    return pl.pallas_call(
        kernel,
        out_shape=[jax.ShapeDtypeStruct(shape, dtype) for shape in shapes],
        in_specs=[pl.BlockSpec(memory_space=pltpu.VMEM)] * len(arrays),
        out_specs=[pl.BlockSpec(memory_space=pltpu.VMEM)] * len(shapes),
        compiler_params=pltpu.CompilerParams(vmem_limit_bytes=16 * 2**20),
        name=name,
    )(*arrays)


def hop_sum(total, hops):
    for axis, size, bit in hops:
        total = total + swap(total, axis, size, bit)
    return total


def shards(image_embeds, text_embeds, positives, partner, log_temp, bias):
    texts = text_embeds[0]
    labels = positives[0]
    rows = texts.shape[0]
    blocks = lax.axis_size("blk")
    groups = lax.axis_size("group")
    blk_place = lax.axis_index("blk")
    images = with_labels(image_embeds[0], labels)

    def index_of(places):
        return (jnp.stack(places)[:, None] * rows + jnp.arange(rows)[None, :]).reshape(-1)

    def matches(some_labels, index):
        return some_labels[:, None] == index[None, :]

    def grads(slopes, others):
        return temper * jnp.dot(slopes, others, preferred_element_type=jnp.float32)

    settings = jnp.concatenate([log_temp, bias]).reshape(1, 2)
    packed = after(jnp.concatenate([images, texts]), settings)
    tailed = images.shape[0]
    own_images, own_texts = packed[:rows], packed[tailed:]
    hops = [("blk", blocks, 1)] + [("group", groups, 1 << step) for step in range(groups.bit_length() - 1)]
    hops += [("blk", blocks, 1 << step) for step in range(1, blocks.bit_length() - 1)]
    choice = partner.reshape(1, groups)
    texts_across = swap(texts, "group", groups, 2)
    offer = call(offer_kernel, [choice, own_texts, texts_across], [texts.shape], "offer", texts.dtype)[0]
    offered = swap(offer, "group", groups, 1)
    partner_text = call(choose_kernel, [choice, own_texts, texts_across, offered], [texts.shape], "choose", texts.dtype)[0]
    group_images = lax.all_gather(after(packed[:tailed], partner_text), "group")
    scorer_image = call(scorer_kernel, [choice, group_images], [images.shape], "scorer", images.dtype)[0]

    if blocks == 8:

        def along(array, flip):
            return swap(array, "blk", blocks, flip)

        mate = along(packed, 1)
        text_two_off = along(partner_text, 4)
        text_one_off = along(partner_text, 2)
        text_three_off = along(after(text_two_off, text_one_off, mate, scorer_image), 2)
        image_one_off = along(after(scorer_image, text_three_off), 2)
        image_two_off = along(scorer_image, 4)
        column_texts = [partner_text, text_two_off, text_one_off, after(text_three_off, image_two_off)]
        grad_shape, loss_shape = texts.shape, (8, 128)
        own_part, mate_part, total = call(
            image_kernel, [settings, packed[:tailed], mate[:tailed], *column_texts], [grad_shape, grad_shape, loss_shape], "image_side"
        )
        image_two_off = along(scorer_image, 4)
        image_one_off = along(after(scorer_image, text_three_off), 2)
        image_three_off = along(image_two_off, 2)
        total = hop_sum(total, hops[:1])
        image_part = along(after(mate_part, total), 1)
        image_grads = own_part + image_part

        total = hop_sum(after(total, image_one_off), hops[1:3])
        column_images = [scorer_image, image_two_off, image_one_off, after(image_three_off, total)]
        mate_part = call(functools.partial(text_kernel, 1), [settings, mate[tailed:], *column_images], [grad_shape], "text_side_mate")[0]
        own_part = call(functools.partial(text_kernel, 0), [settings, own_texts, *column_images], [grad_shape], "text_side_own")[0]
        text_grads = own_part + along(mate_part, 1)
        total = hop_sum(after(total, image_grads), hops[3:4])
        total = after(total, own_part)
        hops = hops[4:]
    else:
        temper = jnp.exp(log_temp[0])
        offset = bias[0]
        all_texts = lax.all_gather(partner_text, "blk", axis=0, tiled=True)
        every_image = lax.all_gather(scorer_image, "blk", axis=0)
        hits = matches(labels, jnp.arange(blocks * rows))
        logits, hit_values, slopes = pair_slopes(own_images, all_texts, hits, temper, offset)
        total = jnp.sum(jax.nn.softplus(logits) - hit_values * logits)
        total = jnp.zeros((8, 128)).at[0, 0].set(total)
        image_grads = grads(slopes, all_texts)
        all_images = every_image[:, :rows].reshape(blocks * rows, -1)
        back_labels = jax.vmap(lambda block: labels_of(block, rows)[0])(every_image).reshape(-1)
        back_hits = matches(index_of([blk_place]), back_labels)
        back_slopes = pair_slopes(own_texts, all_images, back_hits, temper, offset)[2]
        text_grads = grads(back_slopes, all_images)

    total = hop_sum(total, hops)
    loss = jnp.sum(total * (1.0 / (groups * rows * blocks * blocks))).reshape(1)
    return (image_grads[None], text_grads[None], loss)


def solution(mesh):
    in_specs = (P("group", "blk", None), P("group", "blk", None), P("group", "blk"), P(), P(), P())
    out_specs = (P("group", "blk", None), P("group", "blk", None), P())
    return jax.shard_map(shards, mesh=mesh, in_specs=in_specs, out_specs=out_specs, check_vma=False)
```

```python
import functools

import jax
import jax.numpy as jnp
from jax import lax
from jax.experimental import pallas as pl
from jax.experimental.pallas import tpu as pltpu
from jax.sharding import PartitionSpec as P

TAIL = 16
DIGIT = 128


def pair_slopes(rows, others, hits, temper, offset):
    logits = temper * jnp.dot(rows, others.T, preferred_element_type=jnp.float32) + offset
    hit_values = hits.astype(jnp.float32)
    slopes = (jax.nn.sigmoid(logits) - hit_values).astype(jnp.bfloat16)
    return logits, hit_values, slopes


def exchange(array, axis, size, mate):
    return lax.ppermute(array, axis, [(place, mate(place)) for place in range(size)])


def swap(array, axis, size, bit):
    return exchange(array, axis, size, lambda place: place ^ bit)


def after(array, *earlier):
    return lax.optimization_barrier((array, *earlier))[0]


def entry(partner, group):
    lane = lax.broadcasted_iota(jnp.int32, partner.shape, 1)
    return jnp.sum(jnp.where(lane == group, partner[...], 0), axis=1, keepdims=True)


def position(partner, group):
    lane = lax.broadcasted_iota(jnp.int32, partner.shape, 1)
    return jnp.sum(jnp.where(partner[...] == group, lane, 0), axis=1, keepdims=True)


def same_chip(group, other):
    return (group ^ other) >> 1 == 0


def offer_kernel(partner, own, across, out):
    here = lax.axis_index("group")
    out[...] = jnp.where(same_chip(entry(partner, here ^ 1), here), own[...], across[...])


def choose_kernel(partner, own, across, offered, out):
    here = lax.axis_index("group")
    wanted = entry(partner, here)
    held = jnp.where(same_chip(wanted, here), own[...], across[...])
    out[...] = jnp.where((wanted ^ here) & 1 == 0, held, offered[...])


def scorer_kernel(partner, every, out):
    wanted = position(partner, lax.axis_index("group"))
    found = every[0]
    for group in range(1, every.shape[0]):
        found = jnp.where(wanted == group, every[group], found)
    out[...] = found


LINE = (0, 4, 2, 6)


def with_labels(images, labels):
    digits = jnp.stack([labels // DIGIT, labels % DIGIT]).astype(images.dtype)
    return jnp.concatenate([images, jnp.pad(digits, ((0, TAIL - 2), (0, images.shape[1] - labels.shape[0])))])


def labels_of(block, rows):
    digits = block[rows : rows + TAIL, :rows].astype(jnp.int32)
    return digits[:1] * DIGIT + digits[1:2]


def rows_by_rows(left, right):
    return lax.dot_general(left, right, (((1,), (1,)), ((), ())), preferred_element_type=jnp.float32)


def columns_by_rows(left, right):
    return lax.dot_general(left, right, (((0,), (0,)), ((), ())), preferred_element_type=jnp.float32)


def slopes_and_loss(products, temper, offset, hits):
    logits = temper * products + offset
    hit_values = hits.astype(jnp.float32)
    losses = jnp.maximum(logits, 0.0) + jnp.log1p(jnp.exp(-jnp.abs(logits))) - hit_values * logits
    return (jax.nn.sigmoid(logits) - hit_values).astype(jnp.bfloat16), losses


def image_kernel(settings, images, mate, *refs):
    texts, (own_part, mate_part, loss) = refs[:-3], refs[-3:]
    rows = texts[0].shape[0]
    temper = jnp.exp(settings[:, :1])
    offset = settings[:, 1:2]
    place = lax.axis_index("blk")
    loss[...] = jnp.zeros_like(loss)
    for block, part in ((mate, mate_part), (images, own_part)):
        labels = labels_of(block, rows)
        total = jnp.zeros((rows, block.shape[1]), jnp.float32)
        for flip, some_texts in zip(LINE, texts):
            index = (place ^ flip) * rows + lax.broadcasted_iota(jnp.int32, (rows, rows), 0)
            products = rows_by_rows(some_texts[...], block[:rows, :])
            slopes, losses = slopes_and_loss(products, temper, offset, index == labels)
            loss[:, :rows] += losses.reshape(rows // 8, 8, rows).sum(axis=0)
            total += columns_by_rows(slopes, some_texts[...])
        part[...] = temper * total


def text_kernel(flip, count, settings, texts, *refs):
    images, earlier, part = refs[:count], refs[count:-1], refs[-1]
    rows = texts.shape[0]
    temper = jnp.exp(settings[:, :1])
    index = (lax.axis_index("blk") ^ flip) * rows + lax.broadcasted_iota(jnp.int32, (rows, rows), 0)
    total = jnp.zeros(part.shape, jnp.float32)
    for block in images:
        products = rows_by_rows(texts[...], block[:rows, :])
        slopes, _ = slopes_and_loss(products, temper, settings[:, 1:2], index == labels_of(block, rows))
        total += jnp.dot(slopes, block[:rows, :], preferred_element_type=jnp.float32)
    part[...] = temper * total + earlier[0][...] if earlier else temper * total


def call(kernel, arrays, shapes, name, dtype=jnp.float32):
    return pl.pallas_call(
        kernel,
        out_shape=[jax.ShapeDtypeStruct(shape, dtype) for shape in shapes],
        in_specs=[pl.BlockSpec(memory_space=pltpu.VMEM)] * len(arrays),
        out_specs=[pl.BlockSpec(memory_space=pltpu.VMEM)] * len(shapes),
        compiler_params=pltpu.CompilerParams(vmem_limit_bytes=16 * 2**20),
        name=name,
    )(*arrays)


def hop_sum(total, hops):
    for axis, size, bit in hops:
        total = total + swap(total, axis, size, bit)
    return total


def shards(image_embeds, text_embeds, positives, partner, log_temp, bias):
    texts = text_embeds[0]
    labels = positives[0]
    rows = texts.shape[0]
    blocks = lax.axis_size("blk")
    groups = lax.axis_size("group")
    blk_place = lax.axis_index("blk")
    images = with_labels(image_embeds[0], labels)

    def index_of(places):
        return (jnp.stack(places)[:, None] * rows + jnp.arange(rows)[None, :]).reshape(-1)

    def matches(some_labels, index):
        return some_labels[:, None] == index[None, :]

    def grads(slopes, others):
        return temper * jnp.dot(slopes, others, preferred_element_type=jnp.float32)

    settings = jnp.concatenate([log_temp, bias]).reshape(1, 2)
    packed = after(jnp.concatenate([images, texts]), settings)
    tailed = images.shape[0]
    own_images, own_texts = packed[:rows], packed[tailed:]
    hops = [("group", groups, 1 << step) for step in range(groups.bit_length() - 1)] + [("blk", blocks, 2), ("blk", blocks, 1)]
    hops += [("blk", blocks, 1 << step) for step in range(2, blocks.bit_length() - 1)]
    choice = partner.reshape(1, groups)
    texts_across = swap(texts, "group", groups, 2)
    offer = call(offer_kernel, [choice, own_texts, texts_across], [texts.shape], "offer", texts.dtype)[0]
    offered = swap(offer, "group", groups, 1)
    partner_text = call(choose_kernel, [choice, own_texts, texts_across, offered], [texts.shape], "choose", texts.dtype)[0]
    group_images = lax.all_gather(after(packed[:tailed], partner_text), "group")
    scorer_image = call(scorer_kernel, [choice, group_images], [images.shape], "scorer", images.dtype)[0]

    if blocks == 8:

        def along(array, flip):
            return swap(array, "blk", blocks, flip)

        mate = along(packed, 1)
        text_two_off = along(partner_text, 4)
        text_one_off = along(partner_text, 2)
        text_three_off = along(after(text_two_off, text_one_off, mate, scorer_image), 2)
        image_one_off = along(after(scorer_image, text_three_off), 2)
        image_two_off = along(scorer_image, 4)
        column_texts = [partner_text, text_two_off, text_one_off, after(text_three_off, image_two_off)]
        grad_shape, loss_shape = texts.shape, (8, 128)
        own_part, mate_part, total = call(
            image_kernel, [settings, packed[:tailed], mate[:tailed], *column_texts], [grad_shape, grad_shape, loss_shape], "image_side"
        )
        image_three_off = along(image_two_off, 2)
        image_part = along(mate_part, 1)
        image_grads = own_part + image_part

        total = hop_sum(total, hops[:2])
        total = hop_sum(after(total, image_one_off), hops[2:4])
        early_images = [scorer_image, image_two_off, image_one_off]
        mate_part = call(functools.partial(text_kernel, 1, 3), [settings, mate[tailed:], *early_images], [grad_shape], "text_side_early")[0]
        last_image = after(image_three_off, total)
        mate_part = call(functools.partial(text_kernel, 1, 1), [settings, mate[tailed:], last_image, mate_part], [grad_shape], "text_side_mate")[0]
        column_images = early_images + [last_image]
        own_part = call(functools.partial(text_kernel, 0, 4), [settings, own_texts, *column_images], [grad_shape], "text_side_own")[0]
        text_grads = own_part + along(mate_part, 1)
        total = after(total, image_grads, own_part)
        hops = hops[4:]
    else:
        temper = jnp.exp(log_temp[0])
        offset = bias[0]
        all_texts = lax.all_gather(partner_text, "blk", axis=0, tiled=True)
        every_image = lax.all_gather(scorer_image, "blk", axis=0)
        hits = matches(labels, jnp.arange(blocks * rows))
        logits, hit_values, slopes = pair_slopes(own_images, all_texts, hits, temper, offset)
        total = jnp.sum(jax.nn.softplus(logits) - hit_values * logits)
        total = jnp.zeros((8, 128)).at[0, 0].set(total)
        image_grads = grads(slopes, all_texts)
        all_images = every_image[:, :rows].reshape(blocks * rows, -1)
        back_labels = jax.vmap(lambda block: labels_of(block, rows)[0])(every_image).reshape(-1)
        back_hits = matches(index_of([blk_place]), back_labels)
        back_slopes = pair_slopes(own_texts, all_images, back_hits, temper, offset)[2]
        text_grads = grads(back_slopes, all_images)

    total = hop_sum(total, hops)
    loss = jnp.sum(total * (1.0 / (groups * rows * blocks * blocks))).reshape(1)
    return (image_grads[None], text_grads[None], loss)


def solution(mesh):
    in_specs = (P("group", "blk", None), P("group", "blk", None), P("group", "blk"), P(), P(), P())
    out_specs = (P("group", "blk", None), P("group", "blk", None), P())
    return jax.shard_map(shards, mesh=mesh, in_specs=in_specs, out_specs=out_specs, check_vma=False)
```

```python
import functools

import jax
import jax.numpy as jnp
from jax import lax
from jax.experimental import pallas as pl
from jax.experimental.pallas import tpu as pltpu
from jax.sharding import PartitionSpec as P

TAIL = 16
DIGIT = 128
LANES = 128


def pair_slopes(rows, others, hits, temper, offset):
    logits = temper * jnp.dot(rows, others.T, preferred_element_type=jnp.float32) + offset
    hit_values = hits.astype(jnp.float32)
    slopes = (jax.nn.sigmoid(logits) - hit_values).astype(jnp.bfloat16)
    return logits, hit_values, slopes


def exchange(array, axis, size, mate):
    return lax.ppermute(array, axis, [(place, mate(place)) for place in range(size)])


def swap(array, axis, size, bit):
    return exchange(array, axis, size, lambda place: place ^ bit)


def after(array, *earlier):
    return lax.optimization_barrier((array, *earlier))[0]


def entry(partner, group):
    lane = lax.broadcasted_iota(jnp.int32, partner.shape, 1)
    return jnp.sum(jnp.where(lane == group, partner[...], 0), axis=1, keepdims=True)


def position(partner, group):
    lane = lax.broadcasted_iota(jnp.int32, partner.shape, 1)
    return jnp.sum(jnp.where(partner[...] == group, lane, 0), axis=1, keepdims=True)


def same_chip(group, other):
    return (group ^ other) >> 1 == 0


def offer_kernel(partner, own, across, out):
    here = lax.axis_index("group")
    out[...] = jnp.where(same_chip(entry(partner, here ^ 1), here), own[...], across[...])


def choose_kernel(partner, own, across, offered, out):
    here = lax.axis_index("group")
    wanted = entry(partner, here)
    held = jnp.where(same_chip(wanted, here), own[...], across[...])
    out[...] = jnp.where((wanted ^ here) & 1 == 0, held, offered[...])


def scorer_kernel(partner, every, out):
    wanted = position(partner, lax.axis_index("group"))
    found = every[0]
    for group in range(1, every.shape[0]):
        found = jnp.where(wanted == group, every[group], found)
    out[...] = found


LINE = (0, 4, 2, 6)


def with_labels(images, labels):
    digits = jnp.stack([labels // DIGIT, labels % DIGIT]).astype(images.dtype)
    return jnp.concatenate([images, jnp.pad(digits, ((0, TAIL - 2), (0, images.shape[1] - labels.shape[0])))])


def labels_of(block, rows, width):
    digits = block[rows : rows + TAIL, :width].astype(jnp.int32)
    return digits[:1] * DIGIT + digits[1:2]


def rows_by_rows(left, right):
    return lax.dot_general(left, right, (((1,), (1,)), ((), ())), preferred_element_type=jnp.float32)


def stack(blocks, rows, into):
    for place, block in enumerate(blocks):
        into[place * rows : (place + 1) * rows, :] = block[:rows, :]


def image_kernel(settings, images, mate, *refs):
    texts, (own_part, mate_part, loss, all_images, all_texts) = refs[:-5], refs[-5:]
    rows = texts[0].shape[0]
    temper = jnp.exp(settings[:, :1])
    stack((images, mate), rows, all_images)
    stack(texts, rows, all_texts)
    labels = jnp.concatenate([jnp.broadcast_to(labels_of(block, rows, LANES), (LANES, LANES)).T[:rows] for block in (images, mate)])
    labels = jnp.concatenate([labels] * (all_texts.shape[0] // LANES), axis=1)
    column = lax.broadcasted_iota(jnp.int32, labels.shape, 1)
    index = column
    for place, flip in enumerate(LINE):
        start = place * rows
        index = jnp.where(column >= start, column - start + (lax.axis_index("blk") ^ flip) * rows, index)

    logits = temper * rows_by_rows(all_images[...], all_texts[...]) + settings[:, 1:2]
    hit_values = (index == labels).astype(jnp.float32)
    small = jnp.exp(-jnp.abs(logits))
    losses = jnp.maximum(logits, 0.0) + jnp.log1p(small) - hit_values * logits
    slopes = jnp.where(logits >= 0.0, 1.0, small) / (1.0 + small) - hit_values
    total = losses.reshape(-1, 8, losses.shape[1]).sum(axis=0)
    loss[...] = sum(total[:, lane : lane + LANES] for lane in range(0, total.shape[1], LANES))
    grads = temper * jnp.dot(slopes.astype(jnp.bfloat16), all_texts[...], preferred_element_type=jnp.float32)
    own_part[...] = grads[:rows]
    mate_part[...] = grads[rows:]


def text_kernel(flip, count, settings, texts, *refs):
    images, earlier, part = refs[:count], refs[count:-1], refs[-1]
    rows = texts.shape[0]
    temper = jnp.exp(settings[:, :1])
    index = (lax.axis_index("blk") ^ flip) * rows + lax.broadcasted_iota(jnp.int32, (rows, rows), 0)
    total = jnp.zeros(part.shape, jnp.float32)
    for block in images:
        products = rows_by_rows(texts[...], block[:rows, :])
        hits = index == labels_of(block, rows, rows)
        slopes = (jax.nn.sigmoid(temper * products + settings[:, 1:2]) - hits.astype(jnp.float32)).astype(jnp.bfloat16)
        total += jnp.dot(slopes, block[:rows, :], preferred_element_type=jnp.float32)
    part[...] = temper * total + earlier[0][...] if earlier else temper * total


def call(kernel, arrays, shapes, name, dtype=jnp.float32, scratch=()):
    return pl.pallas_call(
        kernel,
        out_shape=[jax.ShapeDtypeStruct(shape, dtype) for shape in shapes],
        in_specs=[pl.BlockSpec(memory_space=pltpu.VMEM)] * len(arrays),
        out_specs=[pl.BlockSpec(memory_space=pltpu.VMEM)] * len(shapes),
        scratch_shapes=[pltpu.VMEM(shape, jnp.bfloat16) for shape in scratch],
        compiler_params=pltpu.CompilerParams(vmem_limit_bytes=16 * 2**20),
        name=name,
    )(*arrays)


def hop_sum(total, hops):
    for axis, size, bit in hops:
        total = total + swap(total, axis, size, bit)
    return total


def shards(image_embeds, text_embeds, positives, partner, log_temp, bias):
    texts = text_embeds[0]
    labels = positives[0]
    rows = texts.shape[0]
    blocks = lax.axis_size("blk")
    groups = lax.axis_size("group")
    blk_place = lax.axis_index("blk")
    images = with_labels(image_embeds[0], labels)

    def index_of(places):
        return (jnp.stack(places)[:, None] * rows + jnp.arange(rows)[None, :]).reshape(-1)

    def matches(some_labels, index):
        return some_labels[:, None] == index[None, :]

    def grads(slopes, others):
        return temper * jnp.dot(slopes, others, preferred_element_type=jnp.float32)

    settings = jnp.concatenate([log_temp, bias]).reshape(1, 2)
    packed = after(jnp.concatenate([images, texts]), settings)
    tailed = images.shape[0]
    own_images, own_texts = packed[:rows], packed[tailed:]
    hops = [("group", groups, 1 << step) for step in range(groups.bit_length() - 1)]
    hops += [("blk", blocks, 1 << step) for step in range(blocks.bit_length() - 1)]
    choice = partner.reshape(1, groups)
    texts_across = swap(texts, "group", groups, 2)
    offer = call(offer_kernel, [choice, own_texts, texts_across], [texts.shape], "offer", texts.dtype)[0]
    offered = swap(offer, "group", groups, 1)
    partner_text = call(choose_kernel, [choice, own_texts, texts_across, offered], [texts.shape], "choose", texts.dtype)[0]
    group_images = lax.all_gather(after(packed[:tailed], partner_text), "group")
    scorer_image = call(scorer_kernel, [choice, group_images], [images.shape], "scorer", images.dtype)[0]

    if blocks == 8:

        def along(array, flip):
            return swap(array, "blk", blocks, flip)

        mate = along(packed, 1)
        text_two_off = along(partner_text, 4)
        text_one_off = along(partner_text, 2)
        text_three_off = along(after(text_two_off, text_one_off, mate, scorer_image), 2)
        image_one_off = along(after(scorer_image, text_three_off), 2)
        image_two_off = along(scorer_image, 4)
        column_texts = [partner_text, text_two_off, text_one_off, after(text_three_off, image_two_off)]
        grad_shape = texts.shape
        own_part, mate_part, total = call(
            image_kernel,
            [settings, packed[:tailed], mate[:tailed], *column_texts],
            [grad_shape, grad_shape, (8, LANES)],
            "image_side",
            scratch=[(2 * rows, texts.shape[1]), (len(LINE) * rows, texts.shape[1])],
        )
        image_three_off = along(image_two_off, 2)
        image_part = along(mate_part, 1)
        image_grads = own_part + image_part

        total = hop_sum(total, hops[:2])
        total = hop_sum(after(total, image_one_off), hops[2:3])
        early_images = [scorer_image, image_two_off, image_one_off]
        mate_part = call(functools.partial(text_kernel, 1, 3), [settings, mate[tailed:], *early_images], [grad_shape], "text_side_early")[0]
        last_image = after(image_three_off, total)
        mate_part = call(functools.partial(text_kernel, 1, 1), [settings, mate[tailed:], last_image, mate_part], [grad_shape], "text_side_mate")[0]
        column_images = early_images + [last_image]
        own_part = call(functools.partial(text_kernel, 0, 4), [settings, own_texts, *column_images], [grad_shape], "text_side_own")[0]
        text_grads = own_part + along(mate_part, 1)
        total = after(hop_sum(after(total, image_grads), hops[3:4]), own_part)
        hops = hops[4:]
    else:
        temper = jnp.exp(log_temp[0])
        offset = bias[0]
        all_texts = lax.all_gather(partner_text, "blk", axis=0, tiled=True)
        every_image = lax.all_gather(scorer_image, "blk", axis=0)
        hits = matches(labels, jnp.arange(blocks * rows))
        logits, hit_values, slopes = pair_slopes(own_images, all_texts, hits, temper, offset)
        total = jnp.sum(jax.nn.softplus(logits) - hit_values * logits)
        total = jnp.zeros((8, 128)).at[0, 0].set(total)
        image_grads = grads(slopes, all_texts)
        all_images = every_image[:, :rows].reshape(blocks * rows, -1)
        back_labels = jax.vmap(lambda block: labels_of(block, rows, rows)[0])(every_image).reshape(-1)
        back_hits = matches(index_of([blk_place]), back_labels)
        back_slopes = pair_slopes(own_texts, all_images, back_hits, temper, offset)[2]
        text_grads = grads(back_slopes, all_images)

    total = hop_sum(total, hops)
    loss = jnp.sum(total * (1.0 / (groups * rows * blocks * blocks))).reshape(1)
    return (image_grads[None], text_grads[None], loss)


def solution(mesh):
    in_specs = (P("group", "blk", None), P("group", "blk", None), P("group", "blk"), P(), P(), P())
    out_specs = (P("group", "blk", None), P("group", "blk", None), P())
    return jax.shard_map(shards, mesh=mesh, in_specs=in_specs, out_specs=out_specs, check_vma=False)
```

```python
import functools

import jax
import jax.numpy as jnp
from jax import lax
from jax.experimental import pallas as pl
from jax.experimental.pallas import tpu as pltpu
from jax.sharding import PartitionSpec as P

TAIL = 16
DIGIT = 128
LANES = 128


def pair_slopes(rows, others, hits, temper, offset):
    logits = temper * jnp.dot(rows, others.T, preferred_element_type=jnp.float32) + offset
    hit_values = hits.astype(jnp.float32)
    slopes = (jax.nn.sigmoid(logits) - hit_values).astype(jnp.bfloat16)
    return logits, hit_values, slopes


def exchange(array, axis, size, mate):
    return lax.ppermute(array, axis, [(place, mate(place)) for place in range(size)])


def swap(array, axis, size, bit):
    return exchange(array, axis, size, lambda place: place ^ bit)


def after(array, *earlier):
    return lax.optimization_barrier((array, *earlier))[0]


def entry(partner, group):
    lane = lax.broadcasted_iota(jnp.int32, partner.shape, 1)
    return jnp.sum(jnp.where(lane == group, partner[...], 0), axis=1, keepdims=True)


def position(partner, group):
    lane = lax.broadcasted_iota(jnp.int32, partner.shape, 1)
    return jnp.sum(jnp.where(partner[...] == group, lane, 0), axis=1, keepdims=True)


def same_chip(group, other):
    return (group ^ other) >> 1 == 0


def offer_kernel(partner, own, across, out):
    here = lax.axis_index("group")
    out[...] = jnp.where(same_chip(entry(partner, here ^ 1), here), own[...], across[...])


def choose_kernel(partner, own, across, offered, out):
    here = lax.axis_index("group")
    wanted = entry(partner, here)
    held = jnp.where(same_chip(wanted, here), own[...], across[...])
    out[...] = jnp.where((wanted ^ here) & 1 == 0, held, offered[...])


def scorer_kernel(partner, every, out):
    wanted = position(partner, lax.axis_index("group"))
    found = every[0]
    for group in range(1, every.shape[0]):
        found = jnp.where(wanted == group, every[group], found)
    out[...] = found


LINE = (0, 4, 2, 6)


def with_labels(images, labels):
    digits = jnp.stack([labels // DIGIT, labels % DIGIT]).astype(images.dtype)
    return jnp.concatenate([images, jnp.pad(digits, ((0, TAIL - 2), (0, images.shape[1] - labels.shape[0])))])


def labels_of(block, rows, width):
    digits = block[rows : rows + TAIL, :width].astype(jnp.int32)
    return digits[:1] * DIGIT + digits[1:2]


def rows_by_rows(left, right):
    return lax.dot_general(left, right, (((1,), (1,)), ((), ())), preferred_element_type=jnp.float32)


def stack(blocks, rows, into):
    for place, block in enumerate(blocks):
        into[place * rows : (place + 1) * rows, :] = block[:rows, :]


def image_kernel(settings, images, mate, *refs):
    texts, (own_part, mate_part, loss, all_images, all_texts) = refs[:-5], refs[-5:]
    rows = texts[0].shape[0]
    temper = jnp.exp(settings[:, :1])
    stack((images, mate), rows, all_images)
    stack(texts, rows, all_texts)
    labels = jnp.concatenate([jnp.broadcast_to(labels_of(block, rows, LANES), (LANES, LANES)).T[:rows] for block in (images, mate)])
    labels = jnp.concatenate([labels] * (all_texts.shape[0] // LANES), axis=1)
    column = lax.broadcasted_iota(jnp.int32, labels.shape, 1)
    index = column
    for place, flip in enumerate(LINE):
        start = place * rows
        index = jnp.where(column >= start, column - start + (lax.axis_index("blk") ^ flip) * rows, index)

    logits = temper * rows_by_rows(all_images[...], all_texts[...]) + settings[:, 1:2]
    hit_values = (index == labels).astype(jnp.float32)
    small = jnp.exp(-jnp.abs(logits))
    losses = jnp.maximum(logits, 0.0) + jnp.log1p(small) - hit_values * logits
    slopes = jnp.where(logits >= 0.0, 1.0, small) / (1.0 + small) - hit_values
    total = losses.reshape(-1, 8, losses.shape[1]).sum(axis=0)
    loss[...] = sum(total[:, lane : lane + LANES] for lane in range(0, total.shape[1], LANES))
    grads = temper * jnp.dot(slopes.astype(jnp.bfloat16), all_texts[...], preferred_element_type=jnp.float32)
    own_part[...] = grads[:rows]
    mate_part[...] = grads[rows:]


def text_kernel(flip, count, settings, texts, *refs):
    images, earlier, part = refs[:count], refs[count:-1], refs[-1]
    rows = texts.shape[0]
    temper = jnp.exp(settings[:, :1])
    index = (lax.axis_index("blk") ^ flip) * rows + lax.broadcasted_iota(jnp.int32, (rows, rows), 0)
    total = jnp.zeros(part.shape, jnp.float32)
    for block in images:
        products = rows_by_rows(texts[...], block[:rows, :])
        hits = index == labels_of(block, rows, rows)
        slopes = (jax.nn.sigmoid(temper * products + settings[:, 1:2]) - hits.astype(jnp.float32)).astype(jnp.bfloat16)
        total += jnp.dot(slopes, block[:rows, :], preferred_element_type=jnp.float32)
    part[...] = temper * total + earlier[0][...] if earlier else temper * total


def call(kernel, arrays, shapes, name, dtype=jnp.float32, scratch=()):
    return pl.pallas_call(
        kernel,
        out_shape=[jax.ShapeDtypeStruct(shape, dtype) for shape in shapes],
        in_specs=[pl.BlockSpec(memory_space=pltpu.VMEM)] * len(arrays),
        out_specs=[pl.BlockSpec(memory_space=pltpu.VMEM)] * len(shapes),
        scratch_shapes=[pltpu.VMEM(shape, jnp.bfloat16) for shape in scratch],
        compiler_params=pltpu.CompilerParams(vmem_limit_bytes=16 * 2**20),
        name=name,
    )(*arrays)


def hop_sum(total, hops):
    for axis, size, bit in hops:
        total = total + swap(total, axis, size, bit)
    return total


def shards(image_embeds, text_embeds, positives, partner, log_temp, bias):
    texts = text_embeds[0]
    labels = positives[0]
    rows = texts.shape[0]
    blocks = lax.axis_size("blk")
    groups = lax.axis_size("group")
    blk_place = lax.axis_index("blk")
    images = with_labels(image_embeds[0], labels)

    def index_of(places):
        return (jnp.stack(places)[:, None] * rows + jnp.arange(rows)[None, :]).reshape(-1)

    def matches(some_labels, index):
        return some_labels[:, None] == index[None, :]

    def grads(slopes, others):
        return temper * jnp.dot(slopes, others, preferred_element_type=jnp.float32)

    settings = jnp.concatenate([log_temp, bias]).reshape(1, 2)
    packed = after(jnp.concatenate([images, texts]), settings)
    tailed = images.shape[0]
    own_images, own_texts = packed[:rows], packed[tailed:]
    hops = [("group", groups, 1 << step) for step in range(groups.bit_length() - 1)]
    hops += [("blk", blocks, 1 << step) for step in range(blocks.bit_length() - 1)]
    choice = partner.reshape(1, groups)
    texts_across = swap(texts, "group", groups, 2)
    offer = call(offer_kernel, [choice, own_texts, texts_across], [texts.shape], "offer", texts.dtype)[0]
    offered = swap(offer, "group", groups, 1)
    partner_text = call(choose_kernel, [choice, own_texts, texts_across, offered], [texts.shape], "choose", texts.dtype)[0]
    group_images = lax.all_gather(after(packed[:tailed], partner_text), "group")
    scorer_image = call(scorer_kernel, [choice, group_images], [images.shape], "scorer", images.dtype)[0]

    if blocks == 8:

        def along(array, flip):
            return swap(array, "blk", blocks, flip)

        mate = along(packed, 1)
        text_two_off = along(partner_text, 4)
        text_one_off = along(partner_text, 2)
        text_three_off = along(after(text_two_off, text_one_off, mate, scorer_image), 2)
        image_one_off = along(after(scorer_image, text_three_off), 2)
        image_two_off = along(scorer_image, 4)
        column_texts = [partner_text, text_two_off, text_one_off, after(text_three_off, image_two_off)]
        grad_shape = texts.shape
        own_part, mate_part, total = call(
            image_kernel,
            [settings, packed[:tailed], mate[:tailed], *column_texts],
            [grad_shape, grad_shape, (8, LANES)],
            "image_side",
            scratch=[(2 * rows, texts.shape[1]), (len(LINE) * rows, texts.shape[1])],
        )
        image_three_off = along(image_two_off, 2)
        cut = rows * 2 // 3
        first_part = along(mate_part[:cut], 1)
        total = hop_sum(total, hops[:2])
        total = hop_sum(after(total, image_one_off), hops[2:3])
        early_images = [scorer_image, image_two_off, image_one_off]
        early_part = call(functools.partial(text_kernel, 1, 3), [settings, mate[tailed:], *early_images], [grad_shape], "text_side_early")[0]
        last_image = after(image_three_off, total, early_part)
        second_part = along(after(mate_part[cut:], last_image), 1)
        image_grads = own_part + jnp.concatenate([first_part, second_part])
        mate_part = call(functools.partial(text_kernel, 1, 1), [settings, mate[tailed:], last_image, early_part], [grad_shape], "text_side_mate")[0]
        column_images = early_images + [last_image]
        own_part = call(functools.partial(text_kernel, 0, 4), [settings, own_texts, *column_images], [grad_shape], "text_side_own")[0]
        text_grads = own_part + along(mate_part, 1)
        total = after(hop_sum(after(total, image_grads), hops[3:4]), own_part)
        hops = hops[4:]
    else:
        temper = jnp.exp(log_temp[0])
        offset = bias[0]
        all_texts = lax.all_gather(partner_text, "blk", axis=0, tiled=True)
        every_image = lax.all_gather(scorer_image, "blk", axis=0)
        hits = matches(labels, jnp.arange(blocks * rows))
        logits, hit_values, slopes = pair_slopes(own_images, all_texts, hits, temper, offset)
        total = jnp.sum(jax.nn.softplus(logits) - hit_values * logits)
        total = jnp.zeros((8, 128)).at[0, 0].set(total)
        image_grads = grads(slopes, all_texts)
        all_images = every_image[:, :rows].reshape(blocks * rows, -1)
        back_labels = jax.vmap(lambda block: labels_of(block, rows, rows)[0])(every_image).reshape(-1)
        back_hits = matches(index_of([blk_place]), back_labels)
        back_slopes = pair_slopes(own_texts, all_images, back_hits, temper, offset)[2]
        text_grads = grads(back_slopes, all_images)

    total = hop_sum(total, hops)
    loss = jnp.sum(total * (1.0 / (groups * rows * blocks * blocks))).reshape(1)
    return (image_grads[None], text_grads[None], loss)


def solution(mesh):
    in_specs = (P("group", "blk", None), P("group", "blk", None), P("group", "blk"), P(), P(), P())
    out_specs = (P("group", "blk", None), P("group", "blk", None), P())
    return jax.shard_map(shards, mesh=mesh, in_specs=in_specs, out_specs=out_specs, check_vma=False)
```

```python
import functools

import jax
import jax.numpy as jnp
from jax import lax
from jax.experimental import pallas as pl
from jax.experimental.pallas import tpu as pltpu
from jax.sharding import PartitionSpec as P

TAIL = 16
DIGIT = 128
LANES = 128


def pair_slopes(rows, others, hits, temper, offset):
    logits = temper * jnp.dot(rows, others.T, preferred_element_type=jnp.float32) + offset
    hit_values = hits.astype(jnp.float32)
    slopes = (jax.nn.sigmoid(logits) - hit_values).astype(jnp.bfloat16)
    return logits, hit_values, slopes


def exchange(array, axis, size, mate):
    return lax.ppermute(array, axis, [(place, mate(place)) for place in range(size)])


def swap(array, axis, size, bit):
    return exchange(array, axis, size, lambda place: place ^ bit)


def after(array, *earlier):
    return lax.optimization_barrier((array, *earlier))[0]


def entry(partner, group):
    lane = lax.broadcasted_iota(jnp.int32, partner.shape, 1)
    return jnp.sum(jnp.where(lane == group, partner[...], 0), axis=1, keepdims=True)


def position(partner, group):
    lane = lax.broadcasted_iota(jnp.int32, partner.shape, 1)
    return jnp.sum(jnp.where(partner[...] == group, lane, 0), axis=1, keepdims=True)


def same_chip(group, other):
    return (group ^ other) >> 1 == 0


def offer_kernel(partner, own, across, out):
    here = lax.axis_index("group")
    out[...] = jnp.where(same_chip(entry(partner, here ^ 1), here), own[...], across[...])


def choose_kernel(partner, own, across, offered, out):
    here = lax.axis_index("group")
    wanted = entry(partner, here)
    held = jnp.where(same_chip(wanted, here), own[...], across[...])
    out[...] = jnp.where((wanted ^ here) & 1 == 0, held, offered[...])


def scorer_kernel(partner, every, out):
    wanted = position(partner, lax.axis_index("group"))
    found = every[0]
    for group in range(1, every.shape[0]):
        found = jnp.where(wanted == group, every[group], found)
    out[...] = found


LINE = (0, 4, 2, 6)


def with_labels(images, labels):
    digits = jnp.stack([labels // DIGIT, labels % DIGIT]).astype(images.dtype)
    return jnp.concatenate([images, jnp.pad(digits, ((0, TAIL - 2), (0, images.shape[1] - labels.shape[0])))])


def labels_of(block, rows, width):
    digits = block[rows : rows + TAIL, :width].astype(jnp.int32)
    return digits[:1] * DIGIT + digits[1:2]


def rows_by_rows(left, right):
    return lax.dot_general(left, right, (((1,), (1,)), ((), ())), preferred_element_type=jnp.float32)


def stack(blocks, rows, into):
    for place, block in enumerate(blocks):
        into[place * rows : (place + 1) * rows, :] = block[:rows, :]


def image_kernel(settings, images, mate, *refs):
    texts, (own_part, mate_part, loss, all_images, all_texts) = refs[:-5], refs[-5:]
    rows = texts[0].shape[0]
    temper = jnp.exp(settings[:, :1])
    stack((images, mate), rows, all_images)
    stack(texts, rows, all_texts)
    labels = jnp.concatenate([jnp.broadcast_to(labels_of(block, rows, LANES), (LANES, LANES)).T[:rows] for block in (images, mate)])
    labels = jnp.concatenate([labels] * (all_texts.shape[0] // LANES), axis=1)
    column = lax.broadcasted_iota(jnp.int32, labels.shape, 1)
    index = column
    for place, flip in enumerate(LINE):
        start = place * rows
        index = jnp.where(column >= start, column - start + (lax.axis_index("blk") ^ flip) * rows, index)

    logits = temper * rows_by_rows(all_images[...], all_texts[...]) + settings[:, 1:2]
    hit_values = (index == labels).astype(jnp.float32)
    small = jnp.exp(-jnp.abs(logits))
    losses = jnp.maximum(logits, 0.0) + jnp.log1p(small) - hit_values * logits
    slopes = jnp.where(logits >= 0.0, 1.0, small) / (1.0 + small) - hit_values
    total = losses.reshape(-1, 8, losses.shape[1]).sum(axis=0)
    loss[...] = sum(total[:, lane : lane + LANES] for lane in range(0, total.shape[1], LANES))
    grads = temper * jnp.dot(slopes.astype(jnp.bfloat16), all_texts[...], preferred_element_type=jnp.float32)
    own_part[...] = grads[:rows]
    mate_part[...] = grads[rows:]


def text_kernel(flip, count, settings, texts, *refs):
    images, earlier, part = refs[:count], refs[count:-1], refs[-1]
    rows = texts.shape[0]
    temper = jnp.exp(settings[:, :1])
    index = (lax.axis_index("blk") ^ flip) * rows + lax.broadcasted_iota(jnp.int32, (rows, rows), 0)
    total = jnp.zeros(part.shape, jnp.float32)
    for block in images:
        products = rows_by_rows(texts[...], block[:rows, :])
        hits = index == labels_of(block, rows, rows)
        slopes = (jax.nn.sigmoid(temper * products + settings[:, 1:2]) - hits.astype(jnp.float32)).astype(jnp.bfloat16)
        total += jnp.dot(slopes, block[:rows, :], preferred_element_type=jnp.float32)
    part[...] = temper * total + earlier[0][...] if earlier else temper * total


def finish_kernel(own_text, arrived, first, rest, text_grads, image_grads):
    rows, cut = own_text.shape[0], first.shape[0]
    text_grads[...] = own_text[...] + arrived[:rows]
    image_grads[:cut] = first[...]
    image_grads[cut:] = rest[...] + arrived[rows:]


def call(kernel, arrays, shapes, name, dtype=jnp.float32, scratch=()):
    return pl.pallas_call(
        kernel,
        out_shape=[jax.ShapeDtypeStruct(shape, dtype) for shape in shapes],
        in_specs=[pl.BlockSpec(memory_space=pltpu.VMEM)] * len(arrays),
        out_specs=[pl.BlockSpec(memory_space=pltpu.VMEM)] * len(shapes),
        scratch_shapes=[pltpu.VMEM(shape, jnp.bfloat16) for shape in scratch],
        compiler_params=pltpu.CompilerParams(vmem_limit_bytes=16 * 2**20),
        name=name,
    )(*arrays)


def hop_sum(total, hops):
    for axis, size, bit in hops:
        total = total + swap(total, axis, size, bit)
    return total


def shards(image_embeds, text_embeds, positives, partner, log_temp, bias):
    texts = text_embeds[0]
    labels = positives[0]
    rows = texts.shape[0]
    blocks = lax.axis_size("blk")
    groups = lax.axis_size("group")
    blk_place = lax.axis_index("blk")
    images = with_labels(image_embeds[0], labels)

    def index_of(places):
        return (jnp.stack(places)[:, None] * rows + jnp.arange(rows)[None, :]).reshape(-1)

    def matches(some_labels, index):
        return some_labels[:, None] == index[None, :]

    def grads(slopes, others):
        return temper * jnp.dot(slopes, others, preferred_element_type=jnp.float32)

    settings = jnp.concatenate([log_temp, bias]).reshape(1, 2)
    packed = after(jnp.concatenate([images, texts]), settings)
    tailed = images.shape[0]
    own_images, own_texts = packed[:rows], packed[tailed:]
    hops = [("group", groups, 1 << step) for step in range(groups.bit_length() - 1)]
    hops += [("blk", blocks, 1 << step) for step in range(blocks.bit_length() - 1)]
    choice = partner.reshape(1, groups)
    texts_across = swap(texts, "group", groups, 2)
    offer = call(offer_kernel, [choice, own_texts, texts_across], [texts.shape], "offer", texts.dtype)[0]
    offered = swap(offer, "group", groups, 1)
    partner_text = call(choose_kernel, [choice, own_texts, texts_across, offered], [texts.shape], "choose", texts.dtype)[0]
    group_images = lax.all_gather(after(packed[:tailed], partner_text), "group")
    scorer_image = call(scorer_kernel, [choice, group_images], [images.shape], "scorer", images.dtype)[0]

    if blocks == 8:

        def along(array, flip):
            return swap(array, "blk", blocks, flip)

        mate = along(packed, 1)
        text_two_off = along(partner_text, 4)
        text_one_off = along(partner_text, 2)
        text_three_off = along(after(text_two_off, text_one_off, mate, scorer_image), 2)
        image_one_off = along(after(scorer_image, text_three_off), 2)
        image_two_off = along(scorer_image, 4)
        column_texts = [partner_text, text_two_off, text_one_off, after(text_three_off, image_two_off)]
        grad_shape = texts.shape
        own_part, mate_part, total = call(
            image_kernel,
            [settings, packed[:tailed], mate[:tailed], *column_texts],
            [grad_shape, grad_shape, (8, LANES)],
            "image_side",
            scratch=[(2 * rows, texts.shape[1]), (len(LINE) * rows, texts.shape[1])],
        )
        image_three_off = along(image_two_off, 2)
        cut = rows * 5 // 6
        first_grads = own_part[:cut] + along(mate_part[:cut], 1)
        rest_own, rest = own_part[cut:], mate_part[cut:]
        total = hop_sum(total, hops[:2])
        total = hop_sum(after(total, image_one_off), hops[2:3])
        early_images = [scorer_image, image_two_off, image_one_off]
        early_part = call(functools.partial(text_kernel, 1, 3), [settings, mate[tailed:], *early_images], [grad_shape], "text_side_early")[0]
        last_image = after(image_three_off, total, early_part)
        mate_part = call(functools.partial(text_kernel, 1, 1), [settings, mate[tailed:], last_image, early_part], [grad_shape], "text_side_mate")[0]
        column_images = early_images + [last_image]
        arrived = along(jnp.concatenate([mate_part, rest]), 1)
        own_part = call(functools.partial(text_kernel, 0, 4), [settings, own_texts, *column_images], [grad_shape], "text_side_own")[0]
        text_grads, image_grads = call(
            finish_kernel, [own_part, arrived, first_grads, rest_own], [grad_shape, grad_shape], "finish"
        )
        total = after(hop_sum(after(total, first_grads), hops[3:4]), own_part)
        hops = hops[4:]
    else:
        temper = jnp.exp(log_temp[0])
        offset = bias[0]
        all_texts = lax.all_gather(partner_text, "blk", axis=0, tiled=True)
        every_image = lax.all_gather(scorer_image, "blk", axis=0)
        hits = matches(labels, jnp.arange(blocks * rows))
        logits, hit_values, slopes = pair_slopes(own_images, all_texts, hits, temper, offset)
        total = jnp.sum(jax.nn.softplus(logits) - hit_values * logits)
        total = jnp.zeros((8, 128)).at[0, 0].set(total)
        image_grads = grads(slopes, all_texts)
        all_images = every_image[:, :rows].reshape(blocks * rows, -1)
        back_labels = jax.vmap(lambda block: labels_of(block, rows, rows)[0])(every_image).reshape(-1)
        back_hits = matches(index_of([blk_place]), back_labels)
        back_slopes = pair_slopes(own_texts, all_images, back_hits, temper, offset)[2]
        text_grads = grads(back_slopes, all_images)

    total = hop_sum(total, hops)
    loss = jnp.sum(total * (1.0 / (groups * rows * blocks * blocks))).reshape(1)
    return (image_grads[None], text_grads[None], loss)


def solution(mesh):
    in_specs = (P("group", "blk", None), P("group", "blk", None), P("group", "blk"), P(), P(), P())
    out_specs = (P("group", "blk", None), P("group", "blk", None), P())
    return jax.shard_map(shards, mesh=mesh, in_specs=in_specs, out_specs=out_specs, check_vma=False)
```

```python
import functools

import jax
import jax.numpy as jnp
from jax import lax
from jax.experimental import pallas as pl
from jax.experimental.pallas import tpu as pltpu
from jax.sharding import PartitionSpec as P

TAIL = 8
DIGIT = 128
LANES = 128


def pair_slopes(rows, others, hits, temper, offset):
    logits = temper * jnp.dot(rows, others.T, preferred_element_type=jnp.float32) + offset
    hit_values = hits.astype(jnp.float32)
    slopes = (jax.nn.sigmoid(logits) - hit_values).astype(jnp.bfloat16)
    return logits, hit_values, slopes


def exchange(array, axis, size, mate):
    return lax.ppermute(array, axis, [(place, mate(place)) for place in range(size)])


def swap(array, axis, size, bit):
    return exchange(array, axis, size, lambda place: place ^ bit)


def after(array, *earlier):
    return lax.optimization_barrier((array, *earlier))[0]


def entry(partner, group):
    lane = lax.broadcasted_iota(jnp.int32, partner.shape, 1)
    return jnp.sum(jnp.where(lane == group, partner[...], 0), axis=1, keepdims=True)


def position(partner, group):
    lane = lax.broadcasted_iota(jnp.int32, partner.shape, 1)
    return jnp.sum(jnp.where(partner[...] == group, lane, 0), axis=1, keepdims=True)


def same_chip(group, other):
    return (group ^ other) >> 1 == 0


def offer_kernel(partner, own, across, out):
    here = lax.axis_index("group")
    out[...] = jnp.where(same_chip(entry(partner, here ^ 1), here), own[...], across[...])


def choose_kernel(partner, own, across, offered, out):
    here = lax.axis_index("group")
    wanted = entry(partner, here)
    held = jnp.where(same_chip(wanted, here), own[...], across[...])
    out[...] = jnp.where((wanted ^ here) & 1 == 0, held, offered[...])


def scorer_kernel(partner, every, out):
    wanted = position(partner, lax.axis_index("group"))
    found = every[0]
    for group in range(1, every.shape[0]):
        found = jnp.where(wanted == group, every[group], found)
    out[...] = found


LINE = (0, 4, 2, 6)


def with_labels(images, labels):
    digits = jnp.stack([labels // DIGIT, labels % DIGIT]).astype(images.dtype)
    return jnp.concatenate([images, jnp.pad(digits, ((0, TAIL - 2), (0, images.shape[1] - labels.shape[0])))])


def labels_of(block, rows, width):
    digits = block[rows : rows + TAIL, :width].astype(jnp.int32)
    return digits[:1] * DIGIT + digits[1:2]


def rows_by_rows(left, right):
    return lax.dot_general(left, right, (((1,), (1,)), ((), ())), preferred_element_type=jnp.float32)


def stack(blocks, rows, into):
    for place, block in enumerate(blocks):
        into[place * rows : (place + 1) * rows, :] = block[:rows, :]


def image_kernel(settings, images, mate, *refs):
    texts, (own_part, mate_part, loss, all_images, all_texts) = refs[:-5], refs[-5:]
    rows = texts[0].shape[0]
    temper = jnp.exp(settings[:, :1])
    stack((images, mate), rows, all_images)
    stack(texts, rows, all_texts)
    labels = jnp.concatenate([jnp.broadcast_to(labels_of(block, rows, LANES), (LANES, LANES)).T[:rows] for block in (images, mate)])
    labels = jnp.concatenate([labels] * (all_texts.shape[0] // LANES), axis=1)
    column = lax.broadcasted_iota(jnp.int32, labels.shape, 1)
    index = column
    for place, flip in enumerate(LINE):
        start = place * rows
        index = jnp.where(column >= start, column - start + (lax.axis_index("blk") ^ flip) * rows, index)

    logits = temper * rows_by_rows(all_images[...], all_texts[...]) + settings[:, 1:2]
    hit_values = (index == labels).astype(jnp.float32)
    small = jnp.exp(-jnp.abs(logits))
    losses = jnp.maximum(logits, 0.0) + jnp.log1p(small) - hit_values * logits
    slopes = jnp.where(logits >= 0.0, 1.0, small) / (1.0 + small) - hit_values
    total = losses.reshape(-1, 8, losses.shape[1]).sum(axis=0)
    loss[...] = sum(total[:, lane : lane + LANES] for lane in range(0, total.shape[1], LANES))
    grads = temper * jnp.dot(slopes.astype(jnp.bfloat16), all_texts[...], preferred_element_type=jnp.float32)
    own_part[...] = grads[:rows]
    mate_part[...] = grads[rows:]


def text_kernel(flip, count, settings, texts, *refs):
    images, earlier, part = refs[:count], refs[count:-1], refs[-1]
    rows = texts.shape[0]
    temper = jnp.exp(settings[:, :1])
    index = (lax.axis_index("blk") ^ flip) * rows + lax.broadcasted_iota(jnp.int32, (rows, rows), 0)
    total = jnp.zeros(part.shape, jnp.float32)
    for block in images:
        products = rows_by_rows(texts[...], block[:rows, :])
        hits = index == labels_of(block, rows, rows)
        slopes = (jax.nn.sigmoid(temper * products + settings[:, 1:2]) - hits.astype(jnp.float32)).astype(jnp.bfloat16)
        total += jnp.dot(slopes, block[:rows, :], preferred_element_type=jnp.float32)
    part[...] = temper * total + earlier[0][...] if earlier else temper * total


def finish_kernel(own_text, arrived, first, rest, text_grads, image_grads):
    rows, cut = own_text.shape[0], first.shape[0]
    text_grads[...] = own_text[...] + arrived[:rows]
    image_grads[:cut] = first[...]
    image_grads[cut:] = rest[...] + arrived[rows:]


def call(kernel, arrays, shapes, name, dtype=jnp.float32, scratch=()):
    return pl.pallas_call(
        kernel,
        out_shape=[jax.ShapeDtypeStruct(shape, dtype) for shape in shapes],
        in_specs=[pl.BlockSpec(memory_space=pltpu.VMEM)] * len(arrays),
        out_specs=[pl.BlockSpec(memory_space=pltpu.VMEM)] * len(shapes),
        scratch_shapes=[pltpu.VMEM(shape, jnp.bfloat16) for shape in scratch],
        compiler_params=pltpu.CompilerParams(vmem_limit_bytes=16 * 2**20),
        name=name,
    )(*arrays)


def hop_sum(total, hops):
    for axis, size, bit in hops:
        total = total + swap(total, axis, size, bit)
    return total


def shards(image_embeds, text_embeds, positives, partner, log_temp, bias):
    texts = text_embeds[0]
    labels = positives[0]
    rows = texts.shape[0]
    blocks = lax.axis_size("blk")
    groups = lax.axis_size("group")
    blk_place = lax.axis_index("blk")
    images = with_labels(image_embeds[0], labels)

    def index_of(places):
        return (jnp.stack(places)[:, None] * rows + jnp.arange(rows)[None, :]).reshape(-1)

    def matches(some_labels, index):
        return some_labels[:, None] == index[None, :]

    def grads(slopes, others):
        return temper * jnp.dot(slopes, others, preferred_element_type=jnp.float32)

    settings = jnp.concatenate([log_temp, bias]).reshape(1, 2)
    packed = after(jnp.concatenate([images, texts]), settings)
    tailed = images.shape[0]
    own_images, own_texts = packed[:rows], packed[tailed:]
    hops = [("group", groups, 1 << step) for step in range(groups.bit_length() - 1)]
    hops += [("blk", blocks, 1 << step) for step in range(blocks.bit_length() - 1)]
    choice = partner.reshape(1, groups)
    texts_across = swap(texts, "group", groups, 2)
    offer = call(offer_kernel, [choice, own_texts, texts_across], [texts.shape], "offer", texts.dtype)[0]
    offered = swap(offer, "group", groups, 1)
    partner_text = call(choose_kernel, [choice, own_texts, texts_across, offered], [texts.shape], "choose", texts.dtype)[0]
    group_images = lax.all_gather(after(packed[:tailed], partner_text), "group")
    scorer_image = call(scorer_kernel, [choice, group_images], [images.shape], "scorer", images.dtype)[0]

    if blocks == 8:

        def along(array, flip):
            return swap(array, "blk", blocks, flip)

        mate = along(packed, 1)
        text_two_off = along(partner_text, 4)
        text_one_off = along(partner_text, 2)
        text_three_off = along(after(text_two_off, text_one_off, mate, scorer_image), 2)
        image_one_off = along(after(scorer_image, text_three_off), 2)
        image_two_off = along(scorer_image, 4)
        column_texts = [partner_text, text_two_off, text_one_off, after(text_three_off, image_two_off)]
        grad_shape = texts.shape
        own_part, mate_part, total = call(
            image_kernel,
            [settings, packed[:tailed], mate[:tailed], *column_texts],
            [grad_shape, grad_shape, (8, LANES)],
            "image_side",
            scratch=[(2 * rows, texts.shape[1]), (len(LINE) * rows, texts.shape[1])],
        )
        image_three_off = along(image_two_off, 2)
        cut = rows * 5 // 6
        first_grads = own_part[:cut] + along(mate_part[:cut], 1)
        rest_own, rest = own_part[cut:], mate_part[cut:]
        total = hop_sum(total, hops[:2])
        total = hop_sum(after(total, image_one_off), hops[2:3])
        early_images = [scorer_image, image_two_off, image_one_off]
        early_part = call(functools.partial(text_kernel, 1, 3), [settings, mate[tailed:], *early_images], [grad_shape], "text_side_early")[0]
        last_image = after(image_three_off, total, early_part)
        mate_part = call(functools.partial(text_kernel, 1, 1), [settings, mate[tailed:], last_image, early_part], [grad_shape], "text_side_mate")[0]
        column_images = early_images + [last_image]
        arrived = along(jnp.concatenate([mate_part, rest]), 1)
        own_part = call(functools.partial(text_kernel, 0, 4), [settings, own_texts, *column_images], [grad_shape], "text_side_own")[0]
        text_grads, image_grads = call(
            finish_kernel, [own_part, arrived, first_grads, rest_own], [grad_shape, grad_shape], "finish"
        )
        total = after(hop_sum(after(total, first_grads), hops[3:4]), own_part)
        hops = hops[4:]
    else:
        temper = jnp.exp(log_temp[0])
        offset = bias[0]
        all_texts = lax.all_gather(partner_text, "blk", axis=0, tiled=True)
        every_image = lax.all_gather(scorer_image, "blk", axis=0)
        hits = matches(labels, jnp.arange(blocks * rows))
        logits, hit_values, slopes = pair_slopes(own_images, all_texts, hits, temper, offset)
        total = jnp.sum(jax.nn.softplus(logits) - hit_values * logits)
        total = jnp.zeros((8, 128)).at[0, 0].set(total)
        image_grads = grads(slopes, all_texts)
        all_images = every_image[:, :rows].reshape(blocks * rows, -1)
        back_labels = jax.vmap(lambda block: labels_of(block, rows, rows)[0])(every_image).reshape(-1)
        back_hits = matches(index_of([blk_place]), back_labels)
        back_slopes = pair_slopes(own_texts, all_images, back_hits, temper, offset)[2]
        text_grads = grads(back_slopes, all_images)

    total = hop_sum(total, hops)
    loss = jnp.sum(total * (1.0 / (groups * rows * blocks * blocks))).reshape(1)
    return (image_grads[None], text_grads[None], loss)


def solution(mesh):
    in_specs = (P("group", "blk", None), P("group", "blk", None), P("group", "blk"), P(), P(), P())
    out_specs = (P("group", "blk", None), P("group", "blk", None), P())
    return jax.shard_map(shards, mesh=mesh, in_specs=in_specs, out_specs=out_specs, check_vma=False)
```

```python
import functools

import jax
import jax.numpy as jnp
from jax import lax
from jax.experimental import pallas as pl
from jax.experimental.pallas import tpu as pltpu
from jax.sharding import PartitionSpec as P

TAIL = 8
DIGIT = 128
LANES = 128


def pair_slopes(rows, others, hits, temper, offset):
    logits = temper * jnp.dot(rows, others.T, preferred_element_type=jnp.float32) + offset
    hit_values = hits.astype(jnp.float32)
    slopes = (jax.nn.sigmoid(logits) - hit_values).astype(jnp.bfloat16)
    return logits, hit_values, slopes


def exchange(array, axis, size, mate):
    return lax.ppermute(array, axis, [(place, mate(place)) for place in range(size)])


def swap(array, axis, size, bit):
    return exchange(array, axis, size, lambda place: place ^ bit)


def after(array, *earlier):
    return lax.optimization_barrier((array, *earlier))[0]


def entry(partner, group):
    lane = lax.broadcasted_iota(jnp.int32, partner.shape, 1)
    return jnp.sum(jnp.where(lane == group, partner[...], 0), axis=1, keepdims=True)


def position(partner, group):
    lane = lax.broadcasted_iota(jnp.int32, partner.shape, 1)
    return jnp.sum(jnp.where(partner[...] == group, lane, 0), axis=1, keepdims=True)


def same_chip(group, other):
    return (group ^ other) >> 1 == 0


def offer_kernel(partner, own, across, out):
    here = lax.axis_index("group")
    out[...] = jnp.where(same_chip(entry(partner, here ^ 1), here), own[...], across[...])


def choose_kernel(partner, own, across, offered, out):
    here = lax.axis_index("group")
    wanted = entry(partner, here)
    held = jnp.where(same_chip(wanted, here), own[...], across[...])
    out[...] = jnp.where((wanted ^ here) & 1 == 0, held, offered[...])


def scorer_kernel(partner, every, out):
    wanted = position(partner, lax.axis_index("group"))
    found = every[0]
    for group in range(1, every.shape[0]):
        found = jnp.where(wanted == group, every[group], found)
    out[...] = found


LINE = (0, 4, 2, 6)


def with_labels(images, labels):
    digits = jnp.stack([labels // DIGIT, labels % DIGIT]).astype(images.dtype)
    return jnp.concatenate([images, jnp.pad(digits, ((0, TAIL - 2), (0, images.shape[1] - labels.shape[0])))])


def labels_of(block, rows, width):
    digits = block[rows : rows + TAIL, :width].astype(jnp.int32)
    return digits[:1] * DIGIT + digits[1:2]


def rows_by_rows(left, right):
    return lax.dot_general(left, right, (((1,), (1,)), ((), ())), preferred_element_type=jnp.float32)


def stack(blocks, rows, into):
    for place, block in enumerate(blocks):
        into[place * rows : (place + 1) * rows, :] = block[:rows, :]


def image_kernel(settings, images, mate, *refs):
    texts, (own_part, mate_part, loss, all_images, all_texts) = refs[:-5], refs[-5:]
    rows = texts[0].shape[0]
    temper = jnp.exp(settings[:, :1])
    stack((images, mate), rows, all_images)
    stack(texts, rows, all_texts)
    labels = jnp.concatenate([jnp.broadcast_to(labels_of(block, rows, LANES), (LANES, LANES)).T[:rows] for block in (images, mate)])
    labels = jnp.concatenate([labels] * (all_texts.shape[0] // LANES), axis=1)
    column = lax.broadcasted_iota(jnp.int32, labels.shape, 1)
    index = column
    for place, flip in enumerate(LINE):
        start = place * rows
        index = jnp.where(column >= start, column - start + (lax.axis_index("blk") ^ flip) * rows, index)

    logits = temper * rows_by_rows(all_images[...], all_texts[...]) + settings[:, 1:2]
    hit_values = (index == labels).astype(jnp.float32)
    small = jnp.exp(-jnp.abs(logits))
    losses = jnp.maximum(logits, 0.0) + jnp.log1p(small) - hit_values * logits
    slopes = jnp.where(logits >= 0.0, 1.0, small) / (1.0 + small) - hit_values
    total = losses.reshape(-1, 8, losses.shape[1]).sum(axis=0)
    loss[...] = sum(total[:, lane : lane + LANES] for lane in range(0, total.shape[1], LANES))
    grads = temper * jnp.dot(slopes.astype(jnp.bfloat16), all_texts[...], preferred_element_type=jnp.float32)
    own_part[...] = grads[:rows]
    mate_part[...] = grads[rows:]


def text_kernel(flip, count, settings, texts, *refs):
    images, earlier, part = refs[:count], refs[count:-1], refs[-1]
    rows = texts.shape[0]
    temper = jnp.exp(settings[:, :1])
    index = (lax.axis_index("blk") ^ flip) * rows + lax.broadcasted_iota(jnp.int32, (rows, rows), 0)
    total = jnp.zeros(part.shape, jnp.float32)
    for block in images:
        products = rows_by_rows(texts[...], block[:rows, :])
        hits = index == labels_of(block, rows, rows)
        slopes = (jax.nn.sigmoid(temper * products + settings[:, 1:2]) - hits.astype(jnp.float32)).astype(jnp.bfloat16)
        total += jnp.dot(slopes, block[:rows, :], preferred_element_type=jnp.float32)
    part[...] = temper * total + earlier[0][...] if earlier else temper * total


def finish_kernel(own_text, arrived, first, rest, text_grads, image_grads):
    rows, cut = own_text.shape[0], first.shape[0]
    text_grads[...] = own_text[...] + arrived[:rows]
    image_grads[:cut] = first[...]
    image_grads[cut:] = rest[...] + arrived[rows:]


def call(kernel, arrays, shapes, name, dtype=jnp.float32, scratch=()):
    return pl.pallas_call(
        kernel,
        out_shape=[jax.ShapeDtypeStruct(shape, dtype) for shape in shapes],
        in_specs=[pl.BlockSpec(memory_space=pltpu.VMEM)] * len(arrays),
        out_specs=[pl.BlockSpec(memory_space=pltpu.VMEM)] * len(shapes),
        scratch_shapes=[pltpu.VMEM(shape, jnp.bfloat16) for shape in scratch],
        compiler_params=pltpu.CompilerParams(vmem_limit_bytes=16 * 2**20),
        name=name,
    )(*arrays)


def hop_sum(total, hops):
    for axis, size, bit in hops:
        total = total + swap(total, axis, size, bit)
    return total


def shards(image_embeds, text_embeds, positives, partner, log_temp, bias):
    texts = text_embeds[0]
    labels = positives[0]
    rows = texts.shape[0]
    blocks = lax.axis_size("blk")
    groups = lax.axis_size("group")
    blk_place = lax.axis_index("blk")
    images = with_labels(image_embeds[0], labels)

    def index_of(places):
        return (jnp.stack(places)[:, None] * rows + jnp.arange(rows)[None, :]).reshape(-1)

    def matches(some_labels, index):
        return some_labels[:, None] == index[None, :]

    def grads(slopes, others):
        return temper * jnp.dot(slopes, others, preferred_element_type=jnp.float32)

    settings = jnp.concatenate([log_temp, bias]).reshape(1, 2)
    packed = after(jnp.concatenate([images, texts]), settings)
    tailed = images.shape[0]
    own_images, own_texts = packed[:rows], packed[tailed:]
    hops = [("group", groups, 1 << step) for step in range(groups.bit_length() - 1)]
    hops += [("blk", blocks, 1 << step) for step in range(blocks.bit_length() - 1)]
    choice = partner.reshape(1, groups)
    texts_across = swap(texts, "group", groups, 2)
    offer = call(offer_kernel, [choice, own_texts, texts_across], [texts.shape], "offer", texts.dtype)[0]
    offered = swap(offer, "group", groups, 1)
    partner_text = call(choose_kernel, [choice, own_texts, texts_across, offered], [texts.shape], "choose", texts.dtype)[0]
    group_images = lax.all_gather(after(packed[:tailed], partner_text), "group")
    scorer_image = call(scorer_kernel, [choice, group_images], [images.shape], "scorer", images.dtype)[0]

    if blocks == 8:

        def along(array, flip):
            return swap(array, "blk", blocks, flip)

        mate = along(packed, 1)
        text_two_off = along(partner_text, 4)
        text_one_off = along(partner_text, 2)
        text_three_off = along(after(text_two_off, text_one_off, mate, scorer_image), 2)
        image_one_off = along(after(scorer_image, text_three_off), 2)
        image_two_off = along(scorer_image, 4)
        column_texts = [partner_text, text_two_off, text_one_off, text_three_off]
        grad_shape = texts.shape
        own_part, mate_part, total = call(
            image_kernel,
            [settings, packed[:tailed], mate[:tailed], *column_texts],
            [grad_shape, grad_shape, (8, LANES)],
            "image_side",
            scratch=[(2 * rows, texts.shape[1]), (len(LINE) * rows, texts.shape[1])],
        )
        image_three_off = along(after(image_two_off, own_part), 2)
        cut = rows * 5 // 6
        first_grads = own_part[:cut] + along(mate_part[:cut], 1)
        rest_own, rest = own_part[cut:], mate_part[cut:]
        total = hop_sum(total, hops[:2])
        total = hop_sum(after(total, image_one_off), hops[2:3])
        early_images = [scorer_image, image_two_off, image_one_off]
        early_part = call(functools.partial(text_kernel, 1, 3), [settings, mate[tailed:], *early_images], [grad_shape], "text_side_early")[0]
        last_image = after(image_three_off, total, early_part)
        mate_part = call(functools.partial(text_kernel, 1, 1), [settings, mate[tailed:], last_image, early_part], [grad_shape], "text_side_mate")[0]
        column_images = early_images + [last_image]
        arrived = along(jnp.concatenate([mate_part, rest]), 1)
        own_part = call(functools.partial(text_kernel, 0, 4), [settings, own_texts, *column_images], [grad_shape], "text_side_own")[0]
        text_grads, image_grads = call(
            finish_kernel, [own_part, arrived, first_grads, rest_own], [grad_shape, grad_shape], "finish"
        )
        total = after(hop_sum(after(total, first_grads), hops[3:4]), own_part)
        hops = hops[4:]
    else:
        temper = jnp.exp(log_temp[0])
        offset = bias[0]
        all_texts = lax.all_gather(partner_text, "blk", axis=0, tiled=True)
        every_image = lax.all_gather(scorer_image, "blk", axis=0)
        hits = matches(labels, jnp.arange(blocks * rows))
        logits, hit_values, slopes = pair_slopes(own_images, all_texts, hits, temper, offset)
        total = jnp.sum(jax.nn.softplus(logits) - hit_values * logits)
        total = jnp.zeros((8, 128)).at[0, 0].set(total)
        image_grads = grads(slopes, all_texts)
        all_images = every_image[:, :rows].reshape(blocks * rows, -1)
        back_labels = jax.vmap(lambda block: labels_of(block, rows, rows)[0])(every_image).reshape(-1)
        back_hits = matches(index_of([blk_place]), back_labels)
        back_slopes = pair_slopes(own_texts, all_images, back_hits, temper, offset)[2]
        text_grads = grads(back_slopes, all_images)

    total = hop_sum(total, hops)
    loss = jnp.sum(total * (1.0 / (groups * rows * blocks * blocks))).reshape(1)
    return (image_grads[None], text_grads[None], loss)


def solution(mesh):
    in_specs = (P("group", "blk", None), P("group", "blk", None), P("group", "blk"), P(), P(), P())
    out_specs = (P("group", "blk", None), P("group", "blk", None), P())
    return jax.shard_map(shards, mesh=mesh, in_specs=in_specs, out_specs=out_specs, check_vma=False)
```

```python
import functools

import jax
import jax.numpy as jnp
from jax import lax
from jax.experimental import pallas as pl
from jax.experimental.pallas import tpu as pltpu
from jax.sharding import PartitionSpec as P

TAIL = 8
DIGIT = 128
LANES = 128


def pair_slopes(rows, others, hits, temper, offset):
    logits = temper * jnp.dot(rows, others.T, preferred_element_type=jnp.float32) + offset
    hit_values = hits.astype(jnp.float32)
    slopes = (jax.nn.sigmoid(logits) - hit_values).astype(jnp.bfloat16)
    return logits, hit_values, slopes


def exchange(array, axis, size, mate):
    return lax.ppermute(array, axis, [(place, mate(place)) for place in range(size)])


def swap(array, axis, size, bit):
    return exchange(array, axis, size, lambda place: place ^ bit)


def after(array, *earlier):
    return lax.optimization_barrier((array, *earlier))[0]


def entry(partner, group):
    lane = lax.broadcasted_iota(jnp.int32, partner.shape, 1)
    return jnp.sum(jnp.where(lane == group, partner[...], 0), axis=1, keepdims=True)


def position(partner, group):
    lane = lax.broadcasted_iota(jnp.int32, partner.shape, 1)
    return jnp.sum(jnp.where(partner[...] == group, lane, 0), axis=1, keepdims=True)


def same_chip(group, other):
    return (group ^ other) >> 1 == 0


def offer_kernel(partner, own, across, out):
    here = lax.axis_index("group")
    out[...] = jnp.where(same_chip(entry(partner, here ^ 1), here), own[...], across[...])


def choose_kernel(partner, own, across, offered, out):
    here = lax.axis_index("group")
    wanted = entry(partner, here)
    held = jnp.where(same_chip(wanted, here), own[...], across[...])
    out[...] = jnp.where((wanted ^ here) & 1 == 0, held, offered[...])


def scorer_kernel(partner, every, out):
    wanted = position(partner, lax.axis_index("group"))
    found = every[0]
    for group in range(1, every.shape[0]):
        found = jnp.where(wanted == group, every[group], found)
    out[...] = found


LINE = (0, 4, 2, 6)


def with_labels(images, labels):
    digits = jnp.stack([labels // DIGIT, labels % DIGIT]).astype(images.dtype)
    return jnp.concatenate([images, jnp.pad(digits, ((0, TAIL - 2), (0, images.shape[1] - labels.shape[0])))])


def labels_of(block, rows, width):
    digits = block[rows : rows + TAIL, :width].astype(jnp.int32)
    return digits[:1] * DIGIT + digits[1:2]


def rows_by_rows(left, right):
    return lax.dot_general(left, right, (((1,), (1,)), ((), ())), preferred_element_type=jnp.float32)


def stack(blocks, rows, into):
    for place, block in enumerate(blocks):
        into[place * rows : (place + 1) * rows, :] = block[:rows, :]


def image_kernel(settings, images, mate, *refs):
    texts, (own_part, mate_part, loss, all_images, all_texts) = refs[:-5], refs[-5:]
    rows = texts[0].shape[0]
    temper = jnp.exp(settings[:, :1])
    stack((images, mate), rows, all_images)
    stack(texts, rows, all_texts)
    labels = jnp.concatenate([jnp.broadcast_to(labels_of(block, rows, LANES), (LANES, LANES)).T[:rows] for block in (images, mate)])
    labels = jnp.concatenate([labels] * (all_texts.shape[0] // LANES), axis=1)
    column = lax.broadcasted_iota(jnp.int32, labels.shape, 1)
    index = column
    for place, flip in enumerate(LINE):
        start = place * rows
        index = jnp.where(column >= start, column - start + (lax.axis_index("blk") ^ flip) * rows, index)

    logits = temper * rows_by_rows(all_images[...], all_texts[...]) + settings[:, 1:2]
    hit_values = (index == labels).astype(jnp.float32)
    small = jnp.exp(-jnp.abs(logits))
    losses = jnp.maximum(logits, 0.0) + jnp.log1p(small) - hit_values * logits
    slopes = jnp.where(logits >= 0.0, 1.0, small) / (1.0 + small) - hit_values
    total = losses.reshape(-1, 8, losses.shape[1]).sum(axis=0)
    loss[...] = sum(total[:, lane : lane + LANES] for lane in range(0, total.shape[1], LANES))
    grads = temper * jnp.dot(slopes.astype(jnp.bfloat16), all_texts[...], preferred_element_type=jnp.float32)
    own_part[...] = grads[:rows]
    mate_part[...] = grads[rows:]


def text_kernel(flip, count, settings, texts, *refs):
    images, earlier, part = refs[:count], refs[count:-1], refs[-1]
    rows = texts.shape[0]
    temper = jnp.exp(settings[:, :1])
    index = (lax.axis_index("blk") ^ flip) * rows + lax.broadcasted_iota(jnp.int32, (rows, rows), 0)
    total = jnp.zeros(part.shape, jnp.float32)
    for block in images:
        products = rows_by_rows(texts[...], block[:rows, :])
        hits = index == labels_of(block, rows, rows)
        slopes = (jax.nn.sigmoid(temper * products + settings[:, 1:2]) - hits.astype(jnp.float32)).astype(jnp.bfloat16)
        total += jnp.dot(slopes, block[:rows, :], preferred_element_type=jnp.float32)
    part[...] = temper * total + earlier[0][...] if earlier else temper * total


def finish_kernel(own_text, text_part, first, rest_own, rest, text_grads, image_grads):
    cut = first.shape[0]
    text_grads[...] = own_text[...] + text_part[...]
    image_grads[:cut] = first[...]
    image_grads[cut:] = rest_own[...] + rest[...]


def call(kernel, arrays, shapes, name, dtype=jnp.float32, scratch=()):
    return pl.pallas_call(
        kernel,
        out_shape=[jax.ShapeDtypeStruct(shape, dtype) for shape in shapes],
        in_specs=[pl.BlockSpec(memory_space=pltpu.VMEM)] * len(arrays),
        out_specs=[pl.BlockSpec(memory_space=pltpu.VMEM)] * len(shapes),
        scratch_shapes=[pltpu.VMEM(shape, jnp.bfloat16) for shape in scratch],
        compiler_params=pltpu.CompilerParams(vmem_limit_bytes=16 * 2**20),
        name=name,
    )(*arrays)


def hop_sum(total, hops):
    for axis, size, bit in hops:
        total = total + swap(total, axis, size, bit)
    return total


def shards(image_embeds, text_embeds, positives, partner, log_temp, bias):
    texts = text_embeds[0]
    labels = positives[0]
    rows = texts.shape[0]
    blocks = lax.axis_size("blk")
    groups = lax.axis_size("group")
    blk_place = lax.axis_index("blk")
    images = with_labels(image_embeds[0], labels)

    def index_of(places):
        return (jnp.stack(places)[:, None] * rows + jnp.arange(rows)[None, :]).reshape(-1)

    def matches(some_labels, index):
        return some_labels[:, None] == index[None, :]

    def grads(slopes, others):
        return temper * jnp.dot(slopes, others, preferred_element_type=jnp.float32)

    settings = jnp.concatenate([log_temp, bias]).reshape(1, 2)
    packed = after(jnp.concatenate([images, texts]), settings)
    tailed = images.shape[0]
    own_images, own_texts = packed[:rows], packed[tailed:]
    hops = [("group", groups, 1 << step) for step in range(groups.bit_length() - 1)]
    hops += [("blk", blocks, 1 << step) for step in range(blocks.bit_length() - 1)]
    choice = partner.reshape(1, groups)
    texts_across = swap(texts, "group", groups, 2)
    offer = call(offer_kernel, [choice, own_texts, texts_across], [texts.shape], "offer", texts.dtype)[0]
    offered = swap(offer, "group", groups, 1)
    partner_text = call(choose_kernel, [choice, own_texts, texts_across, offered], [texts.shape], "choose", texts.dtype)[0]
    group_images = lax.all_gather(after(packed[:tailed], partner_text), "group")
    scorer_image = call(scorer_kernel, [choice, group_images], [images.shape], "scorer", images.dtype)[0]

    if blocks == 8:

        def along(array, flip):
            return swap(array, "blk", blocks, flip)

        mate = along(packed, 1)
        text_two_off = along(partner_text, 4)
        text_one_off = along(partner_text, 2)
        text_three_off = along(after(text_two_off, text_one_off, mate, scorer_image), 2)
        image_one_off = along(after(scorer_image, text_three_off), 2)
        image_two_off = along(scorer_image, 4)
        column_texts = [partner_text, text_two_off, text_one_off, text_three_off]
        grad_shape = texts.shape
        own_part, mate_part, total = call(
            image_kernel,
            [settings, packed[:tailed], mate[:tailed], *column_texts],
            [grad_shape, grad_shape, (8, LANES)],
            "image_side",
            scratch=[(2 * rows, texts.shape[1]), (len(LINE) * rows, texts.shape[1])],
        )
        image_three_off = along(after(image_two_off, own_part), 2)
        cut = rows * 5 // 6
        first_grads = own_part[:cut] + along(mate_part[:cut], 1)
        rest_own, rest = own_part[cut:], mate_part[cut:]
        total = hop_sum(total, hops[:2])
        total = hop_sum(after(total, image_one_off), hops[2:3])
        early_images = [scorer_image, image_two_off, image_one_off]
        early_part = call(functools.partial(text_kernel, 1, 3), [settings, mate[tailed:], *early_images], [grad_shape], "text_side_early")[0]
        rest = along(after(rest, early_part), 1)
        last_image = after(image_three_off, total)
        mate_part = call(functools.partial(text_kernel, 1, 1), [settings, mate[tailed:], last_image, early_part], [grad_shape], "text_side_mate")[0]
        column_images = early_images + [last_image]
        text_part = along(mate_part, 1)
        own_part = call(functools.partial(text_kernel, 0, 4), [settings, own_texts, *column_images], [grad_shape], "text_side_own")[0]
        text_grads, image_grads = call(
            finish_kernel, [own_part, text_part, first_grads, rest_own, rest], [grad_shape, grad_shape], "finish"
        )
        total = after(hop_sum(after(total, first_grads, rest), hops[3:4]), own_part)
        hops = hops[4:]
    else:
        temper = jnp.exp(log_temp[0])
        offset = bias[0]
        all_texts = lax.all_gather(partner_text, "blk", axis=0, tiled=True)
        every_image = lax.all_gather(scorer_image, "blk", axis=0)
        hits = matches(labels, jnp.arange(blocks * rows))
        logits, hit_values, slopes = pair_slopes(own_images, all_texts, hits, temper, offset)
        total = jnp.sum(jax.nn.softplus(logits) - hit_values * logits)
        total = jnp.zeros((8, 128)).at[0, 0].set(total)
        image_grads = grads(slopes, all_texts)
        all_images = every_image[:, :rows].reshape(blocks * rows, -1)
        back_labels = jax.vmap(lambda block: labels_of(block, rows, rows)[0])(every_image).reshape(-1)
        back_hits = matches(index_of([blk_place]), back_labels)
        back_slopes = pair_slopes(own_texts, all_images, back_hits, temper, offset)[2]
        text_grads = grads(back_slopes, all_images)

    total = hop_sum(total, hops)
    loss = jnp.sum(total * (1.0 / (groups * rows * blocks * blocks))).reshape(1)
    return (image_grads[None], text_grads[None], loss)


def solution(mesh):
    in_specs = (P("group", "blk", None), P("group", "blk", None), P("group", "blk"), P(), P(), P())
    out_specs = (P("group", "blk", None), P("group", "blk", None), P())
    return jax.shard_map(shards, mesh=mesh, in_specs=in_specs, out_specs=out_specs, check_vma=False)
```

```python
import functools

import jax
import jax.numpy as jnp
from jax import lax
from jax.experimental import pallas as pl
from jax.experimental.pallas import tpu as pltpu
from jax.sharding import PartitionSpec as P

TAIL = 8
DIGIT = 128
LANES = 128


def pair_slopes(rows, others, hits, temper, offset):
    logits = temper * jnp.dot(rows, others.T, preferred_element_type=jnp.float32) + offset
    hit_values = hits.astype(jnp.float32)
    slopes = (jax.nn.sigmoid(logits) - hit_values).astype(jnp.bfloat16)
    return logits, hit_values, slopes


def exchange(array, axis, size, mate):
    return lax.ppermute(array, axis, [(place, mate(place)) for place in range(size)])


def swap(array, axis, size, bit):
    return exchange(array, axis, size, lambda place: place ^ bit)


def after(array, *earlier):
    return lax.optimization_barrier((array, *earlier))[0]


def entry(partner, group):
    lane = lax.broadcasted_iota(jnp.int32, partner.shape, 1)
    return jnp.sum(jnp.where(lane == group, partner[...], 0), axis=1, keepdims=True)


def position(partner, group):
    lane = lax.broadcasted_iota(jnp.int32, partner.shape, 1)
    return jnp.sum(jnp.where(partner[...] == group, lane, 0), axis=1, keepdims=True)


def same_chip(group, other):
    return (group ^ other) >> 1 == 0


def offer_kernel(partner, own, across, out):
    here = lax.axis_index("group")
    out[...] = jnp.where(same_chip(entry(partner, here ^ 1), here), own[...], across[...])


def choose_kernel(partner, own, across, offered, out):
    here = lax.axis_index("group")
    wanted = entry(partner, here)
    held = jnp.where(same_chip(wanted, here), own[...], across[...])
    out[...] = jnp.where((wanted ^ here) & 1 == 0, held, offered[...])


def scorer_kernel(partner, every, out):
    wanted = position(partner, lax.axis_index("group"))
    found = every[0]
    for group in range(1, every.shape[0]):
        found = jnp.where(wanted == group, every[group], found)
    out[...] = found


LINE = (0, 4, 2, 6)


def with_labels(images, labels):
    digits = jnp.stack([labels // DIGIT, labels % DIGIT]).astype(images.dtype)
    return jnp.concatenate([images, jnp.pad(digits, ((0, TAIL - 2), (0, images.shape[1] - labels.shape[0])))])


def labels_of(block, rows, width):
    digits = block[rows : rows + TAIL, :width].astype(jnp.int32)
    return digits[:1] * DIGIT + digits[1:2]


def rows_by_rows(left, right):
    return lax.dot_general(left, right, (((1,), (1,)), ((), ())), preferred_element_type=jnp.float32)


def stack(blocks, rows, into):
    for place, block in enumerate(blocks):
        into[place * rows : (place + 1) * rows, :] = block[:rows, :]


def image_kernel(settings, images, mate, *refs):
    texts, (own_part, mate_part, loss, all_images, all_texts) = refs[:-5], refs[-5:]
    rows = texts[0].shape[0]
    temper = jnp.exp(settings[:, :1])
    stack((images, mate), rows, all_images)
    stack(texts, rows, all_texts)
    labels = jnp.concatenate([jnp.broadcast_to(labels_of(block, rows, LANES), (LANES, LANES)).T[:rows] for block in (images, mate)])
    labels = jnp.concatenate([labels] * (all_texts.shape[0] // LANES), axis=1)
    column = lax.broadcasted_iota(jnp.int32, labels.shape, 1)
    index = column
    for place, flip in enumerate(LINE):
        start = place * rows
        index = jnp.where(column >= start, column - start + (lax.axis_index("blk") ^ flip) * rows, index)

    logits = temper * rows_by_rows(all_images[...], all_texts[...]) + settings[:, 1:2]
    hit_values = (index == labels).astype(jnp.float32)
    small = jnp.exp(-jnp.abs(logits))
    losses = jnp.maximum(logits, 0.0) + jnp.log1p(small) - hit_values * logits
    slopes = jnp.where(logits >= 0.0, 1.0, small) / (1.0 + small) - hit_values
    total = losses.reshape(-1, 8, losses.shape[1]).sum(axis=0)
    loss[...] = sum(total[:, lane : lane + LANES] for lane in range(0, total.shape[1], LANES))
    grads = temper * jnp.dot(slopes.astype(jnp.bfloat16), all_texts[...], preferred_element_type=jnp.float32)
    own_part[...] = grads[:rows]
    mate_part[...] = grads[rows:]


def text_kernel(flip, count, settings, texts, *refs):
    images, earlier, part = refs[:count], refs[count:-1], refs[-1]
    rows = texts.shape[0]
    temper = jnp.exp(settings[:, :1])
    index = (lax.axis_index("blk") ^ flip) * rows + lax.broadcasted_iota(jnp.int32, (rows, rows), 0)
    total = jnp.zeros(part.shape, jnp.float32)
    for block in images:
        products = rows_by_rows(texts[...], block[:rows, :])
        hits = index == labels_of(block, rows, rows)
        slopes = (jax.nn.sigmoid(temper * products + settings[:, 1:2]) - hits.astype(jnp.float32)).astype(jnp.bfloat16)
        total += jnp.dot(slopes, block[:rows, :], preferred_element_type=jnp.float32)
    part[...] = temper * total + earlier[0][...] if earlier else temper * total


def finish_kernel(own_text, text_part, first, rest_own, rest, text_grads, image_grads):
    cut = first.shape[0]
    text_grads[...] = own_text[...] + text_part[...]
    image_grads[:cut] = first[...]
    image_grads[cut:] = rest_own[...] + rest[...]


def call(kernel, arrays, shapes, name, dtype=jnp.float32, scratch=()):
    return pl.pallas_call(
        kernel,
        out_shape=[jax.ShapeDtypeStruct(shape, dtype) for shape in shapes],
        in_specs=[pl.BlockSpec(memory_space=pltpu.VMEM)] * len(arrays),
        out_specs=[pl.BlockSpec(memory_space=pltpu.VMEM)] * len(shapes),
        scratch_shapes=[pltpu.VMEM(shape, jnp.bfloat16) for shape in scratch],
        compiler_params=pltpu.CompilerParams(vmem_limit_bytes=16 * 2**20),
        name=name,
    )(*arrays)


def hop_sum(total, hops):
    for axis, size, bit in hops:
        total = total + swap(total, axis, size, bit)
    return total


def shards(image_embeds, text_embeds, positives, partner, log_temp, bias):
    texts = text_embeds[0]
    labels = positives[0]
    rows = texts.shape[0]
    blocks = lax.axis_size("blk")
    groups = lax.axis_size("group")
    blk_place = lax.axis_index("blk")
    images = with_labels(image_embeds[0], labels)

    def index_of(places):
        return (jnp.stack(places)[:, None] * rows + jnp.arange(rows)[None, :]).reshape(-1)

    def matches(some_labels, index):
        return some_labels[:, None] == index[None, :]

    def grads(slopes, others):
        return temper * jnp.dot(slopes, others, preferred_element_type=jnp.float32)

    settings = jnp.concatenate([log_temp, bias]).reshape(1, 2)
    packed = after(jnp.concatenate([images, texts]), settings)
    tailed = images.shape[0]
    own_images, own_texts = packed[:rows], packed[tailed:]
    hops = [("group", groups, 1 << step) for step in range(groups.bit_length() - 1)]
    hops += [("blk", blocks, 1 << step) for step in range(blocks.bit_length() - 1)]
    choice = partner.reshape(1, groups)
    texts_across = swap(texts, "group", groups, 2)
    offer = call(offer_kernel, [choice, own_texts, texts_across], [texts.shape], "offer", texts.dtype)[0]
    offered = swap(offer, "group", groups, 1)
    partner_text = call(choose_kernel, [choice, own_texts, texts_across, offered], [texts.shape], "choose", texts.dtype)[0]
    group_images = lax.all_gather(after(packed[:tailed], partner_text), "group")
    scorer_image = call(scorer_kernel, [choice, group_images], [images.shape], "scorer", images.dtype)[0]

    if blocks == 8:

        def along(array, flip):
            return swap(array, "blk", blocks, flip)

        mate = along(packed, 1)
        text_two_off = along(partner_text, 4)
        text_one_off = along(partner_text, 2)
        text_three_off = along(after(text_two_off, text_one_off, mate, scorer_image), 2)
        image_one_off = along(after(scorer_image, text_three_off), 2)
        image_two_off = along(scorer_image, 4)
        column_texts = [partner_text, text_two_off, text_one_off, text_three_off]
        grad_shape = texts.shape
        own_part, mate_part, total = call(
            image_kernel,
            [settings, packed[:tailed], mate[:tailed], *column_texts],
            [grad_shape, grad_shape, (8, LANES)],
            "image_side",
            scratch=[(2 * rows, texts.shape[1]), (len(LINE) * rows, texts.shape[1])],
        )
        image_three_off = along(after(image_two_off, own_part), 2)
        cut = rows * 5 // 6
        first_grads = own_part[:cut] + along(mate_part[:cut], 1)
        rest_own, rest = own_part[cut:], mate_part[cut:]
        total = hop_sum(total, hops[:3])
        early_images = [scorer_image, image_two_off, image_one_off]
        early_part = call(functools.partial(text_kernel, 1, 3), [settings, mate[tailed:], *early_images], [grad_shape], "text_side_early")[0]
        rest = along(after(rest, early_part), 1)
        last_image = after(image_three_off, total)
        mate_part = call(functools.partial(text_kernel, 1, 1), [settings, mate[tailed:], last_image, early_part], [grad_shape], "text_side_mate")[0]
        column_images = early_images + [last_image]
        text_part = along(mate_part, 1)
        own_part = call(functools.partial(text_kernel, 0, 4), [settings, own_texts, *column_images], [grad_shape], "text_side_own")[0]
        text_grads, image_grads = call(
            finish_kernel, [own_part, text_part, first_grads, rest_own, rest], [grad_shape, grad_shape], "finish"
        )
        total = after(hop_sum(after(total, first_grads, rest), hops[3:4]), own_part)
        hops = hops[4:]
    else:
        temper = jnp.exp(log_temp[0])
        offset = bias[0]
        all_texts = lax.all_gather(partner_text, "blk", axis=0, tiled=True)
        every_image = lax.all_gather(scorer_image, "blk", axis=0)
        hits = matches(labels, jnp.arange(blocks * rows))
        logits, hit_values, slopes = pair_slopes(own_images, all_texts, hits, temper, offset)
        total = jnp.sum(jax.nn.softplus(logits) - hit_values * logits)
        total = jnp.zeros((8, 128)).at[0, 0].set(total)
        image_grads = grads(slopes, all_texts)
        all_images = every_image[:, :rows].reshape(blocks * rows, -1)
        back_labels = jax.vmap(lambda block: labels_of(block, rows, rows)[0])(every_image).reshape(-1)
        back_hits = matches(index_of([blk_place]), back_labels)
        back_slopes = pair_slopes(own_texts, all_images, back_hits, temper, offset)[2]
        text_grads = grads(back_slopes, all_images)

    total = hop_sum(total, hops)
    loss = jnp.sum(total * (1.0 / (groups * rows * blocks * blocks))).reshape(1)
    return (image_grads[None], text_grads[None], loss)


def solution(mesh):
    in_specs = (P("group", "blk", None), P("group", "blk", None), P("group", "blk"), P(), P(), P())
    out_specs = (P("group", "blk", None), P("group", "blk", None), P())
    return jax.shard_map(shards, mesh=mesh, in_specs=in_specs, out_specs=out_specs, check_vma=False)
```

```python
import functools

import jax
import jax.numpy as jnp
from jax import lax
from jax.experimental import pallas as pl
from jax.experimental.pallas import tpu as pltpu
from jax.sharding import PartitionSpec as P

TAIL = 8
DIGIT = 128
LANES = 128


def pair_slopes(rows, others, hits, temper, offset):
    logits = temper * jnp.dot(rows, others.T, preferred_element_type=jnp.float32) + offset
    hit_values = hits.astype(jnp.float32)
    slopes = (jax.nn.sigmoid(logits) - hit_values).astype(jnp.bfloat16)
    return logits, hit_values, slopes


def exchange(array, axis, size, mate):
    return lax.ppermute(array, axis, [(place, mate(place)) for place in range(size)])


def swap(array, axis, size, bit):
    return exchange(array, axis, size, lambda place: place ^ bit)


def after(array, *earlier):
    return lax.optimization_barrier((array, *earlier))[0]


def entry(partner, group):
    lane = lax.broadcasted_iota(jnp.int32, partner.shape, 1)
    return jnp.sum(jnp.where(lane == group, partner[...], 0), axis=1, keepdims=True)


def position(partner, group):
    lane = lax.broadcasted_iota(jnp.int32, partner.shape, 1)
    return jnp.sum(jnp.where(partner[...] == group, lane, 0), axis=1, keepdims=True)


def same_chip(group, other):
    return (group ^ other) >> 1 == 0


def offer_kernel(partner, own, across, out):
    here = lax.axis_index("group")
    out[...] = jnp.where(same_chip(entry(partner, here ^ 1), here), own[...], across[...])


def choose_kernel(partner, own, across, offered, out):
    here = lax.axis_index("group")
    wanted = entry(partner, here)
    held = jnp.where(same_chip(wanted, here), own[...], across[...])
    out[...] = jnp.where((wanted ^ here) & 1 == 0, held, offered[...])


def scorer_kernel(partner, every, out):
    wanted = position(partner, lax.axis_index("group"))
    found = every[0]
    for group in range(1, every.shape[0]):
        found = jnp.where(wanted == group, every[group], found)
    out[...] = found


LINE = (0, 4, 2, 6)


def with_labels(images, labels):
    digits = jnp.stack([labels // DIGIT, labels % DIGIT]).astype(images.dtype)
    return jnp.concatenate([images, jnp.pad(digits, ((0, TAIL - 2), (0, images.shape[1] - labels.shape[0])))])


def labels_of(block, rows, width):
    digits = block[rows : rows + TAIL, :width].astype(jnp.int32)
    return digits[:1] * DIGIT + digits[1:2]


def rows_by_rows(left, right):
    return lax.dot_general(left, right, (((1,), (1,)), ((), ())), preferred_element_type=jnp.float32)


def stack(blocks, rows, into):
    for place, block in enumerate(blocks):
        into[place * rows : (place + 1) * rows, :] = block[:rows, :]


def image_kernel(settings, images, mate, *refs):
    texts, (own_part, mate_part, loss, all_images, all_texts) = refs[:-5], refs[-5:]
    rows = texts[0].shape[0]
    temper = jnp.exp(settings[:, :1])
    stack((images, mate), rows, all_images)
    stack(texts, rows, all_texts)
    labels = jnp.concatenate([jnp.broadcast_to(labels_of(block, rows, LANES), (LANES, LANES)).T[:rows] for block in (images, mate)])
    labels = jnp.concatenate([labels] * (all_texts.shape[0] // LANES), axis=1)
    column = lax.broadcasted_iota(jnp.int32, labels.shape, 1)
    index = column
    for place, flip in enumerate(LINE):
        start = place * rows
        index = jnp.where(column >= start, column - start + (lax.axis_index("blk") ^ flip) * rows, index)

    logits = temper * rows_by_rows(all_images[...], all_texts[...]) + settings[:, 1:2]
    hit_values = (index == labels).astype(jnp.float32)
    small = jnp.exp(-jnp.abs(logits))
    losses = jnp.maximum(logits, 0.0) + jnp.log1p(small) - hit_values * logits
    slopes = jnp.where(logits >= 0.0, 1.0, small) / (1.0 + small) - hit_values
    total = losses.reshape(-1, 8, losses.shape[1]).sum(axis=0)
    loss[...] = sum(total[:, lane : lane + LANES] for lane in range(0, total.shape[1], LANES))
    grads = temper * jnp.dot(slopes.astype(jnp.bfloat16), all_texts[...], preferred_element_type=jnp.float32)
    own_part[...] = grads[:rows]
    mate_part[...] = grads[rows:]


def text_kernel(flip, count, settings, texts, *refs):
    images, earlier, part = refs[:count], refs[count:-1], refs[-1]
    rows = texts.shape[0]
    temper = jnp.exp(settings[:, :1])
    index = (lax.axis_index("blk") ^ flip) * rows + lax.broadcasted_iota(jnp.int32, (rows, rows), 0)
    total = jnp.zeros(part.shape, jnp.float32)
    for block in images:
        products = rows_by_rows(texts[...], block[:rows, :])
        hits = index == labels_of(block, rows, rows)
        slopes = (jax.nn.sigmoid(temper * products + settings[:, 1:2]) - hits.astype(jnp.float32)).astype(jnp.bfloat16)
        total += jnp.dot(slopes, block[:rows, :], preferred_element_type=jnp.float32)
    part[...] = temper * total + earlier[0][...] if earlier else temper * total


def call(kernel, arrays, shapes, name, dtype=jnp.float32, scratch=()):
    return pl.pallas_call(
        kernel,
        out_shape=[jax.ShapeDtypeStruct(shape, dtype) for shape in shapes],
        in_specs=[pl.BlockSpec(memory_space=pltpu.VMEM)] * len(arrays),
        out_specs=[pl.BlockSpec(memory_space=pltpu.VMEM)] * len(shapes),
        scratch_shapes=[pltpu.VMEM(shape, jnp.bfloat16) for shape in scratch],
        compiler_params=pltpu.CompilerParams(vmem_limit_bytes=16 * 2**20),
        name=name,
    )(*arrays)


def hop_sum(total, hops):
    for axis, size, bit in hops:
        total = total + swap(total, axis, size, bit)
    return total


def shards(image_embeds, text_embeds, positives, partner, log_temp, bias):
    texts = text_embeds[0]
    labels = positives[0]
    rows = texts.shape[0]
    blocks = lax.axis_size("blk")
    groups = lax.axis_size("group")
    blk_place = lax.axis_index("blk")
    images = with_labels(image_embeds[0], labels)

    def index_of(places):
        return (jnp.stack(places)[:, None] * rows + jnp.arange(rows)[None, :]).reshape(-1)

    def matches(some_labels, index):
        return some_labels[:, None] == index[None, :]

    def grads(slopes, others):
        return temper * jnp.dot(slopes, others, preferred_element_type=jnp.float32)

    settings = jnp.concatenate([log_temp, bias]).reshape(1, 2)
    packed = after(jnp.concatenate([images, texts]), settings)
    tailed = images.shape[0]
    own_images, own_texts = packed[:rows], packed[tailed:]
    hops = [("blk", blocks, 1)] + [("group", groups, 1 << step) for step in range(groups.bit_length() - 1)]
    hops += [("blk", blocks, 1 << step) for step in range(1, blocks.bit_length() - 1)]
    choice = partner.reshape(1, groups)
    texts_across = swap(texts, "group", groups, 2)
    offer = call(offer_kernel, [choice, own_texts, texts_across], [texts.shape], "offer", texts.dtype)[0]
    offered = swap(offer, "group", groups, 1)
    partner_text = call(choose_kernel, [choice, own_texts, texts_across, offered], [texts.shape], "choose", texts.dtype)[0]
    group_images = lax.all_gather(after(packed[:tailed], partner_text), "group")
    scorer_image = call(scorer_kernel, [choice, group_images], [images.shape], "scorer", images.dtype)[0]

    if blocks == 8:

        def along(array, flip):
            return swap(array, "blk", blocks, flip)

        mate = along(packed, 1)
        text_two_off = along(partner_text, 4)
        text_one_off = along(partner_text, 2)
        text_three_off = along(after(text_two_off, text_one_off, mate, scorer_image), 2)
        image_one_off = along(after(scorer_image, text_three_off), 2)
        image_two_off = along(scorer_image, 4)
        column_texts = [partner_text, text_two_off, text_one_off, text_three_off]
        grad_shape = texts.shape
        own_part, mate_part, total = call(
            image_kernel,
            [settings, packed[:tailed], mate[:tailed], *column_texts],
            [grad_shape, grad_shape, (8, LANES)],
            "image_side",
            scratch=[(2 * rows, texts.shape[1]), (len(LINE) * rows, texts.shape[1])],
        )
        image_three_off = along(after(image_two_off, own_part), 2)
        total = hop_sum(total, hops[:1])
        image_grads = own_part + along(after(mate_part, total), 1)
        total = hop_sum(total, hops[1:3])
        total = after(total, image_one_off)
        early_images = [scorer_image, image_two_off, image_one_off]
        early_part = call(functools.partial(text_kernel, 1, 3), [settings, mate[tailed:], *early_images], [grad_shape], "text_side_early")[0]
        last_image = after(image_three_off, total, early_part)
        mate_part = call(functools.partial(text_kernel, 1, 1), [settings, mate[tailed:], last_image, early_part], [grad_shape], "text_side_mate")[0]
        column_images = early_images + [last_image]
        text_part = along(mate_part, 1)
        own_part = call(functools.partial(text_kernel, 0, 4), [settings, own_texts, *column_images], [grad_shape], "text_side_own")[0]
        text_grads = own_part + text_part
        total = after(hop_sum(after(total, image_grads), hops[3:4]), own_part)
        hops = hops[4:]
    else:
        temper = jnp.exp(log_temp[0])
        offset = bias[0]
        all_texts = lax.all_gather(partner_text, "blk", axis=0, tiled=True)
        every_image = lax.all_gather(scorer_image, "blk", axis=0)
        hits = matches(labels, jnp.arange(blocks * rows))
        logits, hit_values, slopes = pair_slopes(own_images, all_texts, hits, temper, offset)
        total = jnp.sum(jax.nn.softplus(logits) - hit_values * logits)
        total = jnp.zeros((8, 128)).at[0, 0].set(total)
        image_grads = grads(slopes, all_texts)
        all_images = every_image[:, :rows].reshape(blocks * rows, -1)
        back_labels = jax.vmap(lambda block: labels_of(block, rows, rows)[0])(every_image).reshape(-1)
        back_hits = matches(index_of([blk_place]), back_labels)
        back_slopes = pair_slopes(own_texts, all_images, back_hits, temper, offset)[2]
        text_grads = grads(back_slopes, all_images)

    total = hop_sum(total, hops)
    loss = jnp.sum(total * (1.0 / (groups * rows * blocks * blocks))).reshape(1)
    return (image_grads[None], text_grads[None], loss)


def solution(mesh):
    in_specs = (P("group", "blk", None), P("group", "blk", None), P("group", "blk"), P(), P(), P())
    out_specs = (P("group", "blk", None), P("group", "blk", None), P())
    return jax.shard_map(shards, mesh=mesh, in_specs=in_specs, out_specs=out_specs, check_vma=False)
```

```python
import functools

import jax
import jax.numpy as jnp
from jax import lax
from jax.experimental import pallas as pl
from jax.experimental.pallas import tpu as pltpu
from jax.sharding import PartitionSpec as P

TAIL = 8
DIGIT = 128
LANES = 128


def pair_slopes(rows, others, hits, temper, offset):
    logits = temper * jnp.dot(rows, others.T, preferred_element_type=jnp.float32) + offset
    hit_values = hits.astype(jnp.float32)
    slopes = (jax.nn.sigmoid(logits) - hit_values).astype(jnp.bfloat16)
    return logits, hit_values, slopes


def exchange(array, axis, size, mate):
    return lax.ppermute(array, axis, [(place, mate(place)) for place in range(size)])


def swap(array, axis, size, bit):
    return exchange(array, axis, size, lambda place: place ^ bit)


def after(array, *earlier):
    return lax.optimization_barrier((array, *earlier))[0]


def entry(partner, group):
    lane = lax.broadcasted_iota(jnp.int32, partner.shape, 1)
    return jnp.sum(jnp.where(lane == group, partner[...], 0), axis=1, keepdims=True)


def position(partner, group):
    lane = lax.broadcasted_iota(jnp.int32, partner.shape, 1)
    return jnp.sum(jnp.where(partner[...] == group, lane, 0), axis=1, keepdims=True)


def same_chip(group, other):
    return (group ^ other) >> 1 == 0


def offer_kernel(partner, own, across, out):
    here = lax.axis_index("group")
    out[...] = jnp.where(same_chip(entry(partner, here ^ 1), here), own[...], across[...])


def choose_kernel(partner, own, across, offered, out):
    here = lax.axis_index("group")
    wanted = entry(partner, here)
    held = jnp.where(same_chip(wanted, here), own[...], across[...])
    out[...] = jnp.where((wanted ^ here) & 1 == 0, held, offered[...])


def scorer_kernel(partner, every, out):
    wanted = position(partner, lax.axis_index("group"))
    found = every[0]
    for group in range(1, every.shape[0]):
        found = jnp.where(wanted == group, every[group], found)
    out[...] = found


LINE = (0, 4, 2, 6)


def with_labels(images, labels):
    digits = jnp.stack([labels // DIGIT, labels % DIGIT]).astype(images.dtype)
    return jnp.concatenate([images, jnp.pad(digits, ((0, TAIL - 2), (0, images.shape[1] - labels.shape[0])))])


def labels_of(block, rows, width):
    digits = block[rows : rows + TAIL, :width].astype(jnp.int32)
    return digits[:1] * DIGIT + digits[1:2]


def rows_by_rows(left, right):
    return lax.dot_general(left, right, (((1,), (1,)), ((), ())), preferred_element_type=jnp.float32)


def stack(blocks, rows, into):
    for place, block in enumerate(blocks):
        into[place * rows : (place + 1) * rows, :] = block[:rows, :]


def image_kernel(settings, images, mate, *refs):
    texts, (own_part, mate_part, loss, all_images, all_texts) = refs[:-5], refs[-5:]
    rows = texts[0].shape[0]
    temper = jnp.exp(settings[:, :1])
    stack((images, mate), rows, all_images)
    stack(texts, rows, all_texts)
    labels = jnp.concatenate([jnp.broadcast_to(labels_of(block, rows, LANES), (LANES, LANES)).T[:rows] for block in (images, mate)])
    labels = jnp.concatenate([labels] * (all_texts.shape[0] // LANES), axis=1)
    column = lax.broadcasted_iota(jnp.int32, labels.shape, 1)
    index = column
    for place, flip in enumerate(LINE):
        start = place * rows
        index = jnp.where(column >= start, column - start + (lax.axis_index("blk") ^ flip) * rows, index)

    logits = temper * rows_by_rows(all_images[...], all_texts[...]) + settings[:, 1:2]
    hit_values = (index == labels).astype(jnp.float32)
    small = jnp.exp(-jnp.abs(logits))
    losses = jnp.maximum(logits, 0.0) + jnp.log1p(small) - hit_values * logits
    slopes = jnp.where(logits >= 0.0, 1.0, small) / (1.0 + small) - hit_values
    total = losses.reshape(-1, 8, losses.shape[1]).sum(axis=0)
    loss[...] = sum(total[:, lane : lane + LANES] for lane in range(0, total.shape[1], LANES))
    grads = temper * jnp.dot(slopes.astype(jnp.bfloat16), all_texts[...], preferred_element_type=jnp.float32)
    own_part[...] = grads[:rows]
    mate_part[...] = grads[rows:]


def text_kernel(flip, count, settings, texts, *refs):
    images, earlier, part = refs[:count], refs[count:-1], refs[-1]
    rows = texts.shape[0]
    temper = jnp.exp(settings[:, :1])
    index = (lax.axis_index("blk") ^ flip) * rows + lax.broadcasted_iota(jnp.int32, (rows, rows), 0)
    total = jnp.zeros(part.shape, jnp.float32)
    for block in images:
        products = rows_by_rows(texts[...], block[:rows, :])
        hits = index == labels_of(block, rows, rows)
        slopes = (jax.nn.sigmoid(temper * products + settings[:, 1:2]) - hits.astype(jnp.float32)).astype(jnp.bfloat16)
        total += jnp.dot(slopes, block[:rows, :], preferred_element_type=jnp.float32)
    part[...] = temper * total + earlier[0][...] if earlier else temper * total


def call(kernel, arrays, shapes, name, dtype=jnp.float32, scratch=()):
    return pl.pallas_call(
        kernel,
        out_shape=[jax.ShapeDtypeStruct(shape, dtype) for shape in shapes],
        in_specs=[pl.BlockSpec(memory_space=pltpu.VMEM)] * len(arrays),
        out_specs=[pl.BlockSpec(memory_space=pltpu.VMEM)] * len(shapes),
        scratch_shapes=[pltpu.VMEM(shape, jnp.bfloat16) for shape in scratch],
        compiler_params=pltpu.CompilerParams(vmem_limit_bytes=16 * 2**20),
        name=name,
    )(*arrays)


def hop_sum(total, hops):
    for axis, size, bit in hops:
        total = total + swap(total, axis, size, bit)
    return total


def shards(image_embeds, text_embeds, positives, partner, log_temp, bias):
    texts = text_embeds[0]
    labels = positives[0]
    rows = texts.shape[0]
    blocks = lax.axis_size("blk")
    groups = lax.axis_size("group")
    blk_place = lax.axis_index("blk")
    images = with_labels(image_embeds[0], labels)

    def index_of(places):
        return (jnp.stack(places)[:, None] * rows + jnp.arange(rows)[None, :]).reshape(-1)

    def matches(some_labels, index):
        return some_labels[:, None] == index[None, :]

    def grads(slopes, others):
        return temper * jnp.dot(slopes, others, preferred_element_type=jnp.float32)

    settings = jnp.concatenate([log_temp, bias]).reshape(1, 2)
    packed = after(jnp.concatenate([images, texts]), settings)
    tailed = images.shape[0]
    own_images, own_texts = packed[:rows], packed[tailed:]
    hops = [("group", groups, 1 << step) for step in range(groups.bit_length() - 1)]
    hops += [("blk", blocks, 1 << step) for step in range(blocks.bit_length() - 1)]
    choice = partner.reshape(1, groups)
    texts_across = swap(texts, "group", groups, 2)
    offer = call(offer_kernel, [choice, own_texts, texts_across], [texts.shape], "offer", texts.dtype)[0]
    offered = swap(offer, "group", groups, 1)
    partner_text = call(choose_kernel, [choice, own_texts, texts_across, offered], [texts.shape], "choose", texts.dtype)[0]
    group_images = lax.all_gather(after(packed[:tailed], partner_text), "group")
    scorer_image = call(scorer_kernel, [choice, group_images], [images.shape], "scorer", images.dtype)[0]

    if blocks == 8:

        def along(array, flip):
            return swap(array, "blk", blocks, flip)

        mate = along(packed, 1)
        text_two_off = along(partner_text, 4)
        text_one_off = along(partner_text, 2)
        text_three_off = along(after(text_two_off, text_one_off, mate, scorer_image), 2)
        image_one_off = along(after(scorer_image, text_three_off), 2)
        image_two_off = along(scorer_image, 4)
        column_texts = [partner_text, text_two_off, text_one_off, text_three_off]
        grad_shape = texts.shape
        own_part, mate_part, total = call(
            image_kernel,
            [settings, packed[:tailed], mate[:tailed], *column_texts],
            [grad_shape, grad_shape, (8, LANES)],
            "image_side",
            scratch=[(2 * rows, texts.shape[1]), (len(LINE) * rows, texts.shape[1])],
        )
        image_three_off = along(after(image_two_off, own_part), 2)
        image_grads = own_part + along(mate_part, 1)
        total = hop_sum(total, hops[:2])
        total = hop_sum(after(total, image_one_off), hops[2:3])
        early_images = [scorer_image, image_two_off, image_one_off]
        early_part = call(functools.partial(text_kernel, 1, 3), [settings, mate[tailed:], *early_images], [grad_shape], "text_side_early")[0]
        last_image = after(image_three_off, total, early_part)
        mate_part = call(functools.partial(text_kernel, 1, 1), [settings, mate[tailed:], last_image, early_part], [grad_shape], "text_side_mate")[0]
        column_images = early_images + [last_image]
        text_part = along(mate_part, 1)
        own_part = call(functools.partial(text_kernel, 0, 4), [settings, own_texts, *column_images], [grad_shape], "text_side_own")[0]
        text_grads = own_part + text_part
        total = after(hop_sum(after(total, image_grads), hops[3:4]), own_part)
        hops = hops[4:]
    else:
        temper = jnp.exp(log_temp[0])
        offset = bias[0]
        all_texts = lax.all_gather(partner_text, "blk", axis=0, tiled=True)
        every_image = lax.all_gather(scorer_image, "blk", axis=0)
        hits = matches(labels, jnp.arange(blocks * rows))
        logits, hit_values, slopes = pair_slopes(own_images, all_texts, hits, temper, offset)
        total = jnp.sum(jax.nn.softplus(logits) - hit_values * logits)
        total = jnp.zeros((8, 128)).at[0, 0].set(total)
        image_grads = grads(slopes, all_texts)
        all_images = every_image[:, :rows].reshape(blocks * rows, -1)
        back_labels = jax.vmap(lambda block: labels_of(block, rows, rows)[0])(every_image).reshape(-1)
        back_hits = matches(index_of([blk_place]), back_labels)
        back_slopes = pair_slopes(own_texts, all_images, back_hits, temper, offset)[2]
        text_grads = grads(back_slopes, all_images)

    total = hop_sum(total, hops)
    loss = jnp.sum(total * (1.0 / (groups * rows * blocks * blocks))).reshape(1)
    return (image_grads[None], text_grads[None], loss)


def solution(mesh):
    in_specs = (P("group", "blk", None), P("group", "blk", None), P("group", "blk"), P(), P(), P())
    out_specs = (P("group", "blk", None), P("group", "blk", None), P())
    return jax.shard_map(shards, mesh=mesh, in_specs=in_specs, out_specs=out_specs, check_vma=False)
```

```python
import functools

import jax
import jax.numpy as jnp
from jax import lax
from jax.experimental import pallas as pl
from jax.experimental.pallas import tpu as pltpu
from jax.sharding import PartitionSpec as P

TAIL = 8
DIGIT = 128
LANES = 128


def pair_slopes(rows, others, hits, temper, offset):
    logits = temper * jnp.dot(rows, others.T, preferred_element_type=jnp.float32) + offset
    hit_values = hits.astype(jnp.float32)
    slopes = (jax.nn.sigmoid(logits) - hit_values).astype(jnp.bfloat16)
    return logits, hit_values, slopes


def exchange(array, axis, size, mate):
    return lax.ppermute(array, axis, [(place, mate(place)) for place in range(size)])


def swap(array, axis, size, bit):
    return exchange(array, axis, size, lambda place: place ^ bit)


def after(array, *earlier):
    return lax.optimization_barrier((array, *earlier))[0]


def entry(partner, group):
    lane = lax.broadcasted_iota(jnp.int32, partner.shape, 1)
    return jnp.sum(jnp.where(lane == group, partner[...], 0), axis=1, keepdims=True)


def position(partner, group):
    lane = lax.broadcasted_iota(jnp.int32, partner.shape, 1)
    return jnp.sum(jnp.where(partner[...] == group, lane, 0), axis=1, keepdims=True)


def same_chip(group, other):
    return (group ^ other) >> 1 == 0


def offer_kernel(partner, own, across, out):
    here = lax.axis_index("group")
    out[...] = jnp.where(same_chip(entry(partner, here ^ 1), here), own[...], across[...])


def choose_kernel(partner, own, across, offered, out):
    here = lax.axis_index("group")
    wanted = entry(partner, here)
    held = jnp.where(same_chip(wanted, here), own[...], across[...])
    out[...] = jnp.where((wanted ^ here) & 1 == 0, held, offered[...])


def scorer_kernel(partner, every, out):
    wanted = position(partner, lax.axis_index("group"))
    found = every[0]
    for group in range(1, every.shape[0]):
        found = jnp.where(wanted == group, every[group], found)
    out[...] = found


LINE = (0, 4, 2, 6)


def with_labels(images, labels):
    digits = jnp.stack([labels // DIGIT, labels % DIGIT]).astype(images.dtype)
    return jnp.concatenate([images, jnp.pad(digits, ((0, TAIL - 2), (0, images.shape[1] - labels.shape[0])))])


def labels_of(block, rows, width):
    digits = block[rows : rows + TAIL, :width].astype(jnp.int32)
    return digits[:1] * DIGIT + digits[1:2]


def rows_by_rows(left, right):
    return lax.dot_general(left, right, (((1,), (1,)), ((), ())), preferred_element_type=jnp.float32)


def stack(blocks, rows, into):
    for place, block in enumerate(blocks):
        into[place * rows : (place + 1) * rows, :] = block[:rows, :]


def image_kernel(settings, images, mate, *refs):
    texts, (own_part, mate_part, loss, all_images, all_texts) = refs[:-5], refs[-5:]
    rows = texts[0].shape[0]
    temper = jnp.exp(settings[:, :1])
    stack((images, mate), rows, all_images)
    stack(texts, rows, all_texts)
    labels = jnp.concatenate([jnp.broadcast_to(labels_of(block, rows, LANES), (LANES, LANES)).T[:rows] for block in (images, mate)])
    labels = jnp.concatenate([labels] * (all_texts.shape[0] // LANES), axis=1)
    column = lax.broadcasted_iota(jnp.int32, labels.shape, 1)
    index = column
    for place, flip in enumerate(LINE):
        start = place * rows
        index = jnp.where(column >= start, column - start + (lax.axis_index("blk") ^ flip) * rows, index)

    logits = temper * rows_by_rows(all_images[...], all_texts[...]) + settings[:, 1:2]
    hit_values = (index == labels).astype(jnp.float32)
    small = jnp.exp(-jnp.abs(logits))
    losses = jnp.maximum(logits, 0.0) + jnp.log1p(small) - hit_values * logits
    slopes = jnp.where(logits >= 0.0, 1.0, small) / (1.0 + small) - hit_values
    total = losses.reshape(-1, 8, losses.shape[1]).sum(axis=0)
    loss[...] = sum(total[:, lane : lane + LANES] for lane in range(0, total.shape[1], LANES))
    grads = temper * jnp.dot(slopes.astype(jnp.bfloat16), all_texts[...], preferred_element_type=jnp.float32)
    own_part[...] = grads[:rows]
    mate_part[...] = grads[rows:]


def text_kernel(flip, count, settings, texts, *refs):
    images, earlier, part = refs[:count], refs[count:-1], refs[-1]
    rows = texts.shape[0]
    temper = jnp.exp(settings[:, :1])
    index = (lax.axis_index("blk") ^ flip) * rows + lax.broadcasted_iota(jnp.int32, (rows, rows), 0)
    total = jnp.zeros(part.shape, jnp.float32)
    for block in images:
        products = rows_by_rows(texts[...], block[:rows, :])
        hits = index == labels_of(block, rows, rows)
        slopes = (jax.nn.sigmoid(temper * products + settings[:, 1:2]) - hits.astype(jnp.float32)).astype(jnp.bfloat16)
        total += jnp.dot(slopes, block[:rows, :], preferred_element_type=jnp.float32)
    part[...] = temper * total + earlier[0][...] if earlier else temper * total


def sum_kernel(own_part, text_part, text_grads):
    text_grads[...] = own_part[...] + text_part[...]


def call(kernel, arrays, shapes, name, dtype=jnp.float32, scratch=()):
    return pl.pallas_call(
        kernel,
        out_shape=[jax.ShapeDtypeStruct(shape, dtype) for shape in shapes],
        in_specs=[pl.BlockSpec(memory_space=pltpu.VMEM)] * len(arrays),
        out_specs=[pl.BlockSpec(memory_space=pltpu.VMEM)] * len(shapes),
        scratch_shapes=[pltpu.VMEM(shape, jnp.bfloat16) for shape in scratch],
        compiler_params=pltpu.CompilerParams(vmem_limit_bytes=16 * 2**20),
        name=name,
    )(*arrays)


def hop_sum(total, hops):
    for axis, size, bit in hops:
        total = total + swap(total, axis, size, bit)
    return total


def shards(image_embeds, text_embeds, positives, partner, log_temp, bias):
    texts = text_embeds[0]
    labels = positives[0]
    rows = texts.shape[0]
    blocks = lax.axis_size("blk")
    groups = lax.axis_size("group")
    blk_place = lax.axis_index("blk")
    images = with_labels(image_embeds[0], labels)

    def index_of(places):
        return (jnp.stack(places)[:, None] * rows + jnp.arange(rows)[None, :]).reshape(-1)

    def matches(some_labels, index):
        return some_labels[:, None] == index[None, :]

    def grads(slopes, others):
        return temper * jnp.dot(slopes, others, preferred_element_type=jnp.float32)

    settings = jnp.concatenate([log_temp, bias]).reshape(1, 2)
    packed = after(jnp.concatenate([images, texts]), settings)
    tailed = images.shape[0]
    own_images, own_texts = packed[:rows], packed[tailed:]
    hops = [("group", groups, 1 << step) for step in range(groups.bit_length() - 1)]
    hops += [("blk", blocks, 1 << step) for step in range(blocks.bit_length() - 1)]
    choice = partner.reshape(1, groups)
    texts_across = swap(texts, "group", groups, 2)
    offer = call(offer_kernel, [choice, own_texts, texts_across], [texts.shape], "offer", texts.dtype)[0]
    offered = swap(offer, "group", groups, 1)
    partner_text = call(choose_kernel, [choice, own_texts, texts_across, offered], [texts.shape], "choose", texts.dtype)[0]
    group_images = lax.all_gather(after(packed[:tailed], partner_text), "group")
    scorer_image = call(scorer_kernel, [choice, group_images], [images.shape], "scorer", images.dtype)[0]

    if blocks == 8:

        def along(array, flip):
            return swap(array, "blk", blocks, flip)

        mate = along(packed, 1)
        text_two_off = along(partner_text, 4)
        text_one_off = along(partner_text, 2)
        text_three_off = along(after(text_two_off, text_one_off, mate, scorer_image), 2)
        image_one_off = along(after(scorer_image, text_three_off), 2)
        image_two_off = along(scorer_image, 4)
        column_texts = [partner_text, text_two_off, text_one_off, text_three_off]
        grad_shape = texts.shape
        own_part, mate_part, total = call(
            image_kernel,
            [settings, packed[:tailed], mate[:tailed], *column_texts],
            [grad_shape, grad_shape, (8, LANES)],
            "image_side",
            scratch=[(2 * rows, texts.shape[1]), (len(LINE) * rows, texts.shape[1])],
        )
        image_three_off = along(after(image_two_off, own_part), 2)
        image_grads = own_part + along(mate_part, 1)
        total = hop_sum(total, hops[:2])
        total = hop_sum(after(total, image_one_off), hops[2:3])
        early_images = [scorer_image, image_two_off, image_one_off]
        early_part = call(functools.partial(text_kernel, 1, 3), [settings, mate[tailed:], *early_images], [grad_shape], "text_side_early")[0]
        last_image = after(image_three_off, total, early_part)
        mate_part = call(functools.partial(text_kernel, 1, 1), [settings, mate[tailed:], last_image, early_part], [grad_shape], "text_side_mate")[0]
        column_images = early_images + [last_image]
        text_part = along(mate_part, 1)
        own_part = call(functools.partial(text_kernel, 0, 4), [settings, own_texts, *column_images], [grad_shape], "text_side_own")[0]
        text_grads = call(sum_kernel, [own_part, text_part], [grad_shape], "text_side_sum")[0]
        total = after(hop_sum(after(total, image_grads), hops[3:4]), own_part)
        hops = hops[4:]
    else:
        temper = jnp.exp(log_temp[0])
        offset = bias[0]
        all_texts = lax.all_gather(partner_text, "blk", axis=0, tiled=True)
        every_image = lax.all_gather(scorer_image, "blk", axis=0)
        hits = matches(labels, jnp.arange(blocks * rows))
        logits, hit_values, slopes = pair_slopes(own_images, all_texts, hits, temper, offset)
        total = jnp.sum(jax.nn.softplus(logits) - hit_values * logits)
        total = jnp.zeros((8, 128)).at[0, 0].set(total)
        image_grads = grads(slopes, all_texts)
        all_images = every_image[:, :rows].reshape(blocks * rows, -1)
        back_labels = jax.vmap(lambda block: labels_of(block, rows, rows)[0])(every_image).reshape(-1)
        back_hits = matches(index_of([blk_place]), back_labels)
        back_slopes = pair_slopes(own_texts, all_images, back_hits, temper, offset)[2]
        text_grads = grads(back_slopes, all_images)

    total = hop_sum(total, hops)
    loss = jnp.sum(total * (1.0 / (groups * rows * blocks * blocks))).reshape(1)
    return (image_grads[None], text_grads[None], loss)


def solution(mesh):
    in_specs = (P("group", "blk", None), P("group", "blk", None), P("group", "blk"), P(), P(), P())
    out_specs = (P("group", "blk", None), P("group", "blk", None), P())
    return jax.shard_map(shards, mesh=mesh, in_specs=in_specs, out_specs=out_specs, check_vma=False)
```
